32 devices in a mesh: dp: 16 (over z, x, core), tensor: 2 (over y).
Axes of the slice: x: 2, y: 2, z: 4, core: 2. Of those that a mesh axis runs over, the one named last changes fastest.
Arguments:
- tokens: bfloat16 [8192, 1280], P(('dp', 'tensor')), may hold values from -6 to 6
- w_query: bfloat16 [1280, 1280], P('dp', 'tensor'), may hold values from -0.15625 to 0.15625
- w_key: bfloat16 [1280, 1280], P('dp', 'tensor'), may hold values from -0.15625 to 0.15625
- w_value: bfloat16 [1280, 1280], P('dp', 'tensor'), may hold values from -0.15625 to 0.15625
- w_output: bfloat16 [1280, 1280], P('tensor', 'dp'), may hold values from -0.625 to 0.625
- w_in: bfloat16 [1280, 1280], P('dp', 'tensor'), may hold values from -0.15625 to 0.15625
- w_out: bfloat16 [1280, 1280], P('tensor', 'dp'), may hold values from -0.15625 to 0.15625
- gain_attn: bfloat16 [1280], P('dp'), may hold values from 0.5 to 1.5
- gain_mlp: bfloat16 [1280], P('dp'), may hold values from 0.5 to 1.5
- seq_lengths: int32 [16, 5], P('dp'), may hold values from 1 to 384, as said below
- seq_offsets: int32 [16, 5], P('dp'), may hold values from 0 to 511, as said below
- cotangent: bfloat16 [8192, 1280], P(('dp', 'tensor')), may hold values from -6 to 6
Outputs:
- mixed: bfloat16 [8192, 1280], P(('dp', 'tensor'))
- grad_tokens: float32 [8192, 1280], P(('dp', 'tensor'))
- grad_w_query: float32 [1280, 1280], P('dp', 'tensor')
- grad_w_key: float32 [1280, 1280], P('dp', 'tensor')
- grad_w_value: float32 [1280, 1280], P('dp', 'tensor')
- grad_w_output: float32 [1280, 1280], P('tensor', 'dp')
- grad_w_in: float32 [1280, 1280], P('dp', 'tensor')
- grad_w_out: float32 [1280, 1280], P('tensor', 'dp')
- grad_gain_attn: float32 [1280], P('dp')
- grad_gain_mlp: float32 [1280], P('dp')
The draws below stay inside these ranges and needn't reach their ends.
Inputs may be any that keep to these rules, and one draw needn't show every extreme that they name: `seq_lengths`: every slot holds a series of at least one row; the series of a group lie in disjoint row ranges, in slot order; the longest is reached in some group. `seq_offsets`: the first row of each slot's series within its group; rows in no series are padding.
All inputs are finite; a program needn't handle non-finite values.
Results may differ from the reference program's by a relative error of at most 0.012.
Values may be sent and summed in bfloat16 or wider, within the bound.
No kernel may reach another device: no remote copies, remote signals or barrier semaphores. Data moves between devices by JAX's collectives and lax.ppermute only.
A program may use at most 192 MiB of HBM per device.

```python
import jax
import jax.numpy as jnp
from jax import lax

D = 1280
FF = 1280
HEAD_DIM = 80
TOK_DEV = 256
SLOTS = 5
ROWS = 512
TOKENS = 8192
N_DP = 16


def series_layout(key):
    keys = jax.random.split(key, 5)
    slot_width = TOK_DEV // 8
    shorts = SLOTS - 1
    tail_start = ROWS - shorts * slot_width
    chosen = jax.random.randint(keys[0], (), 0, N_DP)
    others = (jnp.arange(N_DP, dtype=jnp.int32) != chosen).astype(jnp.int32)
    leading = jax.random.randint(keys[1], (N_DP,), 0, TOK_DEV // 4) * others
    trailing = jax.random.randint(keys[2], (N_DP,), 0, TOK_DEV // 4) * others
    long_length = tail_start - leading - trailing
    short_length = jax.random.randint(keys[3], (N_DP, shorts), 1, slot_width + 1)
    shifts = jax.random.randint(keys[4], (N_DP, shorts), 0, slot_width - short_length + 1)
    short_start = tail_start + slot_width * jnp.arange(shorts, dtype=jnp.int32)[None, :] + shifts
    lengths = jnp.concatenate([long_length[:, None], short_length], axis=1).astype(jnp.int32)
    offsets = jnp.concatenate([leading[:, None], short_start], axis=1).astype(jnp.int32)
    return (lengths, offsets)


def draw_seq_lengths(key, part):
    return series_layout(key)[0]


def draw_seq_offsets(key, part):
    return series_layout(key)[1]


def block_levels(rng, dims, shards, low, high):
    factor_of = 1.0
    for dim, parts in shards:
        heights = jax.random.uniform(jax.random.fold_in(jax.random.fold_in(rng, 6), dim), (parts,), jnp.float32, low / len(shards), high / len(shards))
        factor_of = factor_of * jnp.repeat(jnp.exp(heights), dims[dim] // parts).reshape((-1,) + (1,) * (len(dims) - 1 - dim))
    return factor_of


def centred(rng, extent, width, most, cuts=(), kind=jnp.bfloat16):
    drawn = jax.random.normal(rng, extent, jnp.float32) * width
    if len(cuts) > 0:
        drawn = block_levels(rng, extent, cuts, -0.22, 0.18) * drawn
    return jnp.clip(drawn, min=-most, max=most).astype(kind)


def setup_inputs(seed: int = 0) -> dict:
    key_of = jax.random.split(jax.random.key(seed), 13)
    tokens = centred(key_of[0], (TOKENS, D), 1.0, 6.0, ((0, 32),))
    w_query = centred(key_of[1], (D, D), D ** -0.5, 0.15625, ((0, 16), (1, 2)))
    w_key = centred(key_of[2], (D, D), D ** -0.5, 0.15625, ((0, 16), (1, 2)))
    w_value = centred(key_of[3], (D, D), D ** -0.5, 0.15625, ((0, 16), (1, 2)))
    w_output = centred(key_of[4], (D, D), (D // 16) ** -0.5, 0.625, ((0, 2), (1, 16)))
    w_in = centred(key_of[5], (D, FF), D ** -0.5, 0.15625, ((0, 16), (1, 2)))
    w_out = centred(key_of[6], (FF, D), FF ** -0.5, 0.15625, ((0, 2), (1, 16)))
    gain_attn = jnp.clip(1.0 + 0.1 * jax.random.normal(key_of[7], (D,), jnp.float32), 0.5, 1.5).astype(jnp.bfloat16)
    gain_mlp = jnp.clip(1.0 + 0.1 * jax.random.normal(key_of[8], (D,), jnp.float32), 0.5, 1.5).astype(jnp.bfloat16)
    seq_lengths = draw_seq_lengths(jax.random.fold_in(key_of[12], 71), 0)
    seq_offsets = draw_seq_offsets(jax.random.fold_in(key_of[12], 71), 0)
    cotangent = centred(key_of[11], (TOKENS, D), 1.0, 6.0, ((0, 32),))
    return {"tokens": tokens, "w_query": w_query, "w_key": w_key, "w_value": w_value, "w_output": w_output, "w_in": w_in, "w_out": w_out, "gain_attn": gain_attn, "gain_mlp": gain_mlp, "seq_lengths": seq_lengths, "seq_offsets": seq_offsets, "cotangent": cotangent}


highest = lax.Precision.HIGHEST
epsilon = 1e-06
stat_eps = 1e-05
masked_score = -1e+30

@jax.custom_vjp
def low(v):
    return lax.optimization_barrier(v.astype(jnp.bfloat16)).astype(jnp.float32)

@jax.custom_vjp
def low_back(v):
    return v

def low_keep(v):
    return (low(v), None)

def low_pass(kept, grad):
    return (grad,)

def back_keep(v):
    return (v, None)

def back_low(kept, grad):
    return (low(grad),)
low.defvjp(low_keep, low_pass)
low_back.defvjp(back_keep, back_low)

def row_layout(lengths, offsets, group_rows):
    row_ids = jnp.arange(group_rows, dtype=jnp.int32)
    inside = (row_ids[:, None] >= offsets[None, :]) & (row_ids[:, None] < offsets[None, :] + lengths[None, :])
    member = inside.astype(jnp.float32)
    slot_ids = jnp.arange(offsets.shape[0], dtype=jnp.int32)
    segment = (lax.optimization_barrier(jnp.sum(jnp.where(inside, slot_ids[None, :] + 1, 0), axis=1)) - 1).astype(jnp.int32)
    seq_start = lax.optimization_barrier(jnp.sum(jnp.where(inside, offsets[None, :], 0), axis=1)).astype(jnp.int32)
    position = jnp.where(segment >= 0, row_ids - seq_start, 0).astype(jnp.float32)
    first_rows = (row_ids[:, None] == offsets[None, :]).astype(jnp.float32)
    return (member, segment, position, first_rows)

def rotary_tables(position):
    half_dim = HEAD_DIM // 2
    freqs = 10000.0 ** (-2.0 * jnp.arange(half_dim, dtype=jnp.float32) / HEAD_DIM)
    angles = position[:, None] * freqs[None, :]
    return (jnp.cos(angles), jnp.sin(angles))

def rotate(values, cosine, sine):
    row_count = values.shape[0]
    shaped = values.reshape(row_count, -1, HEAD_DIM)
    half_dim = HEAD_DIM // 2
    first_half = shaped[..., :half_dim]
    second_half = shaped[..., half_dim:]
    cos_b = cosine[:, None, :]
    sin_b = sine[:, None, :]
    turned = jnp.concatenate([first_half * cos_b - second_half * sin_b, first_half * sin_b + second_half * cos_b], axis=-1)
    return turned.reshape(row_count, -1)

def rms(values):
    return values * lax.rsqrt(lax.optimization_barrier(jnp.mean(values * values, axis=-1, keepdims=True)) + epsilon)

def allowed_mask(seg_query, query_ids, segment, key_ids):
    same = (seg_query[:, None] == segment[None, :]) & (key_ids[None, :] <= query_ids[:, None]) & (seg_query[:, None] >= 0)
    return same | (query_ids[:, None] == key_ids[None, :])

def attention(q_rot, k_rot, values, segment):
    group_rows = q_rot.shape[0]
    block_rows = min(512, group_rows)
    query_all = q_rot.reshape(group_rows, -1, HEAD_DIM)
    key_all = k_rot.reshape(group_rows, -1, HEAD_DIM)
    value_all = values.reshape(group_rows, -1, HEAD_DIM)
    key_ids = jnp.arange(group_rows, dtype=jnp.int32)

    def one_block(block_index):
        row_begin = block_index * block_rows
        query_ids = row_begin + jnp.arange(block_rows, dtype=jnp.int32)
        queries = lax.dynamic_slice_in_dim(query_all, row_begin, block_rows, 0)
        scores = jnp.einsum('qhd,khd->hqk', queries, key_all, precision=highest) * HEAD_DIM ** (-0.5)
        scores = low_back(scores)
        seg_query = lax.dynamic_slice_in_dim(segment, row_begin, block_rows, 0)
        mask = allowed_mask(seg_query, query_ids, segment, key_ids)
        scores = jnp.where(mask[None], scores, masked_score)
        top = lax.optimization_barrier(jnp.max(scores, axis=-1, keepdims=True))
        expo = jnp.exp(scores - top)
        probs = expo / lax.optimization_barrier(jnp.sum(expo, axis=-1, keepdims=True))
        heads = jnp.einsum('hqk,khd->qhd', low(probs), value_all, precision=highest)
        return heads.reshape(block_rows, -1)
    outs = lax.map(jax.checkpoint(one_block), jnp.arange(group_rows // block_rows, dtype=jnp.int32))
    return outs.reshape(group_rows, -1)

def layer(tokens, w_query, w_key, w_value, w_output, w_in, w_out, gain_attn, gain_mlp, layout):
    member, segment, position, first_rows = layout
    firsts = jnp.dot(first_rows.T, tokens, precision=highest)
    mu_seq = lax.optimization_barrier(jnp.mean(firsts, axis=1))
    sd_seq = jnp.sqrt(lax.optimization_barrier(jnp.mean(jnp.square(firsts - mu_seq[:, None]), axis=1)) + stat_eps)
    live = lax.optimization_barrier(jnp.sum(member, axis=1))
    mu_row = jnp.dot(member, mu_seq, precision=highest)
    sd_row = jnp.dot(member, sd_seq, precision=highest) + (1.0 - live)
    centered = (tokens - mu_row[:, None]) / sd_row[:, None]
    attn_in = low(rms(centered) * gain_attn)
    queries = low_back(jnp.dot(attn_in, w_query, precision=highest))
    keys = low_back(jnp.dot(attn_in, w_key, precision=highest))
    values = low(low_back(jnp.dot(attn_in, w_value, precision=highest)))
    cosine, sine = rotary_tables(position)
    q_rot = low(rotate(queries, cosine, sine))
    k_rot = low(rotate(keys, cosine, sine))
    heads_low = low(low_back(attention(q_rot, k_rot, values, segment)))
    attn_out = low_back(jnp.dot(heads_low, w_output, precision=highest))
    resid = centered + attn_out
    mid_in = low(rms(resid) * gain_mlp)
    pre_act = low_back(jnp.dot(mid_in, w_in, precision=highest))
    hidden = low(jax.nn.silu(pre_act))
    mlp_out = low_back(jnp.dot(hidden, w_out, precision=highest))
    final = resid + mlp_out
    return mu_row[:, None] + sd_row[:, None] * final

def reference(tokens, w_query, w_key, w_value, w_output, w_in, w_out, gain_attn, gain_mlp, seq_lengths, seq_offsets, cotangent):
    weights = tuple((array.astype(jnp.float32) for array in (w_query, w_key, w_value, w_output, w_in, w_out, gain_attn, gain_mlp)))
    group_tokens = tokens.astype(jnp.float32).reshape(N_DP, ROWS, D)
    group_grads = cotangent.astype(jnp.float32).reshape(N_DP, ROWS, D)

    def one_group(totals, item):
        group_input, group_grad, lengths, offsets = item
        layout = row_layout(lengths, offsets, ROWS)

        def forward(layer_input, *params):
            return layer(layer_input, *params, layout)
        result, pull = jax.vjp(forward, group_input, *weights)
        grads = pull(group_grad)
        totals = tuple((earlier + update for earlier, update in zip(totals, grads[1:])))
        return (totals, (result.astype(jnp.bfloat16), grads[0]))
    zeros = tuple((jnp.zeros(array.shape, jnp.float32) for array in weights))
    totals, (mixed, grad_tokens) = lax.scan(one_group, zeros, (group_tokens, group_grads, seq_lengths, seq_offsets))
    return (mixed.reshape(TOKENS, D), grad_tokens.reshape(TOKENS, D), totals[0], totals[1], totals[2], totals[3], totals[4], totals[5], totals[6], totals[7])
```

```python
import jax
import jax.numpy as jnp
from jax import lax
from jax.experimental import pallas as pl
from jax.experimental.pallas import tpu as pltpu
from jax.sharding import Mesh
from jax.sharding import PartitionSpec as P

HEAD_DIM = 80


highest = lax.Precision.HIGHEST
epsilon = 1e-06
stat_eps = 1e-05
masked_score = -1e30
contract_last = (((1,), (1,)), ((), ()))
contract_first = (((0,), (0,)), ((), ()))


def against(left, right):
    return lax.dot_general(left, right, contract_last, preferred_element_type=jnp.float32)


def across(left, right):
    return lax.dot_general(left, right, contract_first, preferred_element_type=jnp.float32)


def row_layout(lengths, offsets, group_rows):
    row_ids = jnp.arange(group_rows, dtype=jnp.int32)
    inside = (row_ids[:, None] >= offsets[None, :]) & (
        row_ids[:, None] < offsets[None, :] + lengths[None, :]
    )
    member = inside.astype(jnp.float32)
    slot_ids = jnp.arange(offsets.shape[0], dtype=jnp.int32)
    segment = jnp.sum(jnp.where(inside, slot_ids[None, :] + 1, 0), axis=1) - 1
    seq_start = jnp.sum(jnp.where(inside, offsets[None, :], 0), axis=1)
    position = jnp.where(segment >= 0, row_ids - seq_start, 0).astype(jnp.float32)
    first_rows = (row_ids[:, None] == offsets[None, :]).astype(jnp.float32)
    return (member, segment, position, first_rows)


def rotary_tables(position):
    half_dim = HEAD_DIM // 2
    freqs = 10000.0 ** (-2.0 * jnp.arange(half_dim, dtype=jnp.float32) / HEAD_DIM)
    angles = position[:, None] * freqs[None, :]
    return (jnp.cos(angles), jnp.sin(angles))


def rotate(values, cosine, sine, direction):
    row_count = values.shape[0]
    shaped = values.reshape(row_count, -1, HEAD_DIM)
    half_dim = HEAD_DIM // 2
    first_half = shaped[..., :half_dim]
    second_half = shaped[..., half_dim:]
    cos_b = cosine[:, None, :]
    sin_b = sine[:, None, :] * direction
    turned = jnp.concatenate(
        [first_half * cos_b - second_half * sin_b, first_half * sin_b + second_half * cos_b],
        axis=-1,
    )
    return turned.reshape(row_count, -1)


def rms_norm(values):
    factor = lax.rsqrt(jnp.mean(values * values, axis=-1, keepdims=True) + epsilon)
    return (values * factor, factor)


def norm_back(grad_normed, normed, factor):
    return factor * (grad_normed - normed * jnp.mean(grad_normed * normed, axis=-1, keepdims=True))


def allowed_mask(seg_query, query_ids, segment, key_ids):
    same = (
        (seg_query[:, None] == segment[None, :])
        & (key_ids[None, :] <= query_ids[:, None])
        & (seg_query[:, None] >= 0)
    )
    return same | (query_ids[:, None] == key_ids[None, :])


def block_scores(query_all, key_all, segment, row_begin, block_rows):
    group_rows = key_all.shape[0]
    key_ids = jnp.arange(group_rows, dtype=jnp.int32)
    query_ids = row_begin + jnp.arange(block_rows, dtype=jnp.int32)
    queries = lax.dynamic_slice_in_dim(query_all, row_begin, block_rows, 0)
    scores = jnp.einsum(
        "qhd,khd->hqk", queries, key_all, preferred_element_type=jnp.float32
    ) * HEAD_DIM ** (-0.5)
    seg_query = lax.dynamic_slice_in_dim(segment, row_begin, block_rows, 0)
    mask = allowed_mask(seg_query, query_ids, segment, key_ids)
    return (jnp.where(mask[None], scores, masked_score), queries)


def attention_forward(q_rot, k_rot, values, segment):
    group_rows, head_width = q_rot.shape
    block_rows = min(512, group_rows)
    query_all = q_rot.reshape(group_rows, -1, HEAD_DIM)
    key_all = k_rot.reshape(group_rows, -1, HEAD_DIM)
    value_all = values.reshape(group_rows, -1, HEAD_DIM)

    def one_block(block_index):
        scores, queries = block_scores(
            query_all, key_all, segment, block_index * block_rows, block_rows
        )
        top = jnp.max(scores, axis=-1, keepdims=True)
        expo = jnp.exp(scores - top)
        total_exp = jnp.sum(expo, axis=-1, keepdims=True)
        probs = (expo / total_exp).astype(jnp.bfloat16)
        heads = jnp.einsum("hqk,khd->qhd", probs, value_all, preferred_element_type=jnp.float32)
        return (heads.reshape(block_rows, head_width), (top + jnp.log(total_exp))[..., 0])

    outs, log_sums = lax.map(one_block, jnp.arange(group_rows // block_rows, dtype=jnp.int32))
    return (outs.reshape(group_rows, head_width), log_sums)


def attention_backward(q_rot, k_rot, values, segment, log_sums, heads_grad):
    group_rows, head_width = q_rot.shape
    block_rows = min(512, group_rows)
    query_all = q_rot.reshape(group_rows, -1, HEAD_DIM)
    key_all = k_rot.reshape(group_rows, -1, HEAD_DIM)
    value_all = values.reshape(group_rows, -1, HEAD_DIM)
    grad_all = heads_grad.reshape(group_rows, -1, HEAD_DIM)
    scale_factor = HEAD_DIM ** (-0.5)

    def one_block(carry, block_index):
        key_grad, value_grad = carry
        row_begin = block_index * block_rows
        scores, queries = block_scores(query_all, key_all, segment, row_begin, block_rows)
        probs = jnp.exp(scores - log_sums[block_index][..., None])
        grads_block = lax.dynamic_slice_in_dim(grad_all, row_begin, block_rows, 0)
        prob_grad = jnp.einsum(
            "qhd,khd->hqk", grads_block, value_all, preferred_element_type=jnp.float32
        )
        inner = jnp.sum(probs * prob_grad, axis=-1, keepdims=True)
        score_grad = (probs * (prob_grad - inner)).astype(jnp.bfloat16)
        query_grad = (
            jnp.einsum("hqk,khd->qhd", score_grad, key_all, preferred_element_type=jnp.float32)
            * scale_factor
        )
        key_grad = (
            key_grad
            + jnp.einsum("hqk,qhd->khd", score_grad, queries, preferred_element_type=jnp.float32)
            * scale_factor
        )
        value_grad = value_grad + jnp.einsum(
            "hqk,qhd->khd",
            probs.astype(jnp.bfloat16),
            grads_block,
            preferred_element_type=jnp.float32,
        )
        return ((key_grad, value_grad), query_grad.reshape(block_rows, head_width))

    zeros = jnp.zeros(query_all.shape, jnp.float32)
    (key_grad, value_grad), query_grads = lax.scan(
        one_block, (zeros, zeros), jnp.arange(group_rows // block_rows, dtype=jnp.int32)
    )
    return (
        query_grads.reshape(group_rows, head_width),
        key_grad.reshape(group_rows, head_width),
        value_grad.reshape(group_rows, head_width),
    )


def split_weights(rows_full, columns_full, gains_full, head_width):
    qkv_width = 3 * head_width
    return (
        rows_full[:, :qkv_width],
        rows_full[:, qkv_width:],
        columns_full[:head_width],
        columns_full[head_width:],
        gains_full[0].astype(jnp.float32),
        gains_full[1].astype(jnp.float32),
    )


def local(
    tokens,
    w_query,
    w_key,
    w_value,
    w_output,
    w_in,
    w_out,
    gain_attn,
    gain_mlp,
    seq_lengths,
    seq_offsets,
    cotangent,
):
    own_rows = tokens.shape[0]
    feature_count = tokens.shape[1]
    head_width = w_query.shape[1]
    qkv_width = 3 * head_width
    row_blocks = jnp.concatenate([w_query, w_key, w_value, w_in], axis=1)
    column_blocks = jnp.concatenate([w_output, w_out], axis=0)
    gain_pair = jnp.stack([gain_attn, gain_mlp])
    rows_full, columns_full, gains_full = (
        lax.all_gather(row_blocks, "dp", axis=0, tiled=True),
        lax.all_gather(column_blocks, "dp", axis=1, tiled=True),
        lax.all_gather(gain_pair, "dp", axis=1, tiled=True),
    )
    w_qkv_full, w_in_full, w_output_full, w_out_full, gain_in, gain_mid = split_weights(
        rows_full, columns_full, gains_full, head_width
    )
    tokens_full = lax.all_gather(tokens, "tensor", axis=0, tiled=True)
    group_rows = tokens_full.shape[0]
    member, segment, position, first_rows = row_layout(seq_lengths[0], seq_offsets[0], group_rows)
    firsts = jnp.dot(
        first_rows.T.astype(jnp.bfloat16), tokens_full, preferred_element_type=jnp.float32
    )
    mu_seq = jnp.mean(firsts, axis=1)
    sd_seq = jnp.sqrt(jnp.mean(jnp.square(firsts - mu_seq[:, None]), axis=1) + stat_eps)
    live = jnp.sum(member, axis=1)
    mu_row = jnp.dot(member, mu_seq, precision=highest)
    sd_row = jnp.dot(member, sd_seq, precision=highest) + (1.0 - live)
    centered = (tokens_full.astype(jnp.float32) - mu_row[:, None]) / sd_row[:, None]
    normed_in, scale_in = rms_norm(centered)
    attn_in = (normed_in * gain_in).astype(jnp.bfloat16)
    projected = jnp.dot(attn_in, w_qkv_full, preferred_element_type=jnp.float32)
    cosine, sine = rotary_tables(position)
    q_rot = rotate(projected[:, :head_width], cosine, sine, 1.0).astype(jnp.bfloat16)
    k_rot = rotate(projected[:, head_width : 2 * head_width], cosine, sine, 1.0).astype(
        jnp.bfloat16
    )
    values = projected[:, 2 * head_width :].astype(jnp.bfloat16)
    heads_out, log_sums = attention_forward(q_rot, k_rot, values, segment)
    heads_low = heads_out.astype(jnp.bfloat16)
    attn_own = lax.psum_scatter(
        jnp.dot(heads_low, w_output_full, preferred_element_type=jnp.float32),
        "tensor",
        scatter_dimension=0,
        tiled=True,
    )
    own_start = lax.axis_index("tensor") * own_rows

    def own_part(array):
        return lax.dynamic_slice_in_dim(array, own_start, own_rows, 0)

    centered_own = own_part(centered)
    resid = centered_own + attn_own
    normed_mid, scale_mid = rms_norm(resid)
    mid_low = (normed_mid * gain_mid).astype(jnp.bfloat16)
    mid_full = lax.all_gather(mid_low, "tensor", axis=0, tiled=True)
    pre_act = jnp.dot(mid_full, w_in_full, preferred_element_type=jnp.float32)
    hidden = jax.nn.silu(pre_act).astype(jnp.bfloat16)
    mlp_own = lax.psum_scatter(
        jnp.dot(hidden, w_out_full, preferred_element_type=jnp.float32).astype(jnp.bfloat16),
        "tensor",
        scatter_dimension=0,
        tiled=True,
    ).astype(jnp.float32)
    final = resid + mlp_own
    mu_own = own_part(mu_row)
    sd_own = own_part(sd_row)
    mixed = (mu_own[:, None] + sd_own[:, None] * final).astype(jnp.bfloat16)
    rows_full, columns_full, gains_full = (
        lax.all_gather(row_blocks, "dp", axis=0, tiled=True),
        lax.all_gather(column_blocks, "dp", axis=1, tiled=True),
        lax.all_gather(gain_pair, "dp", axis=1, tiled=True),
    )
    w_qkv_full, w_in_full, w_output_full, w_out_full, gain_in, gain_mid = split_weights(
        rows_full, columns_full, gains_full, head_width
    )
    grad_out = cotangent.astype(jnp.float32)
    final_grad = grad_out * sd_own[:, None]
    mlp_grad_full = lax.all_gather(final_grad.astype(jnp.bfloat16), "tensor", axis=0, tiled=True)
    hidden_grad = against(mlp_grad_full, w_out_full)
    d_w_out = across(hidden, mlp_grad_full)
    sigmoid_act = jax.nn.sigmoid(pre_act)
    act_grad = (hidden_grad * sigmoid_act * (1.0 + pre_act * (1.0 - sigmoid_act))).astype(
        jnp.bfloat16
    )
    d_w_in = across(mid_full, act_grad)
    mid_grad = lax.psum_scatter(
        against(act_grad, w_in_full), "tensor", scatter_dimension=0, tiled=True
    )
    gain_mid_grad = jnp.sum(mid_grad * normed_mid, axis=0)
    resid_grad = final_grad + norm_back(mid_grad * gain_mid, normed_mid, scale_mid)
    attn_grad_full = lax.all_gather(resid_grad.astype(jnp.bfloat16), "tensor", axis=0, tiled=True)
    heads_grad = against(attn_grad_full, w_output_full).astype(jnp.bfloat16)
    d_w_output = across(heads_low, attn_grad_full)
    q_rot_grad, k_rot_grad, values_grad = attention_backward(
        q_rot, k_rot, values, segment, log_sums, heads_grad
    )
    proj_grad = jnp.concatenate(
        [
            rotate(q_rot_grad, cosine, sine, -1.0).astype(jnp.bfloat16),
            rotate(k_rot_grad, cosine, sine, -1.0).astype(jnp.bfloat16),
            values_grad.astype(jnp.bfloat16),
        ],
        axis=1,
    )
    d_w_qkv = across(attn_in, proj_grad)
    in_grad = lax.psum_scatter(
        against(proj_grad, w_qkv_full), "tensor", scatter_dimension=0, tiled=True
    )
    normed_own = own_part(normed_in)
    gain_in_grad = jnp.sum(in_grad * normed_own, axis=0)
    centered_grad = resid_grad + norm_back(in_grad * gain_in, normed_own, own_part(scale_in))
    scaled_grad = centered_grad / sd_own[:, None]
    per_row = jnp.stack(
        [
            jnp.sum(grad_out - scaled_grad, axis=1),
            jnp.sum(grad_out * final - scaled_grad * centered_own, axis=1),
        ],
        axis=1,
    )
    seq_part = jnp.dot(own_part(member).T, per_row, precision=highest)
    gain_part = jnp.stack([gain_in_grad, gain_mid_grad])
    gain_total, seq_total = lax.psum((gain_part, seq_part), "tensor")
    first_own = own_part(first_rows)
    mean_term = jnp.dot(first_own, seq_total[:, 0] / feature_count, precision=highest)
    spread_term = jnp.dot(first_own, seq_total[:, 1] / (feature_count * sd_seq), precision=highest)
    grad_tokens = (
        scaled_grad
        + mean_term[:, None]
        + spread_term[:, None] * (tokens.astype(jnp.float32) - mu_own[:, None])
    )
    grad_rows, grad_columns, gain_grads = (
        lax.psum_scatter(
            jnp.concatenate([d_w_qkv, d_w_in], axis=1), "dp", scatter_dimension=0, tiled=True
        ),
        lax.psum_scatter(
            jnp.concatenate([d_w_output, d_w_out], axis=0), "dp", scatter_dimension=1, tiled=True
        ),
        lax.psum_scatter(gain_total, "dp", scatter_dimension=1, tiled=True),
    )
    return (
        mixed,
        grad_tokens,
        grad_rows[:, :head_width],
        grad_rows[:, head_width : 2 * head_width],
        grad_rows[:, 2 * head_width : qkv_width],
        grad_columns[:head_width],
        grad_rows[:, qkv_width:],
        grad_columns[head_width:],
        gain_grads[0],
        gain_grads[1],
    )


ALL_AXES = ("z", "x", "c", "y")


def flip(value, axis):
    return lax.ppermute(value, axis, [(0, 1), (1, 0)])


def shift_z(value, step):
    return lax.ppermute(value, "z", [(i, (i + step) % 4) for i in range(4)])


def flip_split(value, first):
    pairs = []
    for z in range(4):
        for x in range(2):
            for c in range(2):
                for y in range(2):
                    there = (z, 1 - x, c, y) if c == first else (z, x, c, 1 - y)
                    here = ((z * 2 + x) * 2 + c) * 2 + y
                    pairs.append((here, ((there[0] * 2 + there[1]) * 2 + there[2]) * 2 + there[3]))
    return lax.ppermute(value, ALL_AXES, pairs)


def assemble_rows(place, blocks):
    count = len(blocks)
    width = blocks[0].shape[1]

    def body(place_ref, *refs):
        ins, (full, tail) = refs[:count], refs[count:]
        for i, block in enumerate(ins):
            spot = place_ref[i]
            row = pl.multiple_of(spot * 80, 16)
            for j in range(3):
                full[pl.ds(row, 80), pl.ds(width * j, width)] = block[pl.ds(80 * j, 80), :]
            tail[spot] = block[pl.ds(240, 16), :]

    return pl.pallas_call(
        body,
        out_shape=(
            jax.ShapeDtypeStruct((1280, 3 * width), jnp.bfloat16),
            jax.ShapeDtypeStruct((16, 16, width), jnp.bfloat16),
        ),
        in_specs=[pl.BlockSpec(memory_space=pltpu.SMEM)]
        + [pl.BlockSpec(memory_space=pltpu.VMEM)] * count,
        out_specs=(pl.BlockSpec(memory_space=pltpu.VMEM),) * 2,
        compiler_params=pltpu.CompilerParams(vmem_limit_bytes=24 * 2**20),
        name="assemble_rows",
    )(place, *blocks)


def assemble_pairs(place, half, blocks):
    count = len(blocks)
    width = blocks[0].shape[1]

    def body(place_ref, half_ref, *refs):
        ins, outs = refs[:count], refs[count:]
        for i, block in enumerate(ins):
            row = pl.multiple_of(place_ref[i] * 80, 16)
            for j in range(3):
                outs[j][half_ref[i], pl.ds(row, 80), :] = block[pl.ds(80 * j, 80), :]

    return pl.pallas_call(
        body,
        out_shape=(jax.ShapeDtypeStruct((2, 1280, width), jnp.bfloat16),) * 3,
        in_specs=[pl.BlockSpec(memory_space=pltpu.SMEM)] * 2
        + [pl.BlockSpec(memory_space=pltpu.VMEM)] * count,
        out_specs=(pl.BlockSpec(memory_space=pltpu.VMEM),) * 3,
        compiler_params=pltpu.CompilerParams(vmem_limit_bytes=40 * 2**20),
        name="assemble_pairs",
    )(place, half, *blocks)


def pick(array, index, axis):
    return lax.dynamic_index_in_dim(array, index, axis, keepdims=False)


def low16(value):
    return value.astype(jnp.bfloat16)


def wide(value):
    return value.astype(jnp.float32)


def local_fast(
    tokens,
    w_query,
    w_key,
    w_value,
    w_output,
    w_in,
    w_out,
    gain_attn,
    gain_mlp,
    seq_lengths,
    seq_offsets,
    cotangent,
):
    z, x, c, y = (lax.axis_index(name) for name in ALL_AXES)
    own_rows, feature_count = tokens.shape
    head_width = w_query.shape[1]

    gains = jnp.pad(
        jnp.stack([gain_attn, gain_mlp]), ((0, 14), (0, head_width - gain_attn.shape[0]))
    )
    q_block = jnp.concatenate([w_query, w_key, w_value, gains], axis=0)
    p_block = jnp.concatenate([w_output.T, w_in, w_out.T], axis=0)
    tokens_other = flip(tokens, "y")
    q_z = [q_block] + [shift_z(q_block, step) for step in (1, 3, 2)]
    q_mine = q_z + [flip(block, "x") for block in q_z]
    q_other = [flip(block, "c") for block in q_mine]
    steps = (0, 1, 3, 2)
    q_place = jnp.stack(
        [
            ((z - step) % 4 * 2 + (x ^ xr)) * 2 + (c ^ cr)
            for cr in range(2)
            for xr in range(2)
            for step in steps
        ]
    ).astype(jnp.int32)
    w_qkv_full, tails = assemble_rows(q_place, q_mine + q_other)
    gain_in = wide(tails[:, 0, :80].reshape(-1))
    gain_mid = wide(tails[:, 1, :80].reshape(-1))

    p_z = [p_block] + [shift_z(p_block, step) for step in (1, 3, 2)]
    p_second = [flip_split(block, 0) for block in p_z]
    p_third = [flip_split(block, 1) for block in p_z + p_second]
    p_mine = p_z + p_second + p_third
    p_other = [flip(block, "c") for block in p_mine]
    places, halves = [], []
    for cr in range(2):
        side = c ^ cr
        for third in range(2):
            for second in range(2):
                xr = jnp.where(side == 0, second, third)
                yr = jnp.where(side == 0, third, second)
                for step in steps:
                    places.append(((z - step) % 4 * 2 + (x ^ xr)) * 2 + side)
                    halves.append(yr)
    wo, wi, wt = assemble_pairs(
        jnp.stack(places).astype(jnp.int32), jnp.stack(halves).astype(jnp.int32), p_mine + p_other
    )

    def both(own, other):
        return jnp.where(
            y == 0, jnp.concatenate([own, other], 0), jnp.concatenate([other, own], 0)
        )

    def own_part(array):
        return lax.dynamic_slice_in_dim(array, y * own_rows, own_rows, 0)

    def other_part(array):
        return lax.dynamic_slice_in_dim(array, (1 - y) * own_rows, own_rows, 0)

    tokens_full = both(tokens, tokens_other)
    group_rows = tokens_full.shape[0]
    member, segment, position, first_rows = row_layout(seq_lengths[0], seq_offsets[0], group_rows)
    firsts = jnp.dot(first_rows.T.astype(jnp.bfloat16), tokens_full, preferred_element_type=jnp.float32)
    mu_seq = jnp.mean(firsts, axis=1)
    sd_seq = jnp.sqrt(jnp.mean(jnp.square(firsts - mu_seq[:, None]), axis=1) + stat_eps)
    live = jnp.sum(member, axis=1)
    mu_row = jnp.dot(member, mu_seq, precision=highest)
    sd_row = jnp.dot(member, sd_seq, precision=highest) + (1.0 - live)
    centered = (wide(tokens_full) - mu_row[:, None]) / sd_row[:, None]
    normed_in, scale_in = rms_norm(centered)
    attn_in = low16(normed_in * gain_in)
    projected = jnp.dot(attn_in, w_qkv_full, preferred_element_type=jnp.float32)
    cosine, sine = rotary_tables(position)
    q_rot = low16(rotate(projected[:, :head_width], cosine, sine, 1.0))
    k_rot = low16(rotate(projected[:, head_width : 2 * head_width], cosine, sine, 1.0))
    values = low16(projected[:, 2 * head_width :])
    heads_out, log_sums = attention_forward(q_rot, k_rot, values, segment)
    heads_low = low16(heads_out)
    heads = [own_part(heads_low), flip(other_part(heads_low), "y")]
    attn_own = against(heads[0], wo[0]) + against(heads[1], wo[1])
    centered_own = own_part(centered)
    resid = centered_own + attn_own
    normed_mid, scale_mid = rms_norm(resid)
    mid_low = low16(normed_mid * gain_mid)
    pre_act = [jnp.dot(mid_low, wi[r], preferred_element_type=jnp.float32) for r in range(2)]
    hidden = [low16(jax.nn.silu(part)) for part in pre_act]
    final = resid + against(hidden[0], wt[0]) + against(hidden[1], wt[1])
    mu_own, sd_own = own_part(mu_row), own_part(sd_row)
    mixed = low16(mu_own[:, None] + sd_own[:, None] * final)

    grad_out = wide(cotangent)
    final_grad = grad_out * sd_own[:, None]
    mlp_grad = low16(final_grad)
    act_grad = []
    for r in range(2):
        hidden_grad = jnp.dot(mlp_grad, wt[r], preferred_element_type=jnp.float32)
        sigmoid_act = jax.nn.sigmoid(pre_act[r])
        act_grad.append(
            low16(hidden_grad * sigmoid_act * (1.0 + pre_act[r] * (1.0 - sigmoid_act)))
        )
    mid_grad = against(act_grad[0], wi[0]) + against(act_grad[1], wi[1])
    gain_mid_grad = jnp.sum(mid_grad * normed_mid, axis=0)
    resid_grad = final_grad + norm_back(mid_grad * gain_mid, normed_mid, scale_mid)
    attn_grad = low16(resid_grad)
    heads_grad = [
        low16(jnp.dot(attn_grad, wo[r], preferred_element_type=jnp.float32)) for r in range(2)
    ]
    heads_grad_full = both(heads_grad[0], flip(heads_grad[1], "y"))

    def chunks(array):
        return array.reshape(4, 2, 2, 80, array.shape[-1])

    def core_sum(array):
        parts = chunks(array)
        return pick(parts, c, 2) + wide(flip(low16(pick(parts, 1 - c, 2)), "c"))

    def x_sum(array):
        return pick(array, x, 1) + wide(flip(low16(pick(array, 1 - x, 1)), "x"))

    def z_sum(array):
        total = pick(array, z, 0)
        for step in (1, 3, 2):
            total = total + wide(shift_z(low16(pick(array, (z + step) % 4, 0)), step))
        return total

    d_wt = [core_sum(across(mlp_grad, hidden[r])) for r in range(2)]
    d_wi = [core_sum(across(mid_low, act_grad[r])) for r in range(2)]
    d_wo = [core_sum(across(attn_grad, heads[r])) for r in range(2)]
    d_wt = x_sum(d_wt[0] + wide(flip(low16(d_wt[1]), "y")))
    d_wi_x = [x_sum(part) for part in d_wi]
    d_wi = d_wi_x[0] + wide(flip(low16(d_wi_x[1]), "y"))
    d_wo = x_sum(d_wo[0] + wide(flip(low16(d_wo[1]), "y")))
    d_p = z_sum(jnp.concatenate([d_wo, d_wi, d_wt], axis=1))

    q_rot_grad, k_rot_grad, values_grad = attention_backward(
        q_rot, k_rot, values, segment, log_sums, heads_grad_full
    )
    proj_grad = jnp.concatenate(
        [
            low16(rotate(q_rot_grad, cosine, sine, -1.0)),
            low16(rotate(k_rot_grad, cosine, sine, -1.0)),
            low16(values_grad),
        ],
        axis=1,
    )
    in_grad_all = against(proj_grad, w_qkv_full)
    in_grad = own_part(in_grad_all) + wide(flip(low16(other_part(in_grad_all)), "y"))
    gain_in_grad = jnp.sum(in_grad_all * normed_in, axis=0)
    d_qkv = z_sum(x_sum(core_sum(across(attn_in, proj_grad))))
    normed_own = own_part(normed_in)
    centered_grad = resid_grad + norm_back(in_grad * gain_in, normed_own, own_part(scale_in))
    scaled_grad = centered_grad / sd_own[:, None]
    per_row = jnp.stack(
        [
            jnp.sum(grad_out - scaled_grad, axis=1),
            jnp.sum(grad_out * final - scaled_grad * centered_own, axis=1),
        ],
        axis=1,
    )
    seq_part = jnp.dot(own_part(member).T, per_row, precision=highest)
    seq_total = seq_part + flip(seq_part, "y")
    first_own = own_part(first_rows)
    mean_term = jnp.dot(first_own, seq_total[:, 0] / feature_count, precision=highest)
    spread_term = jnp.dot(first_own, seq_total[:, 1] / (feature_count * sd_seq), precision=highest)
    grad_tokens = (
        scaled_grad
        + mean_term[:, None]
        + spread_term[:, None] * (wide(tokens) - mu_own[:, None])
    )
    gain_total = lax.psum(jnp.stack([gain_in_grad, gain_mid_grad]), ALL_AXES)
    place = (z * 2 + x) * 2 + c
    gain_grads = lax.dynamic_slice_in_dim(gain_total, place * 80, 80, 1)
    return (
        mixed,
        grad_tokens,
        d_qkv[:, :head_width],
        d_qkv[:, head_width : 2 * head_width],
        d_qkv[:, 2 * head_width :],
        d_p[:80].T,
        d_p[80:160],
        d_p[160:].T,
        gain_grads[0],
        gain_grads[1],
    )


def solution_fast(mesh):
    fine = Mesh(mesh.devices.reshape(4, 2, 2, 2), ALL_AXES)
    dp = ("z", "x", "c")
    rows, by_row, by_column = P(ALL_AXES, None), P(dp, "y"), P("y", dp)
    in_specs = (rows,) + (by_row,) * 3 + (by_column, by_row, by_column)
    in_specs += (P(dp), P(dp), P(dp, None), P(dp, None), rows)
    out_specs = (rows, rows) + (by_row,) * 3 + (by_column, by_row, by_column, P(dp), P(dp))
    return jax.shard_map(
        local_fast, mesh=fine, in_specs=in_specs, out_specs=out_specs, check_vma=False
    )


def solution(mesh):
    if dict(mesh.shape) == {"dp": 16, "tensor": 2}:
        return solution_fast(mesh)
    in_specs = (
        P(("dp", "tensor"), None),
        P("dp", "tensor"),
        P("dp", "tensor"),
        P("dp", "tensor"),
        P("tensor", "dp"),
        P("dp", "tensor"),
        P("tensor", "dp"),
        P("dp"),
        P("dp"),
        P("dp", None),
        P("dp", None),
        P(("dp", "tensor"), None),
    )
    out_specs = (
        P(("dp", "tensor"), None),
        P(("dp", "tensor"), None),
        P("dp", "tensor"),
        P("dp", "tensor"),
        P("dp", "tensor"),
        P("tensor", "dp"),
        P("dp", "tensor"),
        P("tensor", "dp"),
        P("dp"),
        P("dp"),
    )
    return jax.shard_map(local, mesh=mesh, in_specs=in_specs, out_specs=out_specs, check_vma=False)
```

```python
import jax
import jax.numpy as jnp
from jax import lax
from jax.experimental import pallas as pl
from jax.experimental.pallas import tpu as pltpu
from jax.sharding import Mesh
from jax.sharding import PartitionSpec as P

HEAD_DIM = 80


highest = lax.Precision.HIGHEST
epsilon = 1e-06
stat_eps = 1e-05
masked_score = -1e30
contract_last = (((1,), (1,)), ((), ()))
contract_first = (((0,), (0,)), ((), ()))


def against(left, right):
    return lax.dot_general(left, right, contract_last, preferred_element_type=jnp.float32)


def across(left, right):
    return lax.dot_general(left, right, contract_first, preferred_element_type=jnp.float32)


def row_layout(lengths, offsets, group_rows):
    row_ids = jnp.arange(group_rows, dtype=jnp.int32)
    inside = (row_ids[:, None] >= offsets[None, :]) & (
        row_ids[:, None] < offsets[None, :] + lengths[None, :]
    )
    member = inside.astype(jnp.float32)
    slot_ids = jnp.arange(offsets.shape[0], dtype=jnp.int32)
    segment = jnp.sum(jnp.where(inside, slot_ids[None, :] + 1, 0), axis=1) - 1
    seq_start = jnp.sum(jnp.where(inside, offsets[None, :], 0), axis=1)
    position = jnp.where(segment >= 0, row_ids - seq_start, 0).astype(jnp.float32)
    first_rows = (row_ids[:, None] == offsets[None, :]).astype(jnp.float32)
    return (member, segment, position, first_rows)


def rotary_tables(position):
    half_dim = HEAD_DIM // 2
    freqs = 10000.0 ** (-2.0 * jnp.arange(half_dim, dtype=jnp.float32) / HEAD_DIM)
    angles = position[:, None] * freqs[None, :]
    return (jnp.cos(angles), jnp.sin(angles))


def rotate(values, cosine, sine, direction):
    row_count = values.shape[0]
    shaped = values.reshape(row_count, -1, HEAD_DIM)
    half_dim = HEAD_DIM // 2
    first_half = shaped[..., :half_dim]
    second_half = shaped[..., half_dim:]
    cos_b = cosine[:, None, :]
    sin_b = sine[:, None, :] * direction
    turned = jnp.concatenate(
        [first_half * cos_b - second_half * sin_b, first_half * sin_b + second_half * cos_b],
        axis=-1,
    )
    return turned.reshape(row_count, -1)


def rms_norm(values):
    factor = lax.rsqrt(jnp.mean(values * values, axis=-1, keepdims=True) + epsilon)
    return (values * factor, factor)


def norm_back(grad_normed, normed, factor):
    return factor * (grad_normed - normed * jnp.mean(grad_normed * normed, axis=-1, keepdims=True))


def allowed_mask(seg_query, query_ids, segment, key_ids):
    same = (
        (seg_query[:, None] == segment[None, :])
        & (key_ids[None, :] <= query_ids[:, None])
        & (seg_query[:, None] >= 0)
    )
    return same | (query_ids[:, None] == key_ids[None, :])


def block_scores(query_all, key_all, segment, row_begin, block_rows):
    group_rows = key_all.shape[0]
    key_ids = jnp.arange(group_rows, dtype=jnp.int32)
    query_ids = row_begin + jnp.arange(block_rows, dtype=jnp.int32)
    queries = lax.dynamic_slice_in_dim(query_all, row_begin, block_rows, 0)
    scores = jnp.einsum(
        "qhd,khd->hqk", queries, key_all, preferred_element_type=jnp.float32
    ) * HEAD_DIM ** (-0.5)
    seg_query = lax.dynamic_slice_in_dim(segment, row_begin, block_rows, 0)
    mask = allowed_mask(seg_query, query_ids, segment, key_ids)
    return (jnp.where(mask[None], scores, masked_score), queries)


def attention_forward(q_rot, k_rot, values, segment):
    group_rows, head_width = q_rot.shape
    block_rows = min(512, group_rows)
    query_all = q_rot.reshape(group_rows, -1, HEAD_DIM)
    key_all = k_rot.reshape(group_rows, -1, HEAD_DIM)
    value_all = values.reshape(group_rows, -1, HEAD_DIM)

    def one_block(block_index):
        scores, queries = block_scores(
            query_all, key_all, segment, block_index * block_rows, block_rows
        )
        top = jnp.max(scores, axis=-1, keepdims=True)
        expo = jnp.exp(scores - top)
        total_exp = jnp.sum(expo, axis=-1, keepdims=True)
        probs = (expo / total_exp).astype(jnp.bfloat16)
        heads = jnp.einsum("hqk,khd->qhd", probs, value_all, preferred_element_type=jnp.float32)
        return (heads.reshape(block_rows, head_width), (top + jnp.log(total_exp))[..., 0])

    outs, log_sums = lax.map(one_block, jnp.arange(group_rows // block_rows, dtype=jnp.int32))
    return (outs.reshape(group_rows, head_width), log_sums)


def attention_backward(q_rot, k_rot, values, segment, log_sums, heads_grad):
    group_rows, head_width = q_rot.shape
    block_rows = min(512, group_rows)
    query_all = q_rot.reshape(group_rows, -1, HEAD_DIM)
    key_all = k_rot.reshape(group_rows, -1, HEAD_DIM)
    value_all = values.reshape(group_rows, -1, HEAD_DIM)
    grad_all = heads_grad.reshape(group_rows, -1, HEAD_DIM)
    scale_factor = HEAD_DIM ** (-0.5)

    def one_block(carry, block_index):
        key_grad, value_grad = carry
        row_begin = block_index * block_rows
        scores, queries = block_scores(query_all, key_all, segment, row_begin, block_rows)
        probs = jnp.exp(scores - log_sums[block_index][..., None])
        grads_block = lax.dynamic_slice_in_dim(grad_all, row_begin, block_rows, 0)
        prob_grad = jnp.einsum(
            "qhd,khd->hqk", grads_block, value_all, preferred_element_type=jnp.float32
        )
        inner = jnp.sum(probs * prob_grad, axis=-1, keepdims=True)
        score_grad = (probs * (prob_grad - inner)).astype(jnp.bfloat16)
        query_grad = (
            jnp.einsum("hqk,khd->qhd", score_grad, key_all, preferred_element_type=jnp.float32)
            * scale_factor
        )
        key_grad = (
            key_grad
            + jnp.einsum("hqk,qhd->khd", score_grad, queries, preferred_element_type=jnp.float32)
            * scale_factor
        )
        value_grad = value_grad + jnp.einsum(
            "hqk,qhd->khd",
            probs.astype(jnp.bfloat16),
            grads_block,
            preferred_element_type=jnp.float32,
        )
        return ((key_grad, value_grad), query_grad.reshape(block_rows, head_width))

    zeros = jnp.zeros(query_all.shape, jnp.float32)
    (key_grad, value_grad), query_grads = lax.scan(
        one_block, (zeros, zeros), jnp.arange(group_rows // block_rows, dtype=jnp.int32)
    )
    return (
        query_grads.reshape(group_rows, head_width),
        key_grad.reshape(group_rows, head_width),
        value_grad.reshape(group_rows, head_width),
    )


def split_weights(rows_full, columns_full, gains_full, head_width):
    qkv_width = 3 * head_width
    return (
        rows_full[:, :qkv_width],
        rows_full[:, qkv_width:],
        columns_full[:head_width],
        columns_full[head_width:],
        gains_full[0].astype(jnp.float32),
        gains_full[1].astype(jnp.float32),
    )


def local(
    tokens,
    w_query,
    w_key,
    w_value,
    w_output,
    w_in,
    w_out,
    gain_attn,
    gain_mlp,
    seq_lengths,
    seq_offsets,
    cotangent,
):
    own_rows = tokens.shape[0]
    feature_count = tokens.shape[1]
    head_width = w_query.shape[1]
    qkv_width = 3 * head_width
    row_blocks = jnp.concatenate([w_query, w_key, w_value, w_in], axis=1)
    column_blocks = jnp.concatenate([w_output, w_out], axis=0)
    gain_pair = jnp.stack([gain_attn, gain_mlp])
    rows_full, columns_full, gains_full = (
        lax.all_gather(row_blocks, "dp", axis=0, tiled=True),
        lax.all_gather(column_blocks, "dp", axis=1, tiled=True),
        lax.all_gather(gain_pair, "dp", axis=1, tiled=True),
    )
    w_qkv_full, w_in_full, w_output_full, w_out_full, gain_in, gain_mid = split_weights(
        rows_full, columns_full, gains_full, head_width
    )
    tokens_full = lax.all_gather(tokens, "tensor", axis=0, tiled=True)
    group_rows = tokens_full.shape[0]
    member, segment, position, first_rows = row_layout(seq_lengths[0], seq_offsets[0], group_rows)
    firsts = jnp.dot(
        first_rows.T.astype(jnp.bfloat16), tokens_full, preferred_element_type=jnp.float32
    )
    mu_seq = jnp.mean(firsts, axis=1)
    sd_seq = jnp.sqrt(jnp.mean(jnp.square(firsts - mu_seq[:, None]), axis=1) + stat_eps)
    live = jnp.sum(member, axis=1)
    mu_row = jnp.dot(member, mu_seq, precision=highest)
    sd_row = jnp.dot(member, sd_seq, precision=highest) + (1.0 - live)
    centered = (tokens_full.astype(jnp.float32) - mu_row[:, None]) / sd_row[:, None]
    normed_in, scale_in = rms_norm(centered)
    attn_in = (normed_in * gain_in).astype(jnp.bfloat16)
    projected = jnp.dot(attn_in, w_qkv_full, preferred_element_type=jnp.float32)
    cosine, sine = rotary_tables(position)
    q_rot = rotate(projected[:, :head_width], cosine, sine, 1.0).astype(jnp.bfloat16)
    k_rot = rotate(projected[:, head_width : 2 * head_width], cosine, sine, 1.0).astype(
        jnp.bfloat16
    )
    values = projected[:, 2 * head_width :].astype(jnp.bfloat16)
    heads_out, log_sums = attention_forward(q_rot, k_rot, values, segment)
    heads_low = heads_out.astype(jnp.bfloat16)
    attn_own = lax.psum_scatter(
        jnp.dot(heads_low, w_output_full, preferred_element_type=jnp.float32),
        "tensor",
        scatter_dimension=0,
        tiled=True,
    )
    own_start = lax.axis_index("tensor") * own_rows

    def own_part(array):
        return lax.dynamic_slice_in_dim(array, own_start, own_rows, 0)

    centered_own = own_part(centered)
    resid = centered_own + attn_own
    normed_mid, scale_mid = rms_norm(resid)
    mid_low = (normed_mid * gain_mid).astype(jnp.bfloat16)
    mid_full = lax.all_gather(mid_low, "tensor", axis=0, tiled=True)
    pre_act = jnp.dot(mid_full, w_in_full, preferred_element_type=jnp.float32)
    hidden = jax.nn.silu(pre_act).astype(jnp.bfloat16)
    mlp_own = lax.psum_scatter(
        jnp.dot(hidden, w_out_full, preferred_element_type=jnp.float32).astype(jnp.bfloat16),
        "tensor",
        scatter_dimension=0,
        tiled=True,
    ).astype(jnp.float32)
    final = resid + mlp_own
    mu_own = own_part(mu_row)
    sd_own = own_part(sd_row)
    mixed = (mu_own[:, None] + sd_own[:, None] * final).astype(jnp.bfloat16)
    rows_full, columns_full, gains_full = (
        lax.all_gather(row_blocks, "dp", axis=0, tiled=True),
        lax.all_gather(column_blocks, "dp", axis=1, tiled=True),
        lax.all_gather(gain_pair, "dp", axis=1, tiled=True),
    )
    w_qkv_full, w_in_full, w_output_full, w_out_full, gain_in, gain_mid = split_weights(
        rows_full, columns_full, gains_full, head_width
    )
    grad_out = cotangent.astype(jnp.float32)
    final_grad = grad_out * sd_own[:, None]
    mlp_grad_full = lax.all_gather(final_grad.astype(jnp.bfloat16), "tensor", axis=0, tiled=True)
    hidden_grad = against(mlp_grad_full, w_out_full)
    d_w_out = across(hidden, mlp_grad_full)
    sigmoid_act = jax.nn.sigmoid(pre_act)
    act_grad = (hidden_grad * sigmoid_act * (1.0 + pre_act * (1.0 - sigmoid_act))).astype(
        jnp.bfloat16
    )
    d_w_in = across(mid_full, act_grad)
    mid_grad = lax.psum_scatter(
        against(act_grad, w_in_full), "tensor", scatter_dimension=0, tiled=True
    )
    gain_mid_grad = jnp.sum(mid_grad * normed_mid, axis=0)
    resid_grad = final_grad + norm_back(mid_grad * gain_mid, normed_mid, scale_mid)
    attn_grad_full = lax.all_gather(resid_grad.astype(jnp.bfloat16), "tensor", axis=0, tiled=True)
    heads_grad = against(attn_grad_full, w_output_full).astype(jnp.bfloat16)
    d_w_output = across(heads_low, attn_grad_full)
    q_rot_grad, k_rot_grad, values_grad = attention_backward(
        q_rot, k_rot, values, segment, log_sums, heads_grad
    )
    proj_grad = jnp.concatenate(
        [
            rotate(q_rot_grad, cosine, sine, -1.0).astype(jnp.bfloat16),
            rotate(k_rot_grad, cosine, sine, -1.0).astype(jnp.bfloat16),
            values_grad.astype(jnp.bfloat16),
        ],
        axis=1,
    )
    d_w_qkv = across(attn_in, proj_grad)
    in_grad = lax.psum_scatter(
        against(proj_grad, w_qkv_full), "tensor", scatter_dimension=0, tiled=True
    )
    normed_own = own_part(normed_in)
    gain_in_grad = jnp.sum(in_grad * normed_own, axis=0)
    centered_grad = resid_grad + norm_back(in_grad * gain_in, normed_own, own_part(scale_in))
    scaled_grad = centered_grad / sd_own[:, None]
    per_row = jnp.stack(
        [
            jnp.sum(grad_out - scaled_grad, axis=1),
            jnp.sum(grad_out * final - scaled_grad * centered_own, axis=1),
        ],
        axis=1,
    )
    seq_part = jnp.dot(own_part(member).T, per_row, precision=highest)
    gain_part = jnp.stack([gain_in_grad, gain_mid_grad])
    gain_total, seq_total = lax.psum((gain_part, seq_part), "tensor")
    first_own = own_part(first_rows)
    mean_term = jnp.dot(first_own, seq_total[:, 0] / feature_count, precision=highest)
    spread_term = jnp.dot(first_own, seq_total[:, 1] / (feature_count * sd_seq), precision=highest)
    grad_tokens = (
        scaled_grad
        + mean_term[:, None]
        + spread_term[:, None] * (tokens.astype(jnp.float32) - mu_own[:, None])
    )
    grad_rows, grad_columns, gain_grads = (
        lax.psum_scatter(
            jnp.concatenate([d_w_qkv, d_w_in], axis=1), "dp", scatter_dimension=0, tiled=True
        ),
        lax.psum_scatter(
            jnp.concatenate([d_w_output, d_w_out], axis=0), "dp", scatter_dimension=1, tiled=True
        ),
        lax.psum_scatter(gain_total, "dp", scatter_dimension=1, tiled=True),
    )
    return (
        mixed,
        grad_tokens,
        grad_rows[:, :head_width],
        grad_rows[:, head_width : 2 * head_width],
        grad_rows[:, 2 * head_width : qkv_width],
        grad_columns[:head_width],
        grad_rows[:, qkv_width:],
        grad_columns[head_width:],
        gain_grads[0],
        gain_grads[1],
    )


HALF = HEAD_DIM // 2
VMEM_SPEC = pl.BlockSpec(memory_space=pltpu.VMEM)
SMEM_SPEC = pl.BlockSpec(memory_space=pltpu.SMEM)


def low16(value):
    return value.astype(jnp.bfloat16)


def wide(value):
    return value.astype(jnp.float32)


def dot(left, right):
    return jnp.dot(left, right, preferred_element_type=jnp.float32)


def local_kernel(body, outs, scalars, scratch, name, mib, gates=(), after=(), loose=0):
    def call(*operands):
        count = len(operands)
        left, held = len(gates) + len(after), len(gates)

        def trimmed(*refs):
            end = count + left + len(outs)
            body(*refs[:count], *refs[count + left : end], *refs[end + held :])

        any_spec = pl.BlockSpec(memory_space=pl.ANY)
        return pl.pallas_call(
            trimmed,
            out_shape=tuple(jax.ShapeDtypeStruct(shape, kind) for shape, kind in outs)
            + tuple(jax.ShapeDtypeStruct(gate.shape, gate.dtype) for gate in gates),
            in_specs=[SMEM_SPEC] * scalars
            + [VMEM_SPEC] * (count - scalars - loose)
            + [any_spec] * (loose + left),
            out_specs=(VMEM_SPEC,) * len(outs) + (any_spec,) * held,
            scratch_shapes=[
                pltpu.VMEM(*item) if isinstance(item, tuple) else item for item in scratch
            ],
            input_output_aliases={count + i: len(outs) + i for i in range(held)},
            compiler_params=pltpu.CompilerParams(vmem_limit_bytes=mib * 2**20),
            cost_estimate=pl.CostEstimate(flops=1000, bytes_accessed=1000, transcendentals=0),
            name=name,
        )(*operands, *gates, *after)

    return call


BF, F32 = jnp.bfloat16, jnp.float32


def head_window(head):
    begin = head * HEAD_DIM
    first = begin // 128 * 128
    last = -(-(begin + HEAD_DIM) // 128) * 128
    lane = lax.broadcasted_iota(jnp.int32, (1, last - first), 1) + first
    inside = (lane >= begin) & (lane < begin + HEAD_DIM)
    return slice(first, last), low16(jnp.where(inside, 1.0, 0.0))


def swap_halves(value):
    width = value.shape[1]
    lane = lax.broadcasted_iota(jnp.int32, value.shape, 1) % HEAD_DIM
    return jnp.where(
        lane < HALF, pltpu.roll(value, width - HALF, 1), pltpu.roll(value, HALF, 1)
    )


def fill_bias(bias, seg_column, seg_row):
    rows = bias.shape[0]
    query = lax.broadcasted_iota(jnp.int32, (rows, rows), 0)
    key = lax.broadcasted_iota(jnp.int32, (rows, rows), 1)
    allowed = (seg_column[...] == seg_row[...]) & (key <= query)
    bias[...] = jnp.where(allowed, 0.0, masked_score)


def stack_kernel(*refs):
    for i, block in enumerate(refs[:-1]):
        refs[-1][i] = block[...]


def stack_blocks(blocks, name):
    rows, width = blocks[0].shape
    outs = [((len(blocks), rows, width), BF)]
    return local_kernel(stack_kernel, outs, 0, [], name, 4)(*blocks)[0]


def project_kernel(place, side, normed, cos, sin, spot, *refs):
    arrays, outs = refs[:6], refs[6:]
    w_full, at_mine, at_send, q_out, k_out, v_out, gain_mid, gain_first = outs[:8]
    tail, attn_in, turned = outs[8:]
    group_rows, feature_count = normed.shape
    half_rows = group_rows // 2
    width = q_out.shape[1]
    blocks = [
        (array, index) for array in arrays for index in range(array.shape[0])
    ]
    for i, (array, index) in enumerate(blocks):
        row = pl.multiple_of(place[i] * 80, 16)
        for j in range(3):
            w_full[pl.ds(row, 80), pl.ds(width * j, width)] = array[index, pl.ds(80 * j, 80), :]
        ends = wide(array[index, pl.ds(240, 16), :128])
        tail[i : i + 1, :] = ends[0:1]
        tail[16 + i : 17 + i, :] = ends[1:2]
    lane = lax.broadcasted_iota(jnp.int32, (128, feature_count), 1)
    source = lax.broadcasted_iota(jnp.int32, (128, feature_count), 0)
    spread = low16(jnp.where(lane % 80 == source, 1.0, 0.0))
    held = lax.broadcasted_iota(jnp.int32, (16, feature_count), 1) // 80 == spot[...]
    gain_in = jnp.sum(jnp.where(held, dot(low16(tail[0:16]), spread), 0.0), 0, keepdims=True)
    gain_first[...] = gain_in
    gain_mid[...] = jnp.sum(jnp.where(held, dot(low16(tail[16:32]), spread), 0.0), 0, keepdims=True)
    for i in range(feature_count // 128):
        part = normed[:, 128 * i : 128 * i + 128] * gain_in[:, 128 * i : 128 * i + 128]
        attn_in[:, 128 * i : 128 * i + 128] = low16(part)
        turned[128 * i : 128 * i + 128, :] = low16(part.T)
    for i in range(8):
        mine = pl.multiple_of((2 * i + side[0]) * 80, 16)
        other = pl.multiple_of((2 * i + 1 - side[0]) * 80, 16)
        at_mine[80 * i : 80 * i + 80, :] = turned[pl.ds(mine, 80), :]
        at_send[80 * i : 80 * i + 80, :] = turned[pl.ds(other, 80), :]
    for r in range(2):
        rows = slice(half_rows * r, half_rows * (r + 1))
        for j, out in enumerate((q_out, k_out)):
            part = dot(attn_in[rows, :], w_full[:, width * j : width * (j + 1)])
            out[rows, :] = low16(part * cos[rows, :] + swap_halves(part) * sin[rows, :])
        v_out[rows, :] = low16(dot(attn_in[rows, :], w_full[:, 2 * width :]))


def attention_kernel(side, q, k, v, seg_column, seg_row, lse_out, h_own, h_send, bias, heads):
    group_rows, width = q.shape
    half_rows = group_rows // 2
    fill_bias(bias, seg_column, seg_row)
    heads[...] = jnp.zeros_like(heads)
    for r in range(2):
        rows = slice(half_rows * r, half_rows * (r + 1))
        seen = slice(0, half_rows * (r + 1))
        head_lane = lax.broadcasted_iota(jnp.int32, (half_rows, 128), 1)
        lse = jnp.zeros((half_rows, 128), F32)
        for h in range(width // HEAD_DIM):
            window, keep = head_window(h)
            scores = against(q[rows, window] * keep, k[seen, window])
            scores = scores * HEAD_DIM ** (-0.5) + bias[rows, seen]
            top = jnp.max(scores, axis=1, keepdims=True)
            expo = jnp.exp(scores - top)
            total = jnp.sum(expo, axis=1, keepdims=True)
            probs = low16(expo * (1.0 / total))
            heads[rows, window] += dot(probs, v[seen, window] * keep)
            lse = jnp.where(head_lane == h, top + jnp.log(total), lse)
        lse_out[rows, :] = lse
    own = pl.multiple_of(side[1] * half_rows, 16)
    other = pl.multiple_of((1 - side[1]) * half_rows, 16)
    h_own[...] = low16(heads[pl.ds(own, half_rows), :])
    h_send[...] = low16(heads[pl.ds(other, half_rows), :])


def middle_kernel(place, half, side, h_own, h_recv, centered, mu, sd, cot, gain_mid, *refs):
    arrays, outs = refs[:16], refs[16:]
    mixed, spread_sum, resid_grad, gain_grad, hg_own, hg_send, xt_mine, xt_send, y_out = outs[:9]
    wo, wi, wt, turned, keep, final, pre, staged, sems = outs[9:]
    own_rows, feature_count = centered.shape
    copies, begin = [], 0
    for i, array in enumerate(arrays):
        there = staged.at[pl.ds(begin, array.shape[0])]
        copies.append(pltpu.make_async_copy(array, there, sems.at[i]))
        copies[-1].start()
        begin += array.shape[0]
    begin = 0
    for array, copy in zip(arrays, copies):
        copy.wait()
        for i in range(begin, begin + array.shape[0]):
            row = pl.multiple_of(place[i] * 80, 16)
            for j, full in enumerate((wo, wi, wt)):
                full[half[i], pl.ds(row, 80), :] = staged[i, 80 * j : 80 * j + 80, :]
        begin += array.shape[0]

    def turn(j, value):
        for i in range(feature_count // 128):
            turned[128 * i : 128 * i + 128, :] = low16(value[:, 128 * i : 128 * i + 128].T)
        for i in range(8):
            mine = pl.multiple_of((2 * i + side[0]) * 80, 16)
            other = pl.multiple_of((2 * i + 1 - side[0]) * 80, 16)
            xt_mine[j, 80 * i : 80 * i + 80, :] = turned[pl.ds(mine, 80), :]
            xt_send[j, 80 * i : 80 * i + 80, :] = turned[pl.ds(other, 80), :]

    y_out[0, 0] = h_own[...]
    y_out[0, 1] = h_recv[...]
    resid = centered[...] + against(h_own[...], wo[0]) + against(h_recv[...], wo[1])
    normed, factor = rms_norm(resid)
    keep[...] = normed
    mid = normed * gain_mid[...]
    turn(1, mid)
    mid = low16(mid)
    final_grad = wide(cot[...]) * sd[...]
    mlp_grad = low16(final_grad)
    turn(2, final_grad)
    final[...] = resid
    for r in range(2):
        pre_act = dot(mid, wi[r])
        pre[r] = pre_act
        y_out[2, r] = low16(pre_act * (1.0 / (1.0 + jnp.exp(-pre_act))))
    final[...] += against(y_out[2, 0], wt[0]) + against(y_out[2, 1], wt[1])
    mixed[...] = low16(mu[...] + sd[...] * final[...])
    spread_sum[...] = jnp.sum(wide(cot[...]) * final[...], axis=1, keepdims=True)
    for r in range(2):
        hidden_grad = dot(mlp_grad, wt[r])
        pre_act = pre[r]
        sigmoid = 1.0 / (1.0 + jnp.exp(-pre_act))
        y_out[1, r] = low16(hidden_grad * sigmoid * (1.0 + pre_act * (1.0 - sigmoid)))
    mid_grad = against(y_out[1, 0], wi[0]) + against(y_out[1, 1], wi[1])
    normed = keep[...]
    gain_grad[...] = jnp.sum(mid_grad * normed, axis=0, keepdims=True)
    total = final_grad + norm_back(mid_grad * gain_mid[...], normed, factor)
    resid_grad[...] = total
    attn_grad = low16(total)
    hg_own[...] = low16(dot(attn_grad, wo[0]))
    hg_send[...] = low16(dot(attn_grad, wo[1]))
    turn(0, total)


def middle_weights_kernel(side, xt, xt_recv, y_own, y_recv, send, kept, total):
    for j in range(3):
        for r in range(2):
            total[j, r] = dot(xt[j], y_own[j, r]) + dot(xt_recv[j], y_recv[j, r])
    core, x = side[0], side[2]
    for u in range(2):
        for z in range(4):
            for out, sent in ((send, 1), (kept, 0)):
                other_x = jnp.where(core == 0, u, sent)
                other_y = jnp.where(core == 0, sent, u)
                spot = 2 * z + jnp.where(other_x == 0, x, 1 - x)
                row = pl.multiple_of(spot * 80, 16)
                for j in range(3):
                    out[u, z, 80 * j : 80 * j + 80, :] = low16(total[j, other_y, pl.ds(row, 80), :])


def attention_back_kernel(
    side, q, k, v, lse, hg_own, hg_recv, cos, sin, seg_column, seg_row, out, bias, grad, dq, dk, dv
):
    group_rows, width = q.shape
    half_rows = group_rows // 2
    grad[pl.ds(pl.multiple_of(side[1] * half_rows, 16), half_rows), :] = hg_own[...]
    grad[pl.ds(pl.multiple_of((1 - side[1]) * half_rows, 16), half_rows), :] = hg_recv[...]
    fill_bias(bias, seg_column, seg_row)
    for part in (dq, dk, dv):
        part[...] = jnp.zeros_like(part)
    scale = HEAD_DIM ** (-0.5)
    for r in range(2):
        rows = slice(half_rows * r, half_rows * (r + 1))
        seen = slice(0, half_rows * (r + 1))
        for h in range(width // HEAD_DIM):
            window, keep = head_window(h)
            q_head = q[rows, window] * keep
            g_head = grad[rows, window] * keep
            scores = against(q_head, k[seen, window]) * scale + bias[rows, seen]
            probs = jnp.exp(scores - lse[rows, h : h + 1])
            prob_grad = against(g_head, v[seen, window])
            inner = jnp.sum(probs * prob_grad, axis=1, keepdims=True)
            score_grad = low16(probs * (prob_grad - inner))
            dq[rows, window] += dot(score_grad, k[seen, window] * keep)
            dk[seen, window] += across(score_grad, q_head)
            dv[seen, window] += across(low16(probs), g_head)
    for r in range(2):
        rows = slice(half_rows * r, half_rows * (r + 1))
        for j, part in enumerate((dq, dk)):
            value = part[rows, :] * scale
            out[rows, width * j : width * (j + 1)] = low16(
                value * cos[rows, :] - swap_halves(value) * sin[rows, :]
            )
        out[rows, 2 * width :] = low16(dv[rows, :])


def input_grad_kernel(side, d_qkv, w_full, normed, own, send, gain_grad):
    half_rows = own.shape[0]
    mine = pl.ds(pl.multiple_of(side[1] * half_rows, 16), half_rows)
    other = pl.ds(pl.multiple_of((1 - side[1]) * half_rows, 16), half_rows)
    part = against(d_qkv[other, :], w_full[...])
    send[...] = low16(part)
    gain = jnp.sum(part * normed[other, :], axis=0, keepdims=True)
    part = against(d_qkv[mine, :], w_full[...])
    own[...] = part
    gain_grad[...] = gain + jnp.sum(part * normed[mine, :], axis=0, keepdims=True)


def first_weights_kernel(side, at, at_recv, d_qkv, d_recv, *outs):
    far, near, kept, total = outs
    width = total.shape[1] // 3
    for j in range(3):
        columns = slice(width * j, width * (j + 1))
        total[:, columns] = dot(at[...], d_qkv[:, columns]) + dot(at_recv[...], d_recv[:, columns])
    x, z = side[2], side[3]
    for step in range(4):
        there = lax.rem(z + step, 4)
        row = pl.multiple_of((2 * there + 1 - x) * 80, 16)
        if step == 2:
            far[...] = low16(total[pl.ds(row, 80), :])
        else:
            near[step % 4 // 2 + step % 2] = low16(total[pl.ds(row, 80), :])
        row = pl.multiple_of((2 * there + x) * 80, 16)
        kept[step] = low16(total[pl.ds(row, 80), :])


ALL_AXES = ("z", "x", "c", "y")
Z_STEPS = (1, 3, 2)


def flip(value, axis):
    return lax.ppermute(value, axis, [(0, 1), (1, 0)])


def shift_z(value, step):
    return lax.ppermute(value, "z", [(i, (i + step) % 4) for i in range(4)])


def flip_split(value, first):
    pairs = []
    for z in range(4):
        for x in range(2):
            for c in range(2):
                for y in range(2):
                    there = (z, 1 - x, c, y) if c == first else (z, x, c, 1 - y)
                    here = ((z * 2 + x) * 2 + c) * 2 + y
                    pairs.append((here, ((there[0] * 2 + there[1]) * 2 + there[2]) * 2 + there[3]))
    return lax.ppermute(value, ALL_AXES, pairs)


def pick(array, index, axis=0):
    return lax.dynamic_index_in_dim(array, index, axis, keepdims=False)


def local_fast(
    tokens,
    w_query,
    w_key,
    w_value,
    w_output,
    w_in,
    w_out,
    gain_attn,
    gain_mlp,
    seq_lengths,
    seq_offsets,
    cotangent,
):
    z, x, c, y = (lax.axis_index(name) for name in ALL_AXES)
    own_rows, feature_count = tokens.shape
    head_width = w_query.shape[1]
    group_rows = 2 * own_rows
    side = jnp.stack([c, y, x, z]).astype(jnp.int32)

    gains = jnp.pad(
        jnp.stack([gain_attn, gain_mlp]), ((0, 14), (0, head_width - gain_attn.shape[0]))
    )
    q_block = jnp.concatenate([w_query, w_key, w_value, gains], axis=0)
    p_block = jnp.concatenate([w_output.T, w_in, w_out.T], axis=0)
    tokens_other = flip(tokens, "y")
    far = shift_z(q_block, 2)
    near = [shift_z(q_block, step) for step in (1, 3)]
    across_own = flip(q_block, "x")
    q_first = stack_blocks([q_block, *near, across_own], "stack_first")
    near = stack_blocks(near, "stack_near")
    across_near = flip(near, "x")
    across_far = flip(far, "x")[None]
    q_second = jnp.concatenate([far[None], across_near], axis=0)
    q_marks = [(0, 0), (1, 0), (3, 0), (0, 1), (2, 0), (1, 1), (3, 1), (2, 1)]
    q_parts = [q_first, q_second, across_far]
    q_all = q_parts + [flip(part, "c") for part in q_parts]
    q_place = jnp.stack(
        [
            ((z - step) % 4 * 2 + (x ^ xr)) * 2 + (c ^ cr)
            for cr in range(2)
            for step, xr in q_marks
        ]
    ).astype(jnp.int32)

    p_near = [shift_z(p_block, step) for step in (1, 3)]
    p_far = shift_z(p_block, 2)[None]
    places, halves = [], []
    for cr in range(2):
        core = c ^ cr
        for second, third in ((0, 0), (1, 0), (0, 1), (1, 1)):
            for step in (0, 1, 3, 2):
                xr = jnp.where(core == 0, second, third)
                places.append(((z - step) % 4 * 2 + (x ^ xr)) * 2 + core)
                halves.append(jnp.where(core == 0, third, second))
    p_place = jnp.stack(places).astype(jnp.int32)
    p_half = jnp.stack(halves).astype(jnp.int32)

    def own_part(array):
        return lax.dynamic_slice_in_dim(array, y * own_rows, own_rows, 0)

    tokens_full = jnp.where(
        y == 0,
        jnp.concatenate([tokens, tokens_other], 0),
        jnp.concatenate([tokens_other, tokens], 0),
    )
    member, segment, position, first_rows = row_layout(seq_lengths[0], seq_offsets[0], group_rows)
    firsts = dot(first_rows.T.astype(BF), tokens_full)
    mu_seq = jnp.mean(firsts, axis=1)
    sd_seq = jnp.sqrt(jnp.mean(jnp.square(firsts - mu_seq[:, None]), axis=1) + stat_eps)
    live = jnp.sum(member, axis=1)
    mu_row = jnp.dot(member, mu_seq, precision=highest)
    sd_row = jnp.dot(member, sd_seq, precision=highest) + (1.0 - live)
    centered = (wide(tokens_full) - mu_row[:, None]) / sd_row[:, None]
    normed_in, scale_in = rms_norm(centered)
    cosine, sine = rotary_tables(position)
    heads_here = head_width // HEAD_DIM
    cos_all = jnp.tile(jnp.concatenate([cosine, cosine], 1), (1, heads_here))
    sin_all = jnp.tile(jnp.concatenate([-sine, sine], 1), (1, heads_here))
    row_ids = jnp.arange(group_rows, dtype=jnp.int32)
    segment = jnp.where(segment >= 0, segment, -1 - row_ids)
    seg_column, seg_row = segment[:, None], segment[None, :]

    half = (own_rows, head_width)
    group = (group_rows, head_width)
    vector = ((1, feature_count), F32)
    w_full, at_mine, at_send, q_rot, k_rot, values, gain_mid, gain_in, *p_near = local_kernel(
        project_kernel,
        [
            ((feature_count, 3 * head_width), BF),
            ((feature_count // 2, group_rows), BF),
            ((feature_count // 2, group_rows), BF),
            (group, BF),
            (group, BF),
            (group, BF),
            vector,
            vector,
        ],
        2,
        [((32, 128), F32), ((group_rows, feature_count), BF), ((feature_count, group_rows), BF)],
        "project",
        12,
        gates=p_near,
    )(q_place, side, normed_in, cos_all, sin_all, q_place[:, None], *q_all)
    p_near = stack_blocks([p_block, *p_near], "stack_middle")
    lse, h_own, h_send, p_far = local_kernel(
        attention_kernel,
        [((group_rows, 128), F32), (half, BF), (half, BF)],
        1,
        [((group_rows, group_rows), F32), (group, F32)],
        "attention",
        12,
        gates=[p_far],
    )(side, q_rot, k_rot, values, seg_column, seg_row)
    p_parts = [p_near, p_far]
    p_parts += [flip_split(part, 0) for part in p_parts]
    p_parts += [flip_split(part, 1) for part in p_parts]
    p_all = p_parts + [flip(part, "c") for part in p_parts]
    at_recv = flip(at_send, "c")
    h_recv = flip(h_send, "y")

    mu_own, sd_own = own_part(mu_row)[:, None], own_part(sd_row)[:, None]
    centered_own = own_part(centered)
    own_full = (own_rows, feature_count)
    mixed, spread_sum, resid_grad, gain_mid_grad, hg_own, hg_send, xt_mine, xt_send, y_own = (
        local_kernel(
            middle_kernel,
            [
                (own_full, BF),
                ((own_rows, 1), F32),
                (own_full, F32),
                ((1, feature_count), F32),
                (half, BF),
                (half, BF),
                ((3, feature_count // 2, own_rows), BF),
                ((3, feature_count // 2, own_rows), BF),
                ((3, 2) + half, BF),
            ],
            3,
            [((2, feature_count, head_width), BF)] * 3
            + [((feature_count, own_rows), BF), (own_full, F32), (own_full, F32), ((2,) + half, F32)]
            + [((32, 240, head_width), BF), pltpu.SemaphoreType.DMA((16,))],
            "middle",
            36,
            loose=16,
        )(
            p_place, p_half, side, h_own, h_recv, centered_own, mu_own, sd_own, cotangent, gain_mid,
            *p_all,
        )
    )
    hg_recv = flip(hg_send, "y")
    xt_recv, y_recv = flip(xt_send, "c"), flip(y_own, "c")

    quarter = (2, 4, 3 * 80, head_width)
    p_send, p_kept = local_kernel(
        middle_weights_kernel,
        [(quarter, BF), (quarter, BF)],
        1,
        [((3, 2, feature_count // 2, head_width), F32)],
        "middle_weights",
        16,
    )(side, xt_mine, xt_recv, y_own, y_recv)
    p_recv = flip_split(p_send, 1)

    (d_qkv,) = local_kernel(
        attention_back_kernel,
        [((group_rows, 3 * head_width), BF)],
        1,
        [((group_rows, group_rows), F32), (group, BF), (group, F32), (group, F32), (group, F32)],
        "attention_back",
        14,
        after=[p_send],
    )(side, q_rot, k_rot, values, lse, hg_own, hg_recv, cos_all, sin_all, seg_column, seg_row)
    d_recv = flip(d_qkv, "c")
    in_own, in_send, gain_in_grad = local_kernel(
        input_grad_kernel,
        [(own_full, F32), (own_full, BF), ((1, feature_count), F32)],
        1,
        [],
        "input_grad",
        10,
    )(side, d_qkv, w_full, normed_in)
    in_recv = flip(in_send, "y")
    slab = (80, 3 * head_width)
    far, near, q_kept, p_kept, gain_in_grad, in_own = local_kernel(
        first_weights_kernel,
        [(slab, BF), ((3,) + slab, BF), ((4,) + slab, BF)],
        1,
        [((feature_count // 2, 3 * head_width), F32)],
        "first_weights",
        12,
        gates=[p_kept, gain_in_grad, in_own],
    )(side, at_mine, at_recv, d_qkv, d_recv)
    far = wide(q_kept[2]) + wide(flip(far, "x"))
    near = flip(near, "x")
    d_qkv_own = wide(q_kept[0]) + wide(near[0]) + wide(shift_z(low16(far), 2))
    for i, step in ((1, 1), (2, 3)):
        d_qkv_own = d_qkv_own + wide(shift_z(low16(wide(q_kept[step]) + wide(near[i])), step))

    gain_total = jnp.concatenate([gain_in_grad, gain_mid_grad], axis=0)
    gain_total = gain_total.reshape(2, 16, 80).transpose(1, 0, 2)
    gain_total = jnp.repeat(gain_total, 2, axis=0)
    gain_total = lax.all_to_all(gain_total, ALL_AXES, 0, 0, tiled=True)
    gain_grads = jnp.sum(gain_total, axis=0)

    p_sum = wide(p_kept) + wide(p_recv)
    p_sum = p_sum[0] + wide(flip_split(low16(p_sum[1]), 0))
    d_p = pick(p_sum, z)
    for step in (2, 1, 3):
        d_p = d_p + wide(shift_z(low16(pick(p_sum, (z + step) % 4)), step))

    in_grad = in_own + wide(in_recv)
    normed_own = own_part(normed_in)
    centered_grad = resid_grad + norm_back(in_grad * gain_in, normed_own, own_part(scale_in))
    scaled_grad = centered_grad / sd_own
    grad_out = wide(cotangent)
    per_row = jnp.stack(
        [
            jnp.sum(grad_out - scaled_grad, axis=1),
            spread_sum[:, 0] - jnp.sum(scaled_grad * centered_own, axis=1),
        ],
        axis=1,
    )
    seq_part = jnp.dot(own_part(member).T, per_row, precision=highest)
    seq_total = seq_part + flip(seq_part, "y")
    first_own = own_part(first_rows)
    mean_term = jnp.dot(first_own, seq_total[:, 0] / feature_count, precision=highest)
    spread_term = jnp.dot(first_own, seq_total[:, 1] / (feature_count * sd_seq), precision=highest)
    grad_tokens = (
        scaled_grad + mean_term[:, None] + spread_term[:, None] * (wide(tokens) - mu_own)
    )
    return (
        mixed,
        grad_tokens,
        d_qkv_own[:, :head_width],
        d_qkv_own[:, head_width : 2 * head_width],
        d_qkv_own[:, 2 * head_width :],
        d_p[:80].T,
        d_p[80:160],
        d_p[160:].T,
        gain_grads[0],
        gain_grads[1],
    )


def solution_fast(mesh):
    fine = Mesh(mesh.devices.reshape(4, 2, 2, 2), ALL_AXES)
    dp = ("z", "x", "c")
    rows, by_row, by_column = P(ALL_AXES, None), P(dp, "y"), P("y", dp)
    in_specs = (rows,) + (by_row,) * 3 + (by_column, by_row, by_column)
    in_specs += (P(dp), P(dp), P(dp, None), P(dp, None), rows)
    out_specs = (rows, rows) + (by_row,) * 3 + (by_column, by_row, by_column, P(dp), P(dp))
    return jax.shard_map(
        local_fast, mesh=fine, in_specs=in_specs, out_specs=out_specs, check_vma=False
    )


def solution(mesh):
    if dict(mesh.shape) == {"dp": 16, "tensor": 2}:
        return solution_fast(mesh)
    in_specs = (
        P(("dp", "tensor"), None),
        P("dp", "tensor"),
        P("dp", "tensor"),
        P("dp", "tensor"),
        P("tensor", "dp"),
        P("dp", "tensor"),
        P("tensor", "dp"),
        P("dp"),
        P("dp"),
        P("dp", None),
        P("dp", None),
        P(("dp", "tensor"), None),
    )
    out_specs = (
        P(("dp", "tensor"), None),
        P(("dp", "tensor"), None),
        P("dp", "tensor"),
        P("dp", "tensor"),
        P("dp", "tensor"),
        P("tensor", "dp"),
        P("dp", "tensor"),
        P("tensor", "dp"),
        P("dp"),
        P("dp"),
    )
    return jax.shard_map(local, mesh=mesh, in_specs=in_specs, out_specs=out_specs, check_vma=False)
```

```python
import jax
import jax.numpy as jnp
from jax import lax
from jax.experimental import pallas as pl
from jax.experimental.pallas import tpu as pltpu
from jax.sharding import Mesh
from jax.sharding import PartitionSpec as P

HEAD_DIM = 80


highest = lax.Precision.HIGHEST
epsilon = 1e-06
stat_eps = 1e-05
masked_score = -1e30
contract_last = (((1,), (1,)), ((), ()))
contract_first = (((0,), (0,)), ((), ()))


def against(left, right):
    return lax.dot_general(left, right, contract_last, preferred_element_type=jnp.float32)


def across(left, right):
    return lax.dot_general(left, right, contract_first, preferred_element_type=jnp.float32)


def row_layout(lengths, offsets, group_rows):
    row_ids = jnp.arange(group_rows, dtype=jnp.int32)
    inside = (row_ids[:, None] >= offsets[None, :]) & (
        row_ids[:, None] < offsets[None, :] + lengths[None, :]
    )
    member = inside.astype(jnp.float32)
    slot_ids = jnp.arange(offsets.shape[0], dtype=jnp.int32)
    segment = jnp.sum(jnp.where(inside, slot_ids[None, :] + 1, 0), axis=1) - 1
    seq_start = jnp.sum(jnp.where(inside, offsets[None, :], 0), axis=1)
    position = jnp.where(segment >= 0, row_ids - seq_start, 0).astype(jnp.float32)
    first_rows = (row_ids[:, None] == offsets[None, :]).astype(jnp.float32)
    return (member, segment, position, first_rows)


def rotary_tables(position):
    half_dim = HEAD_DIM // 2
    freqs = 10000.0 ** (-2.0 * jnp.arange(half_dim, dtype=jnp.float32) / HEAD_DIM)
    angles = position[:, None] * freqs[None, :]
    return (jnp.cos(angles), jnp.sin(angles))


def rotate(values, cosine, sine, direction):
    row_count = values.shape[0]
    shaped = values.reshape(row_count, -1, HEAD_DIM)
    half_dim = HEAD_DIM // 2
    first_half = shaped[..., :half_dim]
    second_half = shaped[..., half_dim:]
    cos_b = cosine[:, None, :]
    sin_b = sine[:, None, :] * direction
    turned = jnp.concatenate(
        [first_half * cos_b - second_half * sin_b, first_half * sin_b + second_half * cos_b],
        axis=-1,
    )
    return turned.reshape(row_count, -1)


def rms_norm(values):
    factor = lax.rsqrt(jnp.mean(values * values, axis=-1, keepdims=True) + epsilon)
    return (values * factor, factor)


def norm_back(grad_normed, normed, factor):
    return factor * (grad_normed - normed * jnp.mean(grad_normed * normed, axis=-1, keepdims=True))


def allowed_mask(seg_query, query_ids, segment, key_ids):
    same = (
        (seg_query[:, None] == segment[None, :])
        & (key_ids[None, :] <= query_ids[:, None])
        & (seg_query[:, None] >= 0)
    )
    return same | (query_ids[:, None] == key_ids[None, :])


def block_scores(query_all, key_all, segment, row_begin, block_rows):
    group_rows = key_all.shape[0]
    key_ids = jnp.arange(group_rows, dtype=jnp.int32)
    query_ids = row_begin + jnp.arange(block_rows, dtype=jnp.int32)
    queries = lax.dynamic_slice_in_dim(query_all, row_begin, block_rows, 0)
    scores = jnp.einsum(
        "qhd,khd->hqk", queries, key_all, preferred_element_type=jnp.float32
    ) * HEAD_DIM ** (-0.5)
    seg_query = lax.dynamic_slice_in_dim(segment, row_begin, block_rows, 0)
    mask = allowed_mask(seg_query, query_ids, segment, key_ids)
    return (jnp.where(mask[None], scores, masked_score), queries)


def attention_forward(q_rot, k_rot, values, segment):
    group_rows, head_width = q_rot.shape
    block_rows = min(512, group_rows)
    query_all = q_rot.reshape(group_rows, -1, HEAD_DIM)
    key_all = k_rot.reshape(group_rows, -1, HEAD_DIM)
    value_all = values.reshape(group_rows, -1, HEAD_DIM)

    def one_block(block_index):
        scores, queries = block_scores(
            query_all, key_all, segment, block_index * block_rows, block_rows
        )
        top = jnp.max(scores, axis=-1, keepdims=True)
        expo = jnp.exp(scores - top)
        total_exp = jnp.sum(expo, axis=-1, keepdims=True)
        probs = (expo / total_exp).astype(jnp.bfloat16)
        heads = jnp.einsum("hqk,khd->qhd", probs, value_all, preferred_element_type=jnp.float32)
        return (heads.reshape(block_rows, head_width), (top + jnp.log(total_exp))[..., 0])

    outs, log_sums = lax.map(one_block, jnp.arange(group_rows // block_rows, dtype=jnp.int32))
    return (outs.reshape(group_rows, head_width), log_sums)


def attention_backward(q_rot, k_rot, values, segment, log_sums, heads_grad):
    group_rows, head_width = q_rot.shape
    block_rows = min(512, group_rows)
    query_all = q_rot.reshape(group_rows, -1, HEAD_DIM)
    key_all = k_rot.reshape(group_rows, -1, HEAD_DIM)
    value_all = values.reshape(group_rows, -1, HEAD_DIM)
    grad_all = heads_grad.reshape(group_rows, -1, HEAD_DIM)
    scale_factor = HEAD_DIM ** (-0.5)

    def one_block(carry, block_index):
        key_grad, value_grad = carry
        row_begin = block_index * block_rows
        scores, queries = block_scores(query_all, key_all, segment, row_begin, block_rows)
        probs = jnp.exp(scores - log_sums[block_index][..., None])
        grads_block = lax.dynamic_slice_in_dim(grad_all, row_begin, block_rows, 0)
        prob_grad = jnp.einsum(
            "qhd,khd->hqk", grads_block, value_all, preferred_element_type=jnp.float32
        )
        inner = jnp.sum(probs * prob_grad, axis=-1, keepdims=True)
        score_grad = (probs * (prob_grad - inner)).astype(jnp.bfloat16)
        query_grad = (
            jnp.einsum("hqk,khd->qhd", score_grad, key_all, preferred_element_type=jnp.float32)
            * scale_factor
        )
        key_grad = (
            key_grad
            + jnp.einsum("hqk,qhd->khd", score_grad, queries, preferred_element_type=jnp.float32)
            * scale_factor
        )
        value_grad = value_grad + jnp.einsum(
            "hqk,qhd->khd",
            probs.astype(jnp.bfloat16),
            grads_block,
            preferred_element_type=jnp.float32,
        )
        return ((key_grad, value_grad), query_grad.reshape(block_rows, head_width))

    zeros = jnp.zeros(query_all.shape, jnp.float32)
    (key_grad, value_grad), query_grads = lax.scan(
        one_block, (zeros, zeros), jnp.arange(group_rows // block_rows, dtype=jnp.int32)
    )
    return (
        query_grads.reshape(group_rows, head_width),
        key_grad.reshape(group_rows, head_width),
        value_grad.reshape(group_rows, head_width),
    )


def split_weights(rows_full, columns_full, gains_full, head_width):
    qkv_width = 3 * head_width
    return (
        rows_full[:, :qkv_width],
        rows_full[:, qkv_width:],
        columns_full[:head_width],
        columns_full[head_width:],
        gains_full[0].astype(jnp.float32),
        gains_full[1].astype(jnp.float32),
    )


def local(
    tokens,
    w_query,
    w_key,
    w_value,
    w_output,
    w_in,
    w_out,
    gain_attn,
    gain_mlp,
    seq_lengths,
    seq_offsets,
    cotangent,
):
    own_rows = tokens.shape[0]
    feature_count = tokens.shape[1]
    head_width = w_query.shape[1]
    qkv_width = 3 * head_width
    row_blocks = jnp.concatenate([w_query, w_key, w_value, w_in], axis=1)
    column_blocks = jnp.concatenate([w_output, w_out], axis=0)
    gain_pair = jnp.stack([gain_attn, gain_mlp])
    rows_full, columns_full, gains_full = (
        lax.all_gather(row_blocks, "dp", axis=0, tiled=True),
        lax.all_gather(column_blocks, "dp", axis=1, tiled=True),
        lax.all_gather(gain_pair, "dp", axis=1, tiled=True),
    )
    w_qkv_full, w_in_full, w_output_full, w_out_full, gain_in, gain_mid = split_weights(
        rows_full, columns_full, gains_full, head_width
    )
    tokens_full = lax.all_gather(tokens, "tensor", axis=0, tiled=True)
    group_rows = tokens_full.shape[0]
    member, segment, position, first_rows = row_layout(seq_lengths[0], seq_offsets[0], group_rows)
    firsts = jnp.dot(
        first_rows.T.astype(jnp.bfloat16), tokens_full, preferred_element_type=jnp.float32
    )
    mu_seq = jnp.mean(firsts, axis=1)
    sd_seq = jnp.sqrt(jnp.mean(jnp.square(firsts - mu_seq[:, None]), axis=1) + stat_eps)
    live = jnp.sum(member, axis=1)
    mu_row = jnp.dot(member, mu_seq, precision=highest)
    sd_row = jnp.dot(member, sd_seq, precision=highest) + (1.0 - live)
    centered = (tokens_full.astype(jnp.float32) - mu_row[:, None]) / sd_row[:, None]
    normed_in, scale_in = rms_norm(centered)
    attn_in = (normed_in * gain_in).astype(jnp.bfloat16)
    projected = jnp.dot(attn_in, w_qkv_full, preferred_element_type=jnp.float32)
    cosine, sine = rotary_tables(position)
    q_rot = rotate(projected[:, :head_width], cosine, sine, 1.0).astype(jnp.bfloat16)
    k_rot = rotate(projected[:, head_width : 2 * head_width], cosine, sine, 1.0).astype(
        jnp.bfloat16
    )
    values = projected[:, 2 * head_width :].astype(jnp.bfloat16)
    heads_out, log_sums = attention_forward(q_rot, k_rot, values, segment)
    heads_low = heads_out.astype(jnp.bfloat16)
    attn_own = lax.psum_scatter(
        jnp.dot(heads_low, w_output_full, preferred_element_type=jnp.float32),
        "tensor",
        scatter_dimension=0,
        tiled=True,
    )
    own_start = lax.axis_index("tensor") * own_rows

    def own_part(array):
        return lax.dynamic_slice_in_dim(array, own_start, own_rows, 0)

    centered_own = own_part(centered)
    resid = centered_own + attn_own
    normed_mid, scale_mid = rms_norm(resid)
    mid_low = (normed_mid * gain_mid).astype(jnp.bfloat16)
    mid_full = lax.all_gather(mid_low, "tensor", axis=0, tiled=True)
    pre_act = jnp.dot(mid_full, w_in_full, preferred_element_type=jnp.float32)
    hidden = jax.nn.silu(pre_act).astype(jnp.bfloat16)
    mlp_own = lax.psum_scatter(
        jnp.dot(hidden, w_out_full, preferred_element_type=jnp.float32).astype(jnp.bfloat16),
        "tensor",
        scatter_dimension=0,
        tiled=True,
    ).astype(jnp.float32)
    final = resid + mlp_own
    mu_own = own_part(mu_row)
    sd_own = own_part(sd_row)
    mixed = (mu_own[:, None] + sd_own[:, None] * final).astype(jnp.bfloat16)
    rows_full, columns_full, gains_full = (
        lax.all_gather(row_blocks, "dp", axis=0, tiled=True),
        lax.all_gather(column_blocks, "dp", axis=1, tiled=True),
        lax.all_gather(gain_pair, "dp", axis=1, tiled=True),
    )
    w_qkv_full, w_in_full, w_output_full, w_out_full, gain_in, gain_mid = split_weights(
        rows_full, columns_full, gains_full, head_width
    )
    grad_out = cotangent.astype(jnp.float32)
    final_grad = grad_out * sd_own[:, None]
    mlp_grad_full = lax.all_gather(final_grad.astype(jnp.bfloat16), "tensor", axis=0, tiled=True)
    hidden_grad = against(mlp_grad_full, w_out_full)
    d_w_out = across(hidden, mlp_grad_full)
    sigmoid_act = jax.nn.sigmoid(pre_act)
    act_grad = (hidden_grad * sigmoid_act * (1.0 + pre_act * (1.0 - sigmoid_act))).astype(
        jnp.bfloat16
    )
    d_w_in = across(mid_full, act_grad)
    mid_grad = lax.psum_scatter(
        against(act_grad, w_in_full), "tensor", scatter_dimension=0, tiled=True
    )
    gain_mid_grad = jnp.sum(mid_grad * normed_mid, axis=0)
    resid_grad = final_grad + norm_back(mid_grad * gain_mid, normed_mid, scale_mid)
    attn_grad_full = lax.all_gather(resid_grad.astype(jnp.bfloat16), "tensor", axis=0, tiled=True)
    heads_grad = against(attn_grad_full, w_output_full).astype(jnp.bfloat16)
    d_w_output = across(heads_low, attn_grad_full)
    q_rot_grad, k_rot_grad, values_grad = attention_backward(
        q_rot, k_rot, values, segment, log_sums, heads_grad
    )
    proj_grad = jnp.concatenate(
        [
            rotate(q_rot_grad, cosine, sine, -1.0).astype(jnp.bfloat16),
            rotate(k_rot_grad, cosine, sine, -1.0).astype(jnp.bfloat16),
            values_grad.astype(jnp.bfloat16),
        ],
        axis=1,
    )
    d_w_qkv = across(attn_in, proj_grad)
    in_grad = lax.psum_scatter(
        against(proj_grad, w_qkv_full), "tensor", scatter_dimension=0, tiled=True
    )
    normed_own = own_part(normed_in)
    gain_in_grad = jnp.sum(in_grad * normed_own, axis=0)
    centered_grad = resid_grad + norm_back(in_grad * gain_in, normed_own, own_part(scale_in))
    scaled_grad = centered_grad / sd_own[:, None]
    per_row = jnp.stack(
        [
            jnp.sum(grad_out - scaled_grad, axis=1),
            jnp.sum(grad_out * final - scaled_grad * centered_own, axis=1),
        ],
        axis=1,
    )
    seq_part = jnp.dot(own_part(member).T, per_row, precision=highest)
    gain_part = jnp.stack([gain_in_grad, gain_mid_grad])
    gain_total, seq_total = lax.psum((gain_part, seq_part), "tensor")
    first_own = own_part(first_rows)
    mean_term = jnp.dot(first_own, seq_total[:, 0] / feature_count, precision=highest)
    spread_term = jnp.dot(first_own, seq_total[:, 1] / (feature_count * sd_seq), precision=highest)
    grad_tokens = (
        scaled_grad
        + mean_term[:, None]
        + spread_term[:, None] * (tokens.astype(jnp.float32) - mu_own[:, None])
    )
    grad_rows, grad_columns, gain_grads = (
        lax.psum_scatter(
            jnp.concatenate([d_w_qkv, d_w_in], axis=1), "dp", scatter_dimension=0, tiled=True
        ),
        lax.psum_scatter(
            jnp.concatenate([d_w_output, d_w_out], axis=0), "dp", scatter_dimension=1, tiled=True
        ),
        lax.psum_scatter(gain_total, "dp", scatter_dimension=1, tiled=True),
    )
    return (
        mixed,
        grad_tokens,
        grad_rows[:, :head_width],
        grad_rows[:, head_width : 2 * head_width],
        grad_rows[:, 2 * head_width : qkv_width],
        grad_columns[:head_width],
        grad_rows[:, qkv_width:],
        grad_columns[head_width:],
        gain_grads[0],
        gain_grads[1],
    )


HALF = HEAD_DIM // 2
VMEM_SPEC = pl.BlockSpec(memory_space=pltpu.VMEM)
SMEM_SPEC = pl.BlockSpec(memory_space=pltpu.SMEM)


def low16(value):
    return value.astype(jnp.bfloat16)


def wide(value):
    return value.astype(jnp.float32)


def dot(left, right):
    return jnp.dot(left, right, preferred_element_type=jnp.float32)


def local_kernel(body, outs, scalars, scratch, name, mib, gates=(), after=(), loose=0):
    def call(*operands):
        count = len(operands)
        left, held = len(gates) + len(after), len(gates)

        def trimmed(*refs):
            end = count + left + len(outs)
            body(*refs[:count], *refs[count + left : end], *refs[end + held :])

        any_spec = pl.BlockSpec(memory_space=pl.ANY)
        return pl.pallas_call(
            trimmed,
            out_shape=tuple(jax.ShapeDtypeStruct(shape, kind) for shape, kind in outs)
            + tuple(jax.ShapeDtypeStruct(gate.shape, gate.dtype) for gate in gates),
            in_specs=[SMEM_SPEC] * scalars
            + [VMEM_SPEC] * (count - scalars - loose)
            + [pl.BlockSpec(memory_space=pltpu.HBM)] * loose
            + [any_spec] * left,
            out_specs=(VMEM_SPEC,) * len(outs) + (any_spec,) * held,
            scratch_shapes=[
                pltpu.VMEM(*item) if isinstance(item, tuple) else item for item in scratch
            ],
            input_output_aliases={count + i: len(outs) + i for i in range(held)},
            compiler_params=pltpu.CompilerParams(vmem_limit_bytes=mib * 2**20),
            cost_estimate=pl.CostEstimate(flops=1000, bytes_accessed=1000, transcendentals=0),
            name=name,
        )(*operands, *gates, *after)

    return call


BF, F32 = jnp.bfloat16, jnp.float32


def head_window(head):
    begin = head * HEAD_DIM
    first = begin // 128 * 128
    last = -(-(begin + HEAD_DIM) // 128) * 128
    lane = lax.broadcasted_iota(jnp.int32, (1, last - first), 1) + first
    inside = (lane >= begin) & (lane < begin + HEAD_DIM)
    return slice(first, last), low16(jnp.where(inside, 1.0, 0.0))


def swap_halves(value):
    width = value.shape[1]
    lane = lax.broadcasted_iota(jnp.int32, value.shape, 1) % HEAD_DIM
    return jnp.where(
        lane < HALF, pltpu.roll(value, width - HALF, 1), pltpu.roll(value, HALF, 1)
    )


def fill_bias(bias, seg_column, seg_row):
    rows = bias.shape[0]
    query = lax.broadcasted_iota(jnp.int32, (rows, rows), 0)
    key = lax.broadcasted_iota(jnp.int32, (rows, rows), 1)
    allowed = (seg_column[...] == seg_row[...]) & (key <= query)
    bias[...] = jnp.where(allowed, 0.0, masked_score)


def stack_kernel(*refs):
    for i, block in enumerate(refs[:-1]):
        refs[-1][i] = block[...]


def stack_blocks(blocks, name):
    rows, width = blocks[0].shape
    outs = [((len(blocks), rows, width), BF)]
    return local_kernel(stack_kernel, outs, 0, [], name, 4)(*blocks)[0]


def hold(arrays, after):
    mark = ((8, 128), F32)

    def body(out):
        out[...] = jnp.zeros_like(out)

    return local_kernel(body, [mark], 0, [], "hold", 1, gates=arrays, after=after)()[1:]


def group_kernel(
    side, lengths, offsets, own, other, turns, normed, centered_own, mu_own, sd_own, factor_own, stats,
    cos, sin, seg_column, seg_row, full,
):
    half_rows = own.shape[0]
    lane = lax.broadcasted_iota(jnp.int32, (HEAD_DIM, cos.shape[1]), 1) % HEAD_DIM
    source = lax.broadcasted_iota(jnp.int32, (HEAD_DIM, cos.shape[1]), 0)
    high = low16(turns[...])
    low = low16(turns[...] - wide(high))
    same = lane % HALF == source % HALF
    for table, spread in (
        (cos, jnp.where(same & (source < HALF), 1.0, 0.0)),
        (sin, jnp.where(same & (source >= HALF), jnp.where(lane < HALF, -1.0, 1.0), 0.0)),
    ):
        table[...] = dot(high, low16(spread)) + dot(low, low16(spread))
    for table, axis in ((seg_column, 0), (seg_row, 1)):
        row = lax.broadcasted_iota(jnp.int32, table.shape, axis)
        series = -1 - row
        for s in range(offsets.shape[0]):
            inside = (row >= offsets[s]) & (row < offsets[s] + lengths[s])
            series = jnp.where(inside, s, series)
        table[...] = series
    mine = pl.multiple_of(side[1] * half_rows, 16)
    full[pl.ds(mine, half_rows), :] = own[...]
    full[pl.ds(pl.multiple_of((1 - side[1]) * half_rows, 16), half_rows), :] = other[...]
    slots = offsets.shape[0]
    slot = lax.broadcasted_iota(jnp.int32, (8, 2 * half_rows), 0)
    column = lax.broadcasted_iota(jnp.int32, (8, 2 * half_rows), 1)
    chosen = jnp.zeros((8, 2 * half_rows), F32)
    for s in range(slots):
        chosen = jnp.where((slot == s) & (column == offsets[s]), 1.0, chosen)
    firsts = dot(low16(chosen), full[...])
    mu = jnp.mean(firsts, axis=1, keepdims=True)
    sd = jnp.sqrt(jnp.mean(jnp.square(firsts - mu), axis=1, keepdims=True) + stat_eps)
    lane = lax.broadcasted_iota(jnp.int32, (8, 128), 1)
    stats[...] = jnp.where(lane == 0, mu, sd)
    for r in range(2):
        row = lax.broadcasted_iota(jnp.int32, (half_rows, 1), 0) + r * half_rows
        mu_row = jnp.zeros((half_rows, 1), F32)
        sd_row = jnp.ones((half_rows, 1), F32)
        for s in range(slots):
            inside = (row >= offsets[s]) & (row < offsets[s] + lengths[s])
            mu_row = jnp.where(inside, mu[s : s + 1, :], mu_row)
            sd_row = jnp.where(inside, sd[s : s + 1, :], sd_row)
        rows = slice(half_rows * r, half_rows * (r + 1))
        centered = (wide(full[rows, :]) - mu_row) / sd_row
        value, factor = rms_norm(centered)
        normed[rows, :] = value

        @pl.when(side[1] == r)
        def _():
            centered_own[...] = centered
            mu_own[...] = mu_row
            sd_own[...] = sd_row
            factor_own[...] = factor


def first_sum_kernel(kept, recv, q_kept, q_recv, send, rest, far):
    rest[...] = low16(wide(kept[0]) + wide(recv[0]))
    send[...] = low16(wide(kept[1]) + wide(recv[1]))
    far[...] = low16(wide(q_kept[2]) + wide(q_recv[...]))


def second_sum_kernel(side, kept, recv, *outs):
    for step, out in enumerate(outs):
        there = lax.rem(side[3] + step, 4)
        out[...] = (wide(kept[there]) + wide(recv[there])).astype(out.dtype)


def third_sum_kernel(kept, recv, send):
    send[...] = low16(kept[...] + wide(recv[...]))


def near_sum_kernel(side, kept, recv, passing, gain_parts, own, send_one, send_three, gain_grads):
    own[...] = wide(kept[0]) + wide(recv[0])
    send_one[...] = low16(wide(kept[1]) + wide(recv[1]) + wide(passing[...]))
    send_three[...] = low16(wide(kept[3]) + wide(recv[2]))
    place = (side[3] * 2 + side[2]) * 2 + side[0]
    shift = place * 80 - jnp.minimum(place * 80 // 128 * 128, 1024)
    gain_sum = jnp.concatenate([jnp.sum(gain_parts[...], axis=0), jnp.zeros((6, 256), F32)], 0)
    gain_grads[...] = pltpu.roll(gain_sum, lax.rem(256 - shift, 256), 1)[0:2, 0:80]


def first_total_kernel(own, one, three, *outs):
    for j, out in enumerate(outs):
        part = slice(640 * j, 640 * (j + 1))
        out[...] = own[:, part] + wide(one[:, part]) + wide(three[:, part])


def middle_total_kernel(own, one, three, *outs):
    for j, out in enumerate(outs):
        part = slice(80 * j, 80 * (j + 1))
        total = own[part, :] + wide(one[part, :]) + wide(three[part, :])
        out[...] = total


def token_sums_kernel(
    side, lengths, offsets, in_own, in_recv, gain, resid_grad, normed, factor, sd, cot, centered,
    spread_sum, scaled, sums,
):
    half_rows = in_own.shape[0]
    mine = pl.ds(pl.multiple_of(side[1] * half_rows, 16), half_rows)
    in_grad = in_own[...] + wide(in_recv[...])
    back = norm_back(in_grad * gain[...], normed[mine, :], factor[...])
    value = (resid_grad[...] + back) / sd[...]
    scaled[...] = value
    first = jnp.sum(wide(cot[...]) - value, axis=1, keepdims=True)
    second = spread_sum[...] - jnp.sum(value * centered[...], axis=1, keepdims=True)
    row = lax.broadcasted_iota(jnp.int32, (half_rows, 1), 0) + side[1] * half_rows
    slot = lax.broadcasted_iota(jnp.int32, (8, 128), 0)
    lane = lax.broadcasted_iota(jnp.int32, (8, 128), 1)
    table = jnp.zeros((8, 128), F32)
    for s in range(offsets.shape[0]):
        inside = (row >= offsets[s]) & (row < offsets[s] + lengths[s])
        for j, column in enumerate((first, second)):
            total = jnp.sum(jnp.where(inside, column, 0.0), axis=0, keepdims=True)
            table = jnp.where((slot == s) & (lane == j), total, table)
    sums[...] = table


def token_grad_kernel(side, offsets, scaled, sums, recv, stats, tokens, mu, out):
    half_rows, feature_count = scaled.shape
    total = sums[...] + recv[...]
    row = lax.broadcasted_iota(jnp.int32, (half_rows, 1), 0) + side[1] * half_rows
    mean_term = jnp.zeros((half_rows, 1), F32)
    spread_term = jnp.zeros((half_rows, 1), F32)
    for s in range(offsets.shape[0]):
        here = row == offsets[s]
        mean_term = jnp.where(here, total[s : s + 1, 0:1] / feature_count, mean_term)
        spread = total[s : s + 1, 1:2] / (feature_count * stats[s : s + 1, 1:2])
        spread_term = jnp.where(here, spread, spread_term)
    out[...] = scaled[...] + mean_term + spread_term * (wide(tokens[...]) - mu[...])


def project_kernel(place, side, normed, cos, sin, spot, *refs):
    arrays, outs = refs[:8], refs[8:]
    w_full, at_mine, at_send, q_out, k_out, v_out, gain_mid, gain_first = outs[:8]
    tail, attn_in, turned = outs[8:]
    group_rows, feature_count = normed.shape
    half_rows = group_rows // 2
    width = q_out.shape[1]
    blocks = [(array, index) for array in arrays for index in range(array.shape[0])]
    for i, (array, index) in enumerate(blocks):
        row = pl.multiple_of(place[i] * 80, 16)
        for j in range(3):
            w_full[pl.ds(row, 80), pl.ds(width * j, width)] = array[index, pl.ds(80 * j, 80), :]
        ends = wide(array[index, pl.ds(240, 16), :128])
        tail[i : i + 1, :] = ends[0:1]
        tail[16 + i : 17 + i, :] = ends[1:2]
    lane = lax.broadcasted_iota(jnp.int32, (128, feature_count), 1)
    source = lax.broadcasted_iota(jnp.int32, (128, feature_count), 0)
    spread = low16(jnp.where(lane % 80 == source, 1.0, 0.0))
    held = lax.broadcasted_iota(jnp.int32, (16, feature_count), 1) // 80 == spot[...]
    gain_in = jnp.sum(jnp.where(held, dot(low16(tail[0:16]), spread), 0.0), 0, keepdims=True)
    gain_first[...] = gain_in
    gain_mid[...] = jnp.sum(jnp.where(held, dot(low16(tail[16:32]), spread), 0.0), 0, keepdims=True)
    for i in range(feature_count // 128):
        part = normed[:, 128 * i : 128 * i + 128] * gain_in[:, 128 * i : 128 * i + 128]
        attn_in[:, 128 * i : 128 * i + 128] = low16(part)
        turned[128 * i : 128 * i + 128, :] = low16(part.T)
    for i in range(8):
        mine = pl.multiple_of((2 * i + side[0]) * 80, 16)
        other = pl.multiple_of((2 * i + 1 - side[0]) * 80, 16)
        at_mine[80 * i : 80 * i + 80, :] = turned[pl.ds(mine, 80), :]
        at_send[80 * i : 80 * i + 80, :] = turned[pl.ds(other, 80), :]
    for r in range(2):
        rows = slice(half_rows * r, half_rows * (r + 1))
        for j, out in enumerate((q_out, k_out)):
            part = dot(attn_in[rows, :], w_full[:, width * j : width * (j + 1)])
            out[rows, :] = low16(part * cos[rows, :] + swap_halves(part) * sin[rows, :])
        v_out[rows, :] = low16(dot(attn_in[rows, :], w_full[:, 2 * width :]))


def attention_kernel(side, q, k, v, seg_column, seg_row, lse_out, h_own, h_send, bias, heads):
    group_rows, width = q.shape
    half_rows = group_rows // 2
    fill_bias(bias, seg_column, seg_row)
    heads[...] = jnp.zeros_like(heads)
    for r in range(2):
        rows = slice(half_rows * r, half_rows * (r + 1))
        seen = slice(0, half_rows * (r + 1))
        head_lane = lax.broadcasted_iota(jnp.int32, (half_rows, 128), 1)
        lse = jnp.zeros((half_rows, 128), F32)
        for h in range(width // HEAD_DIM):
            window, keep = head_window(h)
            scores = against(q[rows, window] * keep, k[seen, window])
            scores = scores * HEAD_DIM ** (-0.5) + bias[rows, seen]
            top = jnp.max(scores, axis=1, keepdims=True)
            expo = jnp.exp(scores - top)
            total = jnp.sum(expo, axis=1, keepdims=True)
            probs = low16(expo * (1.0 / total))
            heads[rows, window] += dot(probs, v[seen, window] * keep)
            lse = jnp.where(head_lane == h, top + jnp.log(total), lse)
        lse_out[rows, :] = lse
    own = pl.multiple_of(side[1] * half_rows, 16)
    other = pl.multiple_of((1 - side[1]) * half_rows, 16)
    h_own[...] = low16(heads[pl.ds(own, half_rows), :])
    h_send[...] = low16(heads[pl.ds(other, half_rows), :])


def middle_kernel(place, half, side, h_own, h_recv, centered, mu, sd, cot, gain_mid, *refs):
    arrays, outs = refs[:8], refs[8:]
    mixed, spread_sum, resid_grad, gain_grad, hg_own, hg_send, xt_mine, xt_send, y_out = outs[:9]
    wo, wi, wt, turned, keep, final, pre = outs[9:]
    own_rows, feature_count = centered.shape
    blocks = [(array, index) for array in arrays for index in range(array.shape[0])]
    for i, (array, index) in enumerate(blocks):
        row = pl.multiple_of(place[i] * 80, 16)
        for j, full in enumerate((wo, wi, wt)):
            full[half[i], pl.ds(row, 80), :] = array[index, 80 * j : 80 * j + 80, :]

    def turn(j, value):
        for i in range(feature_count // 128):
            turned[128 * i : 128 * i + 128, :] = low16(value[:, 128 * i : 128 * i + 128].T)
        for i in range(8):
            mine = pl.multiple_of((2 * i + side[0]) * 80, 16)
            other = pl.multiple_of((2 * i + 1 - side[0]) * 80, 16)
            xt_mine[j, 80 * i : 80 * i + 80, :] = turned[pl.ds(mine, 80), :]
            xt_send[j, 80 * i : 80 * i + 80, :] = turned[pl.ds(other, 80), :]

    y_out[0, 0] = h_own[...]
    y_out[0, 1] = h_recv[...]
    resid = centered[...] + against(h_own[...], wo[0]) + against(h_recv[...], wo[1])
    normed, factor = rms_norm(resid)
    keep[...] = normed
    mid = normed * gain_mid[...]
    turn(1, mid)
    mid = low16(mid)
    final_grad = wide(cot[...]) * sd[...]
    mlp_grad = low16(final_grad)
    turn(2, final_grad)
    final[...] = resid
    for r in range(2):
        pre_act = dot(mid, wi[r])
        pre[r] = pre_act
        y_out[2, r] = low16(pre_act * (1.0 / (1.0 + jnp.exp(-pre_act))))
    final[...] += against(y_out[2, 0], wt[0]) + against(y_out[2, 1], wt[1])
    mixed[...] = low16(mu[...] + sd[...] * final[...])
    spread_sum[...] = jnp.sum(wide(cot[...]) * final[...], axis=1, keepdims=True)
    for r in range(2):
        hidden_grad = dot(mlp_grad, wt[r])
        pre_act = pre[r]
        sigmoid = 1.0 / (1.0 + jnp.exp(-pre_act))
        y_out[1, r] = low16(hidden_grad * sigmoid * (1.0 + pre_act * (1.0 - sigmoid)))
    mid_grad = against(y_out[1, 0], wi[0]) + against(y_out[1, 1], wi[1])
    normed = keep[...]
    gain_grad[...] = jnp.sum(mid_grad * normed, axis=0, keepdims=True)
    total = final_grad + norm_back(mid_grad * gain_mid[...], normed, factor)
    resid_grad[...] = total
    attn_grad = low16(total)
    hg_own[...] = low16(dot(attn_grad, wo[0]))
    hg_send[...] = low16(dot(attn_grad, wo[1]))
    turn(0, total)


def middle_weights_kernel(side, xt, xt_recv, y_own, y_recv, send, kept, total):
    for j in range(3):
        for r in range(2):
            total[j, r] = dot(xt[j], y_own[j, r]) + dot(xt_recv[j], y_recv[j, r])
    core, x = side[0], side[2]
    for u in range(2):
        for z in range(4):
            for out, sent in ((send, 1), (kept, 0)):
                other_x = jnp.where(core == 0, u, sent)
                other_y = jnp.where(core == 0, sent, u)
                spot = 2 * z + jnp.where(other_x == 0, x, 1 - x)
                row = pl.multiple_of(spot * 80, 16)
                for j in range(3):
                    out[u, z, 80 * j : 80 * j + 80, :] = low16(total[j, other_y, pl.ds(row, 80), :])


def attention_back_kernel(
    side, q, k, v, lse, hg_own, hg_recv, cos, sin, seg_column, seg_row, out, bias, grad, dq, dk, dv
):
    group_rows, width = q.shape
    half_rows = group_rows // 2
    grad[pl.ds(pl.multiple_of(side[1] * half_rows, 16), half_rows), :] = hg_own[...]
    grad[pl.ds(pl.multiple_of((1 - side[1]) * half_rows, 16), half_rows), :] = hg_recv[...]
    fill_bias(bias, seg_column, seg_row)
    for part in (dq, dk, dv):
        part[...] = jnp.zeros_like(part)
    scale = HEAD_DIM ** (-0.5)
    for r in range(2):
        rows = slice(half_rows * r, half_rows * (r + 1))
        seen = slice(0, half_rows * (r + 1))
        for h in range(width // HEAD_DIM):
            window, keep = head_window(h)
            q_head = q[rows, window] * keep
            g_head = grad[rows, window] * keep
            scores = against(q_head, k[seen, window]) * scale + bias[rows, seen]
            probs = jnp.exp(scores - lse[rows, h : h + 1])
            prob_grad = against(g_head, v[seen, window])
            inner = jnp.sum(probs * prob_grad, axis=1, keepdims=True)
            score_grad = low16(probs * (prob_grad - inner))
            dq[rows, window] += dot(score_grad, k[seen, window] * keep)
            dk[seen, window] += across(score_grad, q_head)
            dv[seen, window] += across(low16(probs), g_head)
    for r in range(2):
        rows = slice(half_rows * r, half_rows * (r + 1))
        for j, part in enumerate((dq, dk)):
            value = part[rows, :] * scale
            out[rows, width * j : width * (j + 1)] = low16(
                value * cos[rows, :] - swap_halves(value) * sin[rows, :]
            )
        out[rows, 2 * width :] = low16(dv[rows, :])


def gain_window(place):
    return min(place * 80 // 128 * 128, 1024)


def input_grad_kernel(side, d_qkv, w_full, normed, gain_mid_grad, own, send, gain_parts):
    half_rows = own.shape[0]
    mine = pl.ds(pl.multiple_of(side[1] * half_rows, 16), half_rows)
    other = pl.ds(pl.multiple_of((1 - side[1]) * half_rows, 16), half_rows)
    part = against(d_qkv[other, :], w_full[...])
    send[...] = low16(part)
    gain = jnp.sum(part * normed[other, :], axis=0, keepdims=True)
    part = against(d_qkv[mine, :], w_full[...])
    own[...] = part
    gain = gain + jnp.sum(part * normed[mine, :], axis=0, keepdims=True)
    for place in range(16):
        first = gain_window(place)
        for y in range(2):
            gain_parts[2 * place + y, 0:1] = gain[:, first : first + 256]
            gain_parts[2 * place + y, 1:2] = gain_mid_grad[:, first : first + 256]


def first_weights_kernel(side, at, at_recv, d_qkv, d_recv, *outs):
    far, near, kept, total = outs
    width = total.shape[1] // 3
    for j in range(3):
        columns = slice(width * j, width * (j + 1))
        total[:, columns] = dot(at[...], d_qkv[:, columns]) + dot(at_recv[...], d_recv[:, columns])
    x, z = side[2], side[3]
    for step in range(4):
        there = lax.rem(z + step, 4)
        row = pl.multiple_of((2 * there + 1 - x) * 80, 16)
        if step == 2:
            far[...] = low16(total[pl.ds(row, 80), :])
        else:
            near[step % 4 // 2 + step % 2] = low16(total[pl.ds(row, 80), :])
        row = pl.multiple_of((2 * there + x) * 80, 16)
        kept[step] = low16(total[pl.ds(row, 80), :])


ALL_AXES = ("z", "x", "c", "y")
Z_STEPS = (1, 3, 2)


def flip(value, axis):
    return lax.ppermute(value, axis, [(0, 1), (1, 0)])


def shift_z(value, step):
    return lax.ppermute(value, "z", [(i, (i + step) % 4) for i in range(4)])


def flip_split(value, first):
    pairs = []
    for z in range(4):
        for x in range(2):
            for c in range(2):
                for y in range(2):
                    there = (z, 1 - x, c, y) if c == first else (z, x, c, 1 - y)
                    here = ((z * 2 + x) * 2 + c) * 2 + y
                    pairs.append((here, ((there[0] * 2 + there[1]) * 2 + there[2]) * 2 + there[3]))
    return lax.ppermute(value, ALL_AXES, pairs)


def pick(array, index, axis=0):
    return lax.dynamic_index_in_dim(array, index, axis, keepdims=False)


def local_fast(
    tokens,
    w_query,
    w_key,
    w_value,
    w_output,
    w_in,
    w_out,
    gain_attn,
    gain_mlp,
    seq_lengths,
    seq_offsets,
    cotangent,
):
    z, x, c, y = (lax.axis_index(name) for name in ALL_AXES)
    own_rows, feature_count = tokens.shape
    head_width = w_query.shape[1]
    group_rows = 2 * own_rows
    side = jnp.stack([c, y, x, z]).astype(jnp.int32)

    gains = jnp.pad(
        jnp.stack([gain_attn, gain_mlp]), ((0, 14), (0, head_width - gain_attn.shape[0]))
    )
    q_block = jnp.concatenate([w_query, w_key, w_value, gains], axis=0)
    p_block = jnp.concatenate([w_output.T, w_in, w_out.T], axis=0)
    tokens_other = flip(tokens, "y")
    near = [shift_z(q_block, step) for step in (1, 3)]
    far = shift_z(near[0], 1)
    across_own = flip(q_block, "x")
    q_first = stack_blocks([q_block, *near, across_own], "stack_first")
    near = stack_blocks(near, "stack_near")
    lengths, offsets = seq_lengths[0], seq_offsets[0]
    half = (own_rows, head_width)
    group = (group_rows, head_width)
    own_full = (own_rows, feature_count)
    column = ((own_rows, 1), F32)
    position = row_layout(lengths, offsets, group_rows)[2]
    turns = jnp.concatenate(rotary_tables(position), axis=1)
    normed_in, centered_own, mu_own, sd_own, factor_own, stats, *tables = local_kernel(
        group_kernel,
        [
            ((group_rows, feature_count), F32),
            (own_full, F32),
            column,
            column,
            column,
            ((8, 128), F32),
            (group, F32),
            (group, F32),
            ((group_rows, 1), jnp.int32),
            ((1, group_rows), jnp.int32),
        ],
        3,
        [((group_rows, feature_count), BF)],
        "group",
        10,
    )(side, lengths, offsets, tokens, tokens_other, turns)
    cos_all, sin_all, seg_column, seg_row = tables

    (far,) = hold([far], [normed_in])
    q_marks = [(0, 0), (1, 0), (3, 0), (0, 1), (2, 0), (2, 1), (1, 1), (3, 1)]
    q_parts = [q_first, far[None], flip(far, "x")[None], flip(near, "x")]
    q_all = q_parts + [flip(part, "c") for part in q_parts]
    q_place = jnp.stack(
        [
            ((z - step) % 4 * 2 + (x ^ xr)) * 2 + (c ^ cr)
            for cr in range(2)
            for step, xr in q_marks
        ]
    ).astype(jnp.int32)

    (p_block,) = hold([p_block], [far])
    p_near = [shift_z(p_block, step) for step in (1, 3)]
    places, halves = [], []
    for cr in range(2):
        core = c ^ cr
        for second, third in ((0, 0), (1, 0), (0, 1), (1, 1)):
            for step in (0, 1, 3, 2):
                xr = jnp.where(core == 0, second, third)
                places.append(((z - step) % 4 * 2 + (x ^ xr)) * 2 + core)
                halves.append(jnp.where(core == 0, third, second))
    p_place = jnp.stack(places).astype(jnp.int32)
    p_half = jnp.stack(halves).astype(jnp.int32)

    vector = ((1, feature_count), F32)
    w_full, at_mine, at_send, q_rot, k_rot, values, gain_mid, gain_in = local_kernel(
        project_kernel,
        [
            ((feature_count, 3 * head_width), BF),
            ((feature_count // 2, group_rows), BF),
            ((feature_count // 2, group_rows), BF),
            (group, BF),
            (group, BF),
            (group, BF),
            vector,
            vector,
        ],
        2,
        [((32, 128), F32), ((group_rows, feature_count), BF), ((feature_count, group_rows), BF)],
        "project",
        10,
    )(q_place, side, normed_in, cos_all, sin_all, q_place[:, None], *q_all)
    (p_near[0],) = hold([p_near[0]], [q_rot])
    p_far = shift_z(p_near[0], 1)
    lse, h_own, h_send = local_kernel(
        attention_kernel,
        [((group_rows, 128), F32), (half, BF), (half, BF)],
        1,
        [((group_rows, group_rows), F32), (group, F32)],
        "attention",
        8,
    )(side, q_rot, k_rot, values, seg_column, seg_row)
    (p_block,) = hold([p_block], [lse])
    p_first = stack_blocks([p_block, *p_near, p_far], "stack_middle")
    p_second = flip_split(p_first, 0)
    p_third = flip_split(p_first, 1)
    h_recv = flip(h_send, "y")
    (p_second,) = hold([p_second], [h_recv])
    p_parts = [p_first, p_second, p_third, flip_split(p_second, 1)]
    p_all = p_parts + [flip(part, "c") for part in p_parts]
    at_recv = flip(at_send, "c")

    mixed, spread_sum, resid_grad, gain_mid_grad, hg_own, hg_send, xt_mine, xt_send, y_own = (
        local_kernel(
            middle_kernel,
            [
                (own_full, BF),
                ((own_rows, 1), F32),
                (own_full, F32),
                ((1, feature_count), F32),
                (half, BF),
                (half, BF),
                ((3, feature_count // 2, own_rows), BF),
                ((3, feature_count // 2, own_rows), BF),
                ((3, 2) + half, BF),
            ],
            3,
            [((2, feature_count, head_width), BF)] * 3
            + [((feature_count, own_rows), BF), (own_full, F32), (own_full, F32), ((2,) + half, F32)],
            "middle",
            31,
        )(
            p_place, p_half, side, h_own, h_recv, centered_own, mu_own, sd_own, cotangent, gain_mid,
            *p_all,
        )
    )
    hg_recv = flip(hg_send, "y")
    xt_recv, y_recv = flip(xt_send, "c"), flip(y_own, "c")

    quarter = (2, 4, 3 * 80, head_width)
    p_send, p_kept = local_kernel(
        middle_weights_kernel,
        [(quarter, BF), (quarter, BF)],
        1,
        [((3, 2, feature_count // 2, head_width), F32)],
        "middle_weights",
        14,
    )(side, xt_mine, xt_recv, y_own, y_recv)
    (p_send,) = hold([p_send], [hg_recv])
    p_recv = flip_split(p_send, 1)

    (d_qkv,) = local_kernel(
        attention_back_kernel,
        [((group_rows, 3 * head_width), BF)],
        1,
        [((group_rows, group_rows), F32), (group, BF), (group, F32), (group, F32), (group, F32)],
        "attention_back",
        11,
        after=[p_send],
    )(side, q_rot, k_rot, values, lse, hg_own, hg_recv, cos_all, sin_all, seg_column, seg_row)
    d_recv = flip(d_qkv, "c")
    in_own, in_send, gain_parts = local_kernel(
        input_grad_kernel,
        [(own_full, F32), (own_full, BF), ((32, 2, 256), F32)],
        1,
        [],
        "input_grad",
        10,
    )(side, d_qkv, w_full, normed_in, gain_mid_grad)
    slab = (80, 3 * head_width)
    far, near, q_kept, p_kept, gain_parts, in_own = local_kernel(
        first_weights_kernel,
        [(slab, BF), ((3,) + slab, BF), ((4,) + slab, BF)],
        1,
        [((feature_count // 2, 3 * head_width), F32)],
        "first_weights",
        12,
        gates=[p_kept, gain_parts, in_own],
    )(side, at_mine, at_recv, d_qkv, d_recv)
    far = flip(far, "x")

    p_send, p_kept, far = local_kernel(
        first_sum_kernel, [(quarter[1:], BF)] * 2 + [(slab, BF)], 0, [], "first_sum", 4
    )(p_kept, p_recv, q_kept, far)
    p_recv = flip_split(p_send, 0)
    q_two = shift_z(far, 1)
    gain_parts = lax.all_to_all(gain_parts, ALL_AXES, 0, 0, tiled=True)
    near, in_send = hold([near, in_send], [p_recv, q_two, gain_parts])
    near, in_recv = flip(near, "x"), flip(in_send, "y")
    piece = quarter[2:]
    p_own, p_one, p_two, p_three = local_kernel(
        second_sum_kernel,
        [(piece, F32), (piece, F32)] + [(piece, BF)] * 2,
        1,
        [],
        "second_sum",
        4,
    )(side, p_kept, p_recv)
    p_three = shift_z(p_three, 3)
    (p_one,) = local_kernel(third_sum_kernel, [(piece, BF)], 0, [], "third_sum", 2)(
        p_one, shift_z(p_two, 1)
    )
    q_own, near_one, near_three, gain_grads = local_kernel(
        near_sum_kernel,
        [(slab, F32), (slab, BF), (slab, BF), ((2, 80), F32)],
        1,
        [],
        "near_sum",
        4,
        after=[p_one],
    )(side, q_kept, near, q_two, gain_parts)
    q_one, q_three = shift_z(near_one, 1), shift_z(near_three, 3)
    p_one = shift_z(p_one, 1)
    scaled, sums = local_kernel(
        token_sums_kernel,
        [(own_full, F32), ((8, 128), F32)],
        3,
        [],
        "token_sums",
        8,
        after=[near_one],
    )(
        side, lengths, offsets, in_own, in_recv, gain_in, resid_grad, normed_in, factor_own, sd_own,
        cotangent, centered_own, spread_sum,
    )
    sums_recv = flip(sums, "y")
    (grad_tokens,) = local_kernel(
        token_grad_kernel, [(own_full, F32)], 2, [], "token_grad", 6
    )(side, offsets, scaled, sums, sums_recv, stats, tokens, mu_own)

    shard = ((80, head_width), F32)
    grad_query, grad_key, grad_value = local_kernel(
        first_total_kernel, [shard] * 3, 0, [], "first_total", 4
    )(q_own, q_one, q_three)
    grad_output, grad_in, grad_out = local_kernel(
        middle_total_kernel, [shard] * 3, 0, [], "middle_total", 4
    )(p_own, p_one, p_three)
    return (
        mixed,
        grad_tokens,
        grad_query,
        grad_key,
        grad_value,
        grad_output.T,
        grad_in,
        grad_out.T,
        gain_grads[0],
        gain_grads[1],
    )


def solution_fast(mesh):
    fine = Mesh(mesh.devices.reshape(4, 2, 2, 2), ALL_AXES)
    dp = ("z", "x", "c")
    rows, by_row, by_column = P(ALL_AXES, None), P(dp, "y"), P("y", dp)
    in_specs = (rows,) + (by_row,) * 3 + (by_column, by_row, by_column)
    in_specs += (P(dp), P(dp), P(dp, None), P(dp, None), rows)
    out_specs = (rows, rows) + (by_row,) * 3 + (by_column, by_row, by_column, P(dp), P(dp))
    return jax.shard_map(
        local_fast, mesh=fine, in_specs=in_specs, out_specs=out_specs, check_vma=False
    )


def solution(mesh):
    if dict(mesh.shape) == {"dp": 16, "tensor": 2}:
        return solution_fast(mesh)
    in_specs = (
        P(("dp", "tensor"), None),
        P("dp", "tensor"),
        P("dp", "tensor"),
        P("dp", "tensor"),
        P("tensor", "dp"),
        P("dp", "tensor"),
        P("tensor", "dp"),
        P("dp"),
        P("dp"),
        P("dp", None),
        P("dp", None),
        P(("dp", "tensor"), None),
    )
    out_specs = (
        P(("dp", "tensor"), None),
        P(("dp", "tensor"), None),
        P("dp", "tensor"),
        P("dp", "tensor"),
        P("dp", "tensor"),
        P("tensor", "dp"),
        P("dp", "tensor"),
        P("tensor", "dp"),
        P("dp"),
        P("dp"),
    )
    return jax.shard_map(local, mesh=mesh, in_specs=in_specs, out_specs=out_specs, check_vma=False)
```

```python
import jax
import jax.numpy as jnp
from jax import lax
from jax.experimental import pallas as pl
from jax.experimental.pallas import tpu as pltpu
from jax.sharding import Mesh
from jax.sharding import PartitionSpec as P

HEAD_DIM = 80


highest = lax.Precision.HIGHEST
epsilon = 1e-06
stat_eps = 1e-05
masked_score = -1e30
contract_last = (((1,), (1,)), ((), ()))
contract_first = (((0,), (0,)), ((), ()))


def against(left, right):
    return lax.dot_general(left, right, contract_last, preferred_element_type=jnp.float32)


def across(left, right):
    return lax.dot_general(left, right, contract_first, preferred_element_type=jnp.float32)


def row_layout(lengths, offsets, group_rows):
    row_ids = jnp.arange(group_rows, dtype=jnp.int32)
    inside = (row_ids[:, None] >= offsets[None, :]) & (
        row_ids[:, None] < offsets[None, :] + lengths[None, :]
    )
    member = inside.astype(jnp.float32)
    slot_ids = jnp.arange(offsets.shape[0], dtype=jnp.int32)
    segment = jnp.sum(jnp.where(inside, slot_ids[None, :] + 1, 0), axis=1) - 1
    seq_start = jnp.sum(jnp.where(inside, offsets[None, :], 0), axis=1)
    position = jnp.where(segment >= 0, row_ids - seq_start, 0).astype(jnp.float32)
    first_rows = (row_ids[:, None] == offsets[None, :]).astype(jnp.float32)
    return (member, segment, position, first_rows)


def rotary_tables(position):
    half_dim = HEAD_DIM // 2
    freqs = 10000.0 ** (-2.0 * jnp.arange(half_dim, dtype=jnp.float32) / HEAD_DIM)
    angles = position[:, None] * freqs[None, :]
    return (jnp.cos(angles), jnp.sin(angles))


def rotate(values, cosine, sine, direction):
    row_count = values.shape[0]
    shaped = values.reshape(row_count, -1, HEAD_DIM)
    half_dim = HEAD_DIM // 2
    first_half = shaped[..., :half_dim]
    second_half = shaped[..., half_dim:]
    cos_b = cosine[:, None, :]
    sin_b = sine[:, None, :] * direction
    turned = jnp.concatenate(
        [first_half * cos_b - second_half * sin_b, first_half * sin_b + second_half * cos_b],
        axis=-1,
    )
    return turned.reshape(row_count, -1)


def rms_norm(values):
    factor = lax.rsqrt(jnp.mean(values * values, axis=-1, keepdims=True) + epsilon)
    return (values * factor, factor)


def norm_back(grad_normed, normed, factor):
    return factor * (grad_normed - normed * jnp.mean(grad_normed * normed, axis=-1, keepdims=True))


def allowed_mask(seg_query, query_ids, segment, key_ids):
    same = (
        (seg_query[:, None] == segment[None, :])
        & (key_ids[None, :] <= query_ids[:, None])
        & (seg_query[:, None] >= 0)
    )
    return same | (query_ids[:, None] == key_ids[None, :])


def block_scores(query_all, key_all, segment, row_begin, block_rows):
    group_rows = key_all.shape[0]
    key_ids = jnp.arange(group_rows, dtype=jnp.int32)
    query_ids = row_begin + jnp.arange(block_rows, dtype=jnp.int32)
    queries = lax.dynamic_slice_in_dim(query_all, row_begin, block_rows, 0)
    scores = jnp.einsum(
        "qhd,khd->hqk", queries, key_all, preferred_element_type=jnp.float32
    ) * HEAD_DIM ** (-0.5)
    seg_query = lax.dynamic_slice_in_dim(segment, row_begin, block_rows, 0)
    mask = allowed_mask(seg_query, query_ids, segment, key_ids)
    return (jnp.where(mask[None], scores, masked_score), queries)


def attention_forward(q_rot, k_rot, values, segment):
    group_rows, head_width = q_rot.shape
    block_rows = min(512, group_rows)
    query_all = q_rot.reshape(group_rows, -1, HEAD_DIM)
    key_all = k_rot.reshape(group_rows, -1, HEAD_DIM)
    value_all = values.reshape(group_rows, -1, HEAD_DIM)

    def one_block(block_index):
        scores, queries = block_scores(
            query_all, key_all, segment, block_index * block_rows, block_rows
        )
        top = jnp.max(scores, axis=-1, keepdims=True)
        expo = jnp.exp(scores - top)
        total_exp = jnp.sum(expo, axis=-1, keepdims=True)
        probs = (expo / total_exp).astype(jnp.bfloat16)
        heads = jnp.einsum("hqk,khd->qhd", probs, value_all, preferred_element_type=jnp.float32)
        return (heads.reshape(block_rows, head_width), (top + jnp.log(total_exp))[..., 0])

    outs, log_sums = lax.map(one_block, jnp.arange(group_rows // block_rows, dtype=jnp.int32))
    return (outs.reshape(group_rows, head_width), log_sums)


def attention_backward(q_rot, k_rot, values, segment, log_sums, heads_grad):
    group_rows, head_width = q_rot.shape
    block_rows = min(512, group_rows)
    query_all = q_rot.reshape(group_rows, -1, HEAD_DIM)
    key_all = k_rot.reshape(group_rows, -1, HEAD_DIM)
    value_all = values.reshape(group_rows, -1, HEAD_DIM)
    grad_all = heads_grad.reshape(group_rows, -1, HEAD_DIM)
    scale_factor = HEAD_DIM ** (-0.5)

    def one_block(carry, block_index):
        key_grad, value_grad = carry
        row_begin = block_index * block_rows
        scores, queries = block_scores(query_all, key_all, segment, row_begin, block_rows)
        probs = jnp.exp(scores - log_sums[block_index][..., None])
        grads_block = lax.dynamic_slice_in_dim(grad_all, row_begin, block_rows, 0)
        prob_grad = jnp.einsum(
            "qhd,khd->hqk", grads_block, value_all, preferred_element_type=jnp.float32
        )
        inner = jnp.sum(probs * prob_grad, axis=-1, keepdims=True)
        score_grad = (probs * (prob_grad - inner)).astype(jnp.bfloat16)
        query_grad = (
            jnp.einsum("hqk,khd->qhd", score_grad, key_all, preferred_element_type=jnp.float32)
            * scale_factor
        )
        key_grad = (
            key_grad
            + jnp.einsum("hqk,qhd->khd", score_grad, queries, preferred_element_type=jnp.float32)
            * scale_factor
        )
        value_grad = value_grad + jnp.einsum(
            "hqk,qhd->khd",
            probs.astype(jnp.bfloat16),
            grads_block,
            preferred_element_type=jnp.float32,
        )
        return ((key_grad, value_grad), query_grad.reshape(block_rows, head_width))

    zeros = jnp.zeros(query_all.shape, jnp.float32)
    (key_grad, value_grad), query_grads = lax.scan(
        one_block, (zeros, zeros), jnp.arange(group_rows // block_rows, dtype=jnp.int32)
    )
    return (
        query_grads.reshape(group_rows, head_width),
        key_grad.reshape(group_rows, head_width),
        value_grad.reshape(group_rows, head_width),
    )


def split_weights(rows_full, columns_full, gains_full, head_width):
    qkv_width = 3 * head_width
    return (
        rows_full[:, :qkv_width],
        rows_full[:, qkv_width:],
        columns_full[:head_width],
        columns_full[head_width:],
        gains_full[0].astype(jnp.float32),
        gains_full[1].astype(jnp.float32),
    )


def local(
    tokens,
    w_query,
    w_key,
    w_value,
    w_output,
    w_in,
    w_out,
    gain_attn,
    gain_mlp,
    seq_lengths,
    seq_offsets,
    cotangent,
):
    own_rows = tokens.shape[0]
    feature_count = tokens.shape[1]
    head_width = w_query.shape[1]
    qkv_width = 3 * head_width
    row_blocks = jnp.concatenate([w_query, w_key, w_value, w_in], axis=1)
    column_blocks = jnp.concatenate([w_output, w_out], axis=0)
    gain_pair = jnp.stack([gain_attn, gain_mlp])
    rows_full, columns_full, gains_full = (
        lax.all_gather(row_blocks, "dp", axis=0, tiled=True),
        lax.all_gather(column_blocks, "dp", axis=1, tiled=True),
        lax.all_gather(gain_pair, "dp", axis=1, tiled=True),
    )
    w_qkv_full, w_in_full, w_output_full, w_out_full, gain_in, gain_mid = split_weights(
        rows_full, columns_full, gains_full, head_width
    )
    tokens_full = lax.all_gather(tokens, "tensor", axis=0, tiled=True)
    group_rows = tokens_full.shape[0]
    member, segment, position, first_rows = row_layout(seq_lengths[0], seq_offsets[0], group_rows)
    firsts = jnp.dot(
        first_rows.T.astype(jnp.bfloat16), tokens_full, preferred_element_type=jnp.float32
    )
    mu_seq = jnp.mean(firsts, axis=1)
    sd_seq = jnp.sqrt(jnp.mean(jnp.square(firsts - mu_seq[:, None]), axis=1) + stat_eps)
    live = jnp.sum(member, axis=1)
    mu_row = jnp.dot(member, mu_seq, precision=highest)
    sd_row = jnp.dot(member, sd_seq, precision=highest) + (1.0 - live)
    centered = (tokens_full.astype(jnp.float32) - mu_row[:, None]) / sd_row[:, None]
    normed_in, scale_in = rms_norm(centered)
    attn_in = (normed_in * gain_in).astype(jnp.bfloat16)
    projected = jnp.dot(attn_in, w_qkv_full, preferred_element_type=jnp.float32)
    cosine, sine = rotary_tables(position)
    q_rot = rotate(projected[:, :head_width], cosine, sine, 1.0).astype(jnp.bfloat16)
    k_rot = rotate(projected[:, head_width : 2 * head_width], cosine, sine, 1.0).astype(
        jnp.bfloat16
    )
    values = projected[:, 2 * head_width :].astype(jnp.bfloat16)
    heads_out, log_sums = attention_forward(q_rot, k_rot, values, segment)
    heads_low = heads_out.astype(jnp.bfloat16)
    attn_own = lax.psum_scatter(
        jnp.dot(heads_low, w_output_full, preferred_element_type=jnp.float32),
        "tensor",
        scatter_dimension=0,
        tiled=True,
    )
    own_start = lax.axis_index("tensor") * own_rows

    def own_part(array):
        return lax.dynamic_slice_in_dim(array, own_start, own_rows, 0)

    centered_own = own_part(centered)
    resid = centered_own + attn_own
    normed_mid, scale_mid = rms_norm(resid)
    mid_low = (normed_mid * gain_mid).astype(jnp.bfloat16)
    mid_full = lax.all_gather(mid_low, "tensor", axis=0, tiled=True)
    pre_act = jnp.dot(mid_full, w_in_full, preferred_element_type=jnp.float32)
    hidden = jax.nn.silu(pre_act).astype(jnp.bfloat16)
    mlp_own = lax.psum_scatter(
        jnp.dot(hidden, w_out_full, preferred_element_type=jnp.float32).astype(jnp.bfloat16),
        "tensor",
        scatter_dimension=0,
        tiled=True,
    ).astype(jnp.float32)
    final = resid + mlp_own
    mu_own = own_part(mu_row)
    sd_own = own_part(sd_row)
    mixed = (mu_own[:, None] + sd_own[:, None] * final).astype(jnp.bfloat16)
    rows_full, columns_full, gains_full = (
        lax.all_gather(row_blocks, "dp", axis=0, tiled=True),
        lax.all_gather(column_blocks, "dp", axis=1, tiled=True),
        lax.all_gather(gain_pair, "dp", axis=1, tiled=True),
    )
    w_qkv_full, w_in_full, w_output_full, w_out_full, gain_in, gain_mid = split_weights(
        rows_full, columns_full, gains_full, head_width
    )
    grad_out = cotangent.astype(jnp.float32)
    final_grad = grad_out * sd_own[:, None]
    mlp_grad_full = lax.all_gather(final_grad.astype(jnp.bfloat16), "tensor", axis=0, tiled=True)
    hidden_grad = against(mlp_grad_full, w_out_full)
    d_w_out = across(hidden, mlp_grad_full)
    sigmoid_act = jax.nn.sigmoid(pre_act)
    act_grad = (hidden_grad * sigmoid_act * (1.0 + pre_act * (1.0 - sigmoid_act))).astype(
        jnp.bfloat16
    )
    d_w_in = across(mid_full, act_grad)
    mid_grad = lax.psum_scatter(
        against(act_grad, w_in_full), "tensor", scatter_dimension=0, tiled=True
    )
    gain_mid_grad = jnp.sum(mid_grad * normed_mid, axis=0)
    resid_grad = final_grad + norm_back(mid_grad * gain_mid, normed_mid, scale_mid)
    attn_grad_full = lax.all_gather(resid_grad.astype(jnp.bfloat16), "tensor", axis=0, tiled=True)
    heads_grad = against(attn_grad_full, w_output_full).astype(jnp.bfloat16)
    d_w_output = across(heads_low, attn_grad_full)
    q_rot_grad, k_rot_grad, values_grad = attention_backward(
        q_rot, k_rot, values, segment, log_sums, heads_grad
    )
    proj_grad = jnp.concatenate(
        [
            rotate(q_rot_grad, cosine, sine, -1.0).astype(jnp.bfloat16),
            rotate(k_rot_grad, cosine, sine, -1.0).astype(jnp.bfloat16),
            values_grad.astype(jnp.bfloat16),
        ],
        axis=1,
    )
    d_w_qkv = across(attn_in, proj_grad)
    in_grad = lax.psum_scatter(
        against(proj_grad, w_qkv_full), "tensor", scatter_dimension=0, tiled=True
    )
    normed_own = own_part(normed_in)
    gain_in_grad = jnp.sum(in_grad * normed_own, axis=0)
    centered_grad = resid_grad + norm_back(in_grad * gain_in, normed_own, own_part(scale_in))
    scaled_grad = centered_grad / sd_own[:, None]
    per_row = jnp.stack(
        [
            jnp.sum(grad_out - scaled_grad, axis=1),
            jnp.sum(grad_out * final - scaled_grad * centered_own, axis=1),
        ],
        axis=1,
    )
    seq_part = jnp.dot(own_part(member).T, per_row, precision=highest)
    gain_part = jnp.stack([gain_in_grad, gain_mid_grad])
    gain_total, seq_total = lax.psum((gain_part, seq_part), "tensor")
    first_own = own_part(first_rows)
    mean_term = jnp.dot(first_own, seq_total[:, 0] / feature_count, precision=highest)
    spread_term = jnp.dot(first_own, seq_total[:, 1] / (feature_count * sd_seq), precision=highest)
    grad_tokens = (
        scaled_grad
        + mean_term[:, None]
        + spread_term[:, None] * (tokens.astype(jnp.float32) - mu_own[:, None])
    )
    grad_rows, grad_columns, gain_grads = (
        lax.psum_scatter(
            jnp.concatenate([d_w_qkv, d_w_in], axis=1), "dp", scatter_dimension=0, tiled=True
        ),
        lax.psum_scatter(
            jnp.concatenate([d_w_output, d_w_out], axis=0), "dp", scatter_dimension=1, tiled=True
        ),
        lax.psum_scatter(gain_total, "dp", scatter_dimension=1, tiled=True),
    )
    return (
        mixed,
        grad_tokens,
        grad_rows[:, :head_width],
        grad_rows[:, head_width : 2 * head_width],
        grad_rows[:, 2 * head_width : qkv_width],
        grad_columns[:head_width],
        grad_rows[:, qkv_width:],
        grad_columns[head_width:],
        gain_grads[0],
        gain_grads[1],
    )


HALF = HEAD_DIM // 2
VMEM_SPEC = pl.BlockSpec(memory_space=pltpu.VMEM)
SMEM_SPEC = pl.BlockSpec(memory_space=pltpu.SMEM)


def low16(value):
    return value.astype(jnp.bfloat16)


def wide(value):
    return value.astype(jnp.float32)


def dot(left, right):
    return jnp.dot(left, right, preferred_element_type=jnp.float32)


def local_kernel(body, outs, scalars, scratch, name, mib, gates=(), after=(), loose=0):
    def call(*operands):
        count = len(operands)
        left, held = len(gates) + len(after), len(gates)

        def trimmed(*refs):
            end = count + left + len(outs)
            body(*refs[:count], *refs[count + left : end], *refs[end + held :])

        any_spec = pl.BlockSpec(memory_space=pl.ANY)
        return pl.pallas_call(
            trimmed,
            out_shape=tuple(jax.ShapeDtypeStruct(shape, kind) for shape, kind in outs)
            + tuple(jax.ShapeDtypeStruct(gate.shape, gate.dtype) for gate in gates),
            in_specs=[SMEM_SPEC] * scalars
            + [VMEM_SPEC] * (count - scalars - loose)
            + [pl.BlockSpec(memory_space=pltpu.HBM)] * loose
            + [any_spec] * left,
            out_specs=(VMEM_SPEC,) * len(outs) + (any_spec,) * held,
            scratch_shapes=[
                pltpu.VMEM(*item) if isinstance(item, tuple) else item for item in scratch
            ],
            input_output_aliases={count + i: len(outs) + i for i in range(held)},
            compiler_params=pltpu.CompilerParams(vmem_limit_bytes=mib * 2**20),
            cost_estimate=pl.CostEstimate(flops=1000, bytes_accessed=1000, transcendentals=0),
            name=name,
        )(*operands, *gates, *after)

    return call


BF, F32 = jnp.bfloat16, jnp.float32


def head_window(head):
    begin = head * HEAD_DIM
    first = begin // 128 * 128
    last = -(-(begin + HEAD_DIM) // 128) * 128
    lane = lax.broadcasted_iota(jnp.int32, (1, last - first), 1) + first
    inside = (lane >= begin) & (lane < begin + HEAD_DIM)
    return slice(first, last), low16(jnp.where(inside, 1.0, 0.0))


def swap_halves(value):
    width = value.shape[1]
    lane = lax.broadcasted_iota(jnp.int32, value.shape, 1) % HEAD_DIM
    return jnp.where(
        lane < HALF, pltpu.roll(value, width - HALF, 1), pltpu.roll(value, HALF, 1)
    )


def fill_bias(bias, seg_column, seg_row):
    rows = bias.shape[0]
    query = lax.broadcasted_iota(jnp.int32, (rows, rows), 0)
    key = lax.broadcasted_iota(jnp.int32, (rows, rows), 1)
    allowed = (seg_column[...] == seg_row[...]) & (key <= query)
    bias[...] = jnp.where(allowed, 0.0, masked_score)


def stack_kernel(*refs):
    for i, block in enumerate(refs[:-1]):
        refs[-1][i] = block[...]


def stack_blocks(blocks, name):
    rows, width = blocks[0].shape
    outs = [((len(blocks), rows, width), BF)]
    return local_kernel(stack_kernel, outs, 0, [], name, 4)(*blocks)[0]


def hold(arrays, after):
    mark = ((8, 128), F32)

    def body(out):
        out[...] = jnp.zeros_like(out)

    return local_kernel(body, [mark], 0, [], "hold", 1, gates=arrays, after=after)()[1:]


def group_kernel(
    side, lengths, offsets, own, other, turns, normed, rows_own, stats, tables,
    seg_column, seg_row, full,
):
    half_rows = own.shape[0]
    width = tables.shape[1] // 2
    lane = lax.broadcasted_iota(jnp.int32, (HEAD_DIM, width), 1) % HEAD_DIM
    source = lax.broadcasted_iota(jnp.int32, (HEAD_DIM, width), 0)
    high = low16(turns[...])
    low = low16(turns[...] - wide(high))
    same = lane % HALF == source % HALF
    for first, spread in (
        (0, jnp.where(same & (source < HALF), 1.0, 0.0)),
        (width, jnp.where(same & (source >= HALF), jnp.where(lane < HALF, -1.0, 1.0), 0.0)),
    ):
        tables[:, first : first + width] = dot(high, low16(spread)) + dot(low, low16(spread))
    for table, axis in ((seg_column, 0), (seg_row, 1)):
        row = lax.broadcasted_iota(jnp.int32, table.shape, axis)
        series = -1 - row
        for s in range(offsets.shape[0]):
            inside = (row >= offsets[s]) & (row < offsets[s] + lengths[s])
            series = jnp.where(inside, s, series)
        table[...] = series
    mine = pl.multiple_of(side[1] * half_rows, 16)
    full[pl.ds(mine, half_rows), :] = own[...]
    full[pl.ds(pl.multiple_of((1 - side[1]) * half_rows, 16), half_rows), :] = other[...]
    slots = offsets.shape[0]
    slot = lax.broadcasted_iota(jnp.int32, (8, 2 * half_rows), 0)
    column = lax.broadcasted_iota(jnp.int32, (8, 2 * half_rows), 1)
    chosen = jnp.zeros((8, 2 * half_rows), F32)
    for s in range(slots):
        chosen = jnp.where((slot == s) & (column == offsets[s]), 1.0, chosen)
    firsts = dot(low16(chosen), full[...])
    mu = jnp.mean(firsts, axis=1, keepdims=True)
    sd = jnp.sqrt(jnp.mean(jnp.square(firsts - mu), axis=1, keepdims=True) + stat_eps)
    lane = lax.broadcasted_iota(jnp.int32, (8, 128), 1)
    stats[...] = jnp.where(lane == 0, mu, sd)
    features = own.shape[1]
    extra = lax.broadcasted_iota(jnp.int32, (half_rows, 128), 1)
    for r in range(2):
        row = lax.broadcasted_iota(jnp.int32, (half_rows, 1), 0) + r * half_rows
        mu_row = jnp.zeros((half_rows, 1), F32)
        sd_row = jnp.ones((half_rows, 1), F32)
        for s in range(slots):
            inside = (row >= offsets[s]) & (row < offsets[s] + lengths[s])
            mu_row = jnp.where(inside, mu[s : s + 1, :], mu_row)
            sd_row = jnp.where(inside, sd[s : s + 1, :], sd_row)
        rows = slice(half_rows * r, half_rows * (r + 1))
        centered = (wide(full[rows, :]) - mu_row) / sd_row
        value, factor = rms_norm(centered)
        normed[rows, :] = value

        @pl.when(side[1] == r)
        def _():
            rows_own[:, :features] = centered
            rows_own[:, features:] = jnp.where(
                extra == 0, mu_row, jnp.where(extra == 1, sd_row, factor)
            )


def first_sum_kernel(kept, recv, q_kept, q_recv, send, rest, far):
    rest[...] = low16(wide(kept[0]) + wide(recv[0]))
    send[...] = low16(wide(kept[1]) + wide(recv[1]))
    far[...] = low16(wide(q_kept[2]) + wide(q_recv[...]))


def second_sum_kernel(side, kept, recv, *outs):
    for step, out in enumerate(outs):
        there = lax.rem(side[3] + step, 4)
        out[...] = (wide(kept[there]) + wide(recv[there])).astype(out.dtype)


def third_sum_kernel(kept, recv, send):
    send[...] = low16(kept[...] + wide(recv[...]))


def near_sum_kernel(side, kept, recv, passing, gain_parts, own, send_one, send_three, gain_grads):
    own[...] = wide(kept[0]) + wide(recv[0])
    send_one[...] = low16(wide(kept[1]) + wide(recv[1]) + wide(passing[...]))
    send_three[...] = low16(wide(kept[3]) + wide(recv[2]))
    place = (side[3] * 2 + side[2]) * 2 + side[0]
    shift = place * 80 - jnp.minimum(place * 80 // 128 * 128, 1024)
    gain_sum = jnp.concatenate([jnp.sum(gain_parts[...], axis=0), jnp.zeros((6, 256), F32)], 0)
    gain_grads[...] = pltpu.roll(gain_sum, lax.rem(256 - shift, 256), 1)[0:2, 0:80]


def first_total_kernel(own, one, three, *outs):
    for j, out in enumerate(outs):
        part = slice(640 * j, 640 * (j + 1))
        out[...] = own[:, part] + wide(one[:, part]) + wide(three[:, part])


def middle_total_kernel(own, one, three, *outs):
    for j, out in enumerate(outs):
        part = slice(80 * j, 80 * (j + 1))
        total = own[part, :] + wide(one[part, :]) + wide(three[part, :])
        out[...] = total


def token_sums_kernel(
    side, lengths, offsets, in_own, in_recv, gains, resid_grad, normed, own, cot, scaled, sums
):
    half_rows, features = in_own.shape
    sd, factor = own[:, features + 1 : features + 2], own[:, features + 2 : features + 3]
    mine = pl.ds(pl.multiple_of(side[1] * half_rows, 16), half_rows)
    in_grad = in_own[...] + wide(in_recv[...])
    back = norm_back(in_grad * gains[0:1, :], normed[mine, :], factor)
    value = (resid_grad[:, :features] + back) / sd
    scaled[...] = value
    first = jnp.sum(wide(cot[...]) - value, axis=1, keepdims=True)
    second = resid_grad[:, features : features + 1] - jnp.sum(value * own[:, :features], axis=1, keepdims=True)
    row = lax.broadcasted_iota(jnp.int32, (half_rows, 1), 0) + side[1] * half_rows
    slot = lax.broadcasted_iota(jnp.int32, (8, 128), 0)
    lane = lax.broadcasted_iota(jnp.int32, (8, 128), 1)
    table = jnp.zeros((8, 128), F32)
    for s in range(offsets.shape[0]):
        inside = (row >= offsets[s]) & (row < offsets[s] + lengths[s])
        for j, column in enumerate((first, second)):
            total = jnp.sum(jnp.where(inside, column, 0.0), axis=0, keepdims=True)
            table = jnp.where((slot == s) & (lane == j), total, table)
    sums[...] = table


def token_grad_kernel(side, offsets, scaled, sums, recv, stats, tokens, own, out):
    half_rows, feature_count = scaled.shape
    total = sums[...] + recv[...]
    row = lax.broadcasted_iota(jnp.int32, (half_rows, 1), 0) + side[1] * half_rows
    mean_term = jnp.zeros((half_rows, 1), F32)
    spread_term = jnp.zeros((half_rows, 1), F32)
    for s in range(offsets.shape[0]):
        here = row == offsets[s]
        mean_term = jnp.where(here, total[s : s + 1, 0:1] / feature_count, mean_term)
        spread = total[s : s + 1, 1:2] / (feature_count * stats[s : s + 1, 1:2])
        spread_term = jnp.where(here, spread, spread_term)
    out[...] = scaled[...] + mean_term + spread_term * (wide(tokens[...]) - own[:, feature_count : feature_count + 1])


def project_kernel(side, normed, tables, spot, *refs):
    arrays, outs = refs[:8], refs[8:]
    w_full, at_mine, at_send, q_out, k_out, v_out, gains = outs[:7]
    tail, attn_in, turned = outs[7:]
    group_rows, feature_count = normed.shape
    half_rows = group_rows // 2
    width = q_out.shape[1]
    blocks = [(array, index) for array in arrays for index in range(array.shape[0])]
    for i, (array, index) in enumerate(blocks):
        row = pl.multiple_of(side[68 + i] * 80, 16)
        for j in range(3):
            w_full[pl.ds(row, 80), pl.ds(width * j, width)] = array[index, pl.ds(80 * j, 80), :]
        ends = wide(array[index, pl.ds(240, 16), :128])
        tail[i : i + 1, :] = ends[0:1]
        tail[16 + i : 17 + i, :] = ends[1:2]
    lane = lax.broadcasted_iota(jnp.int32, (128, feature_count), 1)
    source = lax.broadcasted_iota(jnp.int32, (128, feature_count), 0)
    spread = low16(jnp.where(lane % 80 == source, 1.0, 0.0))
    held = lax.broadcasted_iota(jnp.int32, (16, feature_count), 1) // 80 == spot[...]
    gain_in = jnp.sum(jnp.where(held, dot(low16(tail[0:16]), spread), 0.0), 0, keepdims=True)
    gains[0:1, :] = gain_in
    gains[1:2, :] = jnp.sum(jnp.where(held, dot(low16(tail[16:32]), spread), 0.0), 0, keepdims=True)
    for i in range(feature_count // 128):
        part = normed[:, 128 * i : 128 * i + 128] * gain_in[:, 128 * i : 128 * i + 128]
        attn_in[:, 128 * i : 128 * i + 128] = low16(part)
        turned[128 * i : 128 * i + 128, :] = low16(part.T)
    for i in range(8):
        mine = pl.multiple_of((2 * i + side[0]) * 80, 16)
        other = pl.multiple_of((2 * i + 1 - side[0]) * 80, 16)
        at_mine[80 * i : 80 * i + 80, :] = turned[pl.ds(mine, 80), :]
        at_send[80 * i : 80 * i + 80, :] = turned[pl.ds(other, 80), :]
    for r in range(2):
        rows = slice(half_rows * r, half_rows * (r + 1))
        for j, out in enumerate((q_out, k_out)):
            part = dot(attn_in[rows, :], w_full[:, width * j : width * (j + 1)])
            part = part * tables[rows, :width] + swap_halves(part) * tables[rows, width:]
            out[rows, :] = low16(part)
        v_out[rows, :] = low16(dot(attn_in[rows, :], w_full[:, 2 * width :]))


def attention_kernel(side, q, k, v, seg_column, seg_row, lse_out, h_own, h_send, bias, heads):
    group_rows, width = q.shape
    half_rows = group_rows // 2
    fill_bias(bias, seg_column, seg_row)
    heads[...] = jnp.zeros_like(heads)
    for r in range(2):
        rows = slice(half_rows * r, half_rows * (r + 1))
        seen = slice(0, half_rows * (r + 1))
        head_lane = lax.broadcasted_iota(jnp.int32, (half_rows, 128), 1)
        lse = jnp.zeros((half_rows, 128), F32)
        for h in range(width // HEAD_DIM):
            window, keep = head_window(h)
            scores = against(q[rows, window] * keep, k[seen, window])
            scores = scores * HEAD_DIM ** (-0.5) + bias[rows, seen]
            top = jnp.max(scores, axis=1, keepdims=True)
            expo = jnp.exp(scores - top)
            total = jnp.sum(expo, axis=1, keepdims=True)
            probs = low16(expo * (1.0 / total))
            heads[rows, window] += dot(probs, v[seen, window] * keep)
            lse = jnp.where(head_lane == h, top + jnp.log(total), lse)
        lse_out[rows, :] = lse
    own = pl.multiple_of(side[1] * half_rows, 16)
    other = pl.multiple_of((1 - side[1]) * half_rows, 16)
    h_own[...] = low16(heads[pl.ds(own, half_rows), :])
    h_send[...] = low16(heads[pl.ds(other, half_rows), :])


def middle_kernel(side, h_own, h_recv, own, cot, gains, *refs):
    arrays, outs = refs[:8], refs[8:]
    mixed, resid_grad, gain_grad, hg_own, hg_send, xt_mine, xt_send, y_out = outs[:8]
    wo, wi, wt, turned, keep, final, pre = outs[8:]
    own_rows, feature_count = cot.shape
    mu, sd = own[:, feature_count : feature_count + 1], own[:, feature_count + 1 : feature_count + 2]
    gain_mid = gains[1:2, :]
    blocks = [(array, index) for array in arrays for index in range(array.shape[0])]
    for i, (array, index) in enumerate(blocks):
        row = pl.multiple_of(side[4 + i] * 80, 16)
        for j, full in enumerate((wo, wi, wt)):
            full[side[36 + i], pl.ds(row, 80), :] = array[index, 80 * j : 80 * j + 80, :]

    def turn(j, value):
        for i in range(feature_count // 128):
            turned[128 * i : 128 * i + 128, :] = low16(value[:, 128 * i : 128 * i + 128].T)
        for i in range(8):
            mine = pl.multiple_of((2 * i + side[0]) * 80, 16)
            other = pl.multiple_of((2 * i + 1 - side[0]) * 80, 16)
            xt_mine[j, 80 * i : 80 * i + 80, :] = turned[pl.ds(mine, 80), :]
            xt_send[j, 80 * i : 80 * i + 80, :] = turned[pl.ds(other, 80), :]

    y_out[0, 0] = h_own[...]
    y_out[0, 1] = h_recv[...]
    resid = own[:, :feature_count] + against(h_own[...], wo[0]) + against(h_recv[...], wo[1])
    normed, factor = rms_norm(resid)
    keep[...] = normed
    mid = normed * gain_mid
    turn(1, mid)
    mid = low16(mid)
    final_grad = wide(cot[...]) * sd
    mlp_grad = low16(final_grad)
    turn(2, final_grad)
    final[...] = resid
    for r in range(2):
        pre_act = dot(mid, wi[r])
        pre[r] = pre_act
        y_out[2, r] = low16(pre_act * (1.0 / (1.0 + jnp.exp(-pre_act))))
    final[...] += against(y_out[2, 0], wt[0]) + against(y_out[2, 1], wt[1])
    mixed[...] = low16(mu + sd * final[...])
    spread = jnp.sum(wide(cot[...]) * final[...], axis=1, keepdims=True)
    resid_grad[:, feature_count:] = jnp.broadcast_to(spread, (own_rows, 128))
    for r in range(2):
        hidden_grad = dot(mlp_grad, wt[r])
        pre_act = pre[r]
        sigmoid = 1.0 / (1.0 + jnp.exp(-pre_act))
        y_out[1, r] = low16(hidden_grad * sigmoid * (1.0 + pre_act * (1.0 - sigmoid)))
    mid_grad = against(y_out[1, 0], wi[0]) + against(y_out[1, 1], wi[1])
    normed = keep[...]
    gain_grad[...] = jnp.sum(mid_grad * normed, axis=0, keepdims=True)
    total = final_grad + norm_back(mid_grad * gain_mid, normed, factor)
    resid_grad[:, :feature_count] = total
    attn_grad = low16(total)
    hg_own[...] = low16(dot(attn_grad, wo[0]))
    hg_send[...] = low16(dot(attn_grad, wo[1]))
    turn(0, total)


def middle_weights_kernel(side, xt, xt_recv, y_own, y_recv, send, kept, total):
    for j in range(3):
        for r in range(2):
            total[j, r] = dot(xt[j], y_own[j, r]) + dot(xt_recv[j], y_recv[j, r])
    core, x = side[0], side[2]
    for u in range(2):
        for z in range(4):
            for out, sent in ((send, 1), (kept, 0)):
                other_x = jnp.where(core == 0, u, sent)
                other_y = jnp.where(core == 0, sent, u)
                spot = 2 * z + jnp.where(other_x == 0, x, 1 - x)
                row = pl.multiple_of(spot * 80, 16)
                for j in range(3):
                    out[u, z, 80 * j : 80 * j + 80, :] = low16(total[j, other_y, pl.ds(row, 80), :])


def attention_back_kernel(
    side, q, k, v, lse, hg_own, hg_recv, tables, seg_column, seg_row, out, bias, grad, dq, dk, dv
):
    group_rows, width = q.shape
    half_rows = group_rows // 2
    grad[pl.ds(pl.multiple_of(side[1] * half_rows, 16), half_rows), :] = hg_own[...]
    grad[pl.ds(pl.multiple_of((1 - side[1]) * half_rows, 16), half_rows), :] = hg_recv[...]
    fill_bias(bias, seg_column, seg_row)
    for part in (dq, dk, dv):
        part[...] = jnp.zeros_like(part)
    scale = HEAD_DIM ** (-0.5)
    for r in range(2):
        rows = slice(half_rows * r, half_rows * (r + 1))
        seen = slice(0, half_rows * (r + 1))
        for h in range(width // HEAD_DIM):
            window, keep = head_window(h)
            q_head = q[rows, window] * keep
            g_head = grad[rows, window] * keep
            scores = against(q_head, k[seen, window]) * scale + bias[rows, seen]
            probs = jnp.exp(scores - lse[rows, h : h + 1])
            prob_grad = against(g_head, v[seen, window])
            inner = jnp.sum(probs * prob_grad, axis=1, keepdims=True)
            score_grad = low16(probs * (prob_grad - inner))
            dq[rows, window] += dot(score_grad, k[seen, window] * keep)
            dk[seen, window] += across(score_grad, q_head)
            dv[seen, window] += across(low16(probs), g_head)
    for r in range(2):
        rows = slice(half_rows * r, half_rows * (r + 1))
        for j, part in enumerate((dq, dk)):
            value = part[rows, :] * scale
            out[rows, width * j : width * (j + 1)] = low16(
                value * tables[rows, :width] - swap_halves(value) * tables[rows, width:]
            )
        out[rows, 2 * width :] = low16(dv[rows, :])


def gain_window(place):
    return min(place * 80 // 128 * 128, 1024)


def input_grad_kernel(side, d_qkv, w_full, normed, gain_mid_grad, own, send, gain_parts):
    half_rows = own.shape[0]
    mine = pl.ds(pl.multiple_of(side[1] * half_rows, 16), half_rows)
    other = pl.ds(pl.multiple_of((1 - side[1]) * half_rows, 16), half_rows)
    part = against(d_qkv[other, :], w_full[...])
    send[...] = low16(part)
    gain = jnp.sum(part * normed[other, :], axis=0, keepdims=True)
    part = against(d_qkv[mine, :], w_full[...])
    own[...] = part
    gain = gain + jnp.sum(part * normed[mine, :], axis=0, keepdims=True)
    for place in range(16):
        first = gain_window(place)
        for y in range(2):
            gain_parts[2 * place + y, 0:1] = gain[:, first : first + 256]
            gain_parts[2 * place + y, 1:2] = gain_mid_grad[:, first : first + 256]


def first_weights_kernel(side, at, at_recv, d_qkv, d_recv, *outs):
    far, near, kept, total = outs
    width = total.shape[1] // 3
    for j in range(3):
        columns = slice(width * j, width * (j + 1))
        total[:, columns] = dot(at[...], d_qkv[:, columns]) + dot(at_recv[...], d_recv[:, columns])
    x, z = side[2], side[3]
    for step in range(4):
        there = lax.rem(z + step, 4)
        row = pl.multiple_of((2 * there + 1 - x) * 80, 16)
        if step == 2:
            far[...] = low16(total[pl.ds(row, 80), :])
        else:
            near[step % 4 // 2 + step % 2] = low16(total[pl.ds(row, 80), :])
        row = pl.multiple_of((2 * there + x) * 80, 16)
        kept[step] = low16(total[pl.ds(row, 80), :])


ALL_AXES = ("z", "x", "c", "y")
Z_STEPS = (1, 3, 2)


def flip(value, axis):
    return lax.ppermute(value, axis, [(0, 1), (1, 0)])


def shift_z(value, step):
    return lax.ppermute(value, "z", [(i, (i + step) % 4) for i in range(4)])


def flip_split(value, first):
    pairs = []
    for z in range(4):
        for x in range(2):
            for c in range(2):
                for y in range(2):
                    there = (z, 1 - x, c, y) if c == first else (z, x, c, 1 - y)
                    here = ((z * 2 + x) * 2 + c) * 2 + y
                    pairs.append((here, ((there[0] * 2 + there[1]) * 2 + there[2]) * 2 + there[3]))
    return lax.ppermute(value, ALL_AXES, pairs)


def pick(array, index, axis=0):
    return lax.dynamic_index_in_dim(array, index, axis, keepdims=False)


def local_fast(
    tokens,
    w_query,
    w_key,
    w_value,
    w_output,
    w_in,
    w_out,
    gain_attn,
    gain_mlp,
    seq_lengths,
    seq_offsets,
    cotangent,
):
    z, x, c, y = (lax.axis_index(name) for name in ALL_AXES)
    own_rows, feature_count = tokens.shape
    head_width = w_query.shape[1]
    group_rows = 2 * own_rows

    q_marks = [(0, 0), (1, 0), (3, 0), (0, 1), (2, 0), (2, 1), (1, 1), (3, 1)]
    q_place = jnp.stack(
        [
            ((z - step) % 4 * 2 + (x ^ xr)) * 2 + (c ^ cr)
            for cr in range(2)
            for step, xr in q_marks
        ]
    ).astype(jnp.int32)
    places, halves = [], []
    for cr in range(2):
        core = c ^ cr
        for second, third in ((0, 0), (1, 0), (0, 1), (1, 1)):
            for step in (0, 1, 3, 2):
                xr = jnp.where(core == 0, second, third)
                places.append(((z - step) % 4 * 2 + (x ^ xr)) * 2 + core)
                halves.append(jnp.where(core == 0, third, second))
    side = jnp.concatenate(
        [jnp.stack([c, y, x, z, *places, *halves]).astype(jnp.int32), q_place]
    )

    gains = jnp.pad(
        jnp.stack([gain_attn, gain_mlp]), ((0, 14), (0, head_width - gain_attn.shape[0]))
    )
    q_block = jnp.concatenate([w_query, w_key, w_value, gains], axis=0)
    p_block = jnp.concatenate([w_output.T, w_in, w_out.T], axis=0)
    tokens_other = flip(tokens, "y")
    near = [shift_z(q_block, step) for step in (1, 3)]
    far = shift_z(near[0], 1)
    across_own = flip(q_block, "x")
    q_first = stack_blocks([q_block, *near, across_own], "stack_first")
    near = stack_blocks(near, "stack_near")
    lengths, offsets = seq_lengths[0], seq_offsets[0]
    half = (own_rows, head_width)
    group = (group_rows, head_width)
    own_full = (own_rows, feature_count)
    own_more = (own_rows, feature_count + 128)
    position = row_layout(lengths, offsets, group_rows)[2]
    turns = jnp.concatenate(rotary_tables(position), axis=1)
    normed_in, rows_own, stats, tables, seg_column, seg_row = local_kernel(
        group_kernel,
        [
            ((group_rows, feature_count), F32),
            (own_more, F32),
            ((8, 128), F32),
            ((group_rows, 2 * head_width), F32),
            ((group_rows, 1), jnp.int32),
            ((1, group_rows), jnp.int32),
        ],
        3,
        [((group_rows, feature_count), BF)],
        "group",
        10,
    )(side, lengths, offsets, tokens, tokens_other, turns)

    (far,) = hold([far], [normed_in])
    q_parts = [q_first, far[None], flip(far, "x")[None], flip(near, "x")]
    q_all = q_parts + [flip(part, "c") for part in q_parts]

    (p_block,) = hold([p_block], [far])
    p_near = [shift_z(p_block, step) for step in (1, 3)]
    vector = ((1, feature_count), F32)
    w_full, at_mine, at_send, q_rot, k_rot, values, gains = local_kernel(
        project_kernel,
        [
            ((feature_count, 3 * head_width), BF),
            ((feature_count // 2, group_rows), BF),
            ((feature_count // 2, group_rows), BF),
            (group, BF),
            (group, BF),
            (group, BF),
            ((2, feature_count), F32),
        ],
        1,
        [((32, 128), F32), ((group_rows, feature_count), BF), ((feature_count, group_rows), BF)],
        "project",
        10,
    )(side, normed_in, tables, q_place[:, None], *q_all)
    (p_near[0],) = hold([p_near[0]], [q_rot])
    p_far = shift_z(p_near[0], 1)
    lse, h_own, h_send = local_kernel(
        attention_kernel,
        [((group_rows, 128), F32), (half, BF), (half, BF)],
        1,
        [((group_rows, group_rows), F32), (group, F32)],
        "attention",
        8,
    )(side, q_rot, k_rot, values, seg_column, seg_row)
    (p_block,) = hold([p_block], [lse])
    p_first = stack_blocks([p_block, *p_near, p_far], "stack_middle")
    p_second = flip_split(p_first, 0)
    p_third = flip_split(p_first, 1)
    h_recv = flip(h_send, "y")
    (p_second,) = hold([p_second], [h_recv])
    p_parts = [p_first, p_second, p_third, flip_split(p_second, 1)]
    p_all = p_parts + [flip(part, "c") for part in p_parts]
    at_recv = flip(at_send, "c")

    mixed, resid_grad, gain_mid_grad, hg_own, hg_send, xt_mine, xt_send, y_own = (
        local_kernel(
            middle_kernel,
            [
                (own_full, BF),
                (own_more, F32),
                ((1, feature_count), F32),
                (half, BF),
                (half, BF),
                ((3, feature_count // 2, own_rows), BF),
                ((3, feature_count // 2, own_rows), BF),
                ((3, 2) + half, BF),
            ],
            1,
            [((2, feature_count, head_width), BF)] * 3
            + [((feature_count, own_rows), BF), (own_full, F32), (own_full, F32), ((2,) + half, F32)],
            "middle",
            31,
        )(
            side, h_own, h_recv, rows_own, cotangent, gains, *p_all
        )
    )
    hg_recv = flip(hg_send, "y")
    xt_recv, y_recv = flip(xt_send, "c"), flip(y_own, "c")

    quarter = (2, 4, 3 * 80, head_width)
    p_send, p_kept = local_kernel(
        middle_weights_kernel,
        [(quarter, BF), (quarter, BF)],
        1,
        [((3, 2, feature_count // 2, head_width), F32)],
        "middle_weights",
        14,
    )(side, xt_mine, xt_recv, y_own, y_recv)
    (p_send,) = hold([p_send], [hg_recv])
    p_recv = flip_split(p_send, 1)

    (d_qkv,) = local_kernel(
        attention_back_kernel,
        [((group_rows, 3 * head_width), BF)],
        1,
        [((group_rows, group_rows), F32), (group, BF), (group, F32), (group, F32), (group, F32)],
        "attention_back",
        11,
        after=[p_send],
    )(side, q_rot, k_rot, values, lse, hg_own, hg_recv, tables, seg_column, seg_row)
    d_recv = flip(d_qkv, "c")
    in_own, in_send, gain_parts = local_kernel(
        input_grad_kernel,
        [(own_full, F32), (own_full, BF), ((32, 2, 256), F32)],
        1,
        [],
        "input_grad",
        10,
    )(side, d_qkv, w_full, normed_in, gain_mid_grad)
    slab = (80, 3 * head_width)
    far, near, q_kept, p_kept, gain_parts, in_own = local_kernel(
        first_weights_kernel,
        [(slab, BF), ((3,) + slab, BF), ((4,) + slab, BF)],
        1,
        [((feature_count // 2, 3 * head_width), F32)],
        "first_weights",
        12,
        gates=[p_kept, gain_parts, in_own],
    )(side, at_mine, at_recv, d_qkv, d_recv)
    far = flip(far, "x")

    p_send, p_kept, far = local_kernel(
        first_sum_kernel, [(quarter[1:], BF)] * 2 + [(slab, BF)], 0, [], "first_sum", 4
    )(p_kept, p_recv, q_kept, far)
    p_recv = flip_split(p_send, 0)
    q_two = shift_z(far, 1)
    gain_parts = lax.all_to_all(gain_parts, ALL_AXES, 0, 0, tiled=True)
    near, in_send = hold([near, in_send], [p_recv, q_two, gain_parts])
    near, in_recv = flip(near, "x"), flip(in_send, "y")
    piece = quarter[2:]
    p_own, p_one, p_two, p_three = local_kernel(
        second_sum_kernel,
        [(piece, F32), (piece, F32)] + [(piece, BF)] * 2,
        1,
        [],
        "second_sum",
        4,
    )(side, p_kept, p_recv)
    p_three = shift_z(p_three, 3)
    (p_one,) = local_kernel(third_sum_kernel, [(piece, BF)], 0, [], "third_sum", 2)(
        p_one, shift_z(p_two, 1)
    )
    q_own, near_one, near_three, gain_grads = local_kernel(
        near_sum_kernel,
        [(slab, F32), (slab, BF), (slab, BF), ((2, 80), F32)],
        1,
        [],
        "near_sum",
        4,
        after=[p_one],
    )(side, q_kept, near, q_two, gain_parts)
    q_one, q_three = shift_z(near_one, 1), shift_z(near_three, 3)
    p_one = shift_z(p_one, 1)
    scaled, sums = local_kernel(
        token_sums_kernel,
        [(own_full, F32), ((8, 128), F32)],
        3,
        [],
        "token_sums",
        8,
        after=[near_one],
    )(
        side, lengths, offsets, in_own, in_recv, gains, resid_grad, normed_in, rows_own, cotangent
    )
    sums_recv = flip(sums, "y")
    (grad_tokens,) = local_kernel(
        token_grad_kernel, [(own_full, F32)], 2, [], "token_grad", 6
    )(side, offsets, scaled, sums, sums_recv, stats, tokens, rows_own)

    shard = ((80, head_width), F32)
    grad_query, grad_key, grad_value = local_kernel(
        first_total_kernel, [shard] * 3, 0, [], "first_total", 4
    )(q_own, q_one, q_three)
    grad_output, grad_in, grad_out = local_kernel(
        middle_total_kernel, [shard] * 3, 0, [], "middle_total", 4
    )(p_own, p_one, p_three)
    return (
        mixed,
        grad_tokens,
        grad_query,
        grad_key,
        grad_value,
        grad_output.T,
        grad_in,
        grad_out.T,
        gain_grads[0],
        gain_grads[1],
    )


def solution_fast(mesh):
    fine = Mesh(mesh.devices.reshape(4, 2, 2, 2), ALL_AXES)
    dp = ("z", "x", "c")
    rows, by_row, by_column = P(ALL_AXES, None), P(dp, "y"), P("y", dp)
    in_specs = (rows,) + (by_row,) * 3 + (by_column, by_row, by_column)
    in_specs += (P(dp), P(dp), P(dp, None), P(dp, None), rows)
    out_specs = (rows, rows) + (by_row,) * 3 + (by_column, by_row, by_column, P(dp), P(dp))
    return jax.shard_map(
        local_fast, mesh=fine, in_specs=in_specs, out_specs=out_specs, check_vma=False
    )


def solution(mesh):
    if dict(mesh.shape) == {"dp": 16, "tensor": 2}:
        return solution_fast(mesh)
    in_specs = (
        P(("dp", "tensor"), None),
        P("dp", "tensor"),
        P("dp", "tensor"),
        P("dp", "tensor"),
        P("tensor", "dp"),
        P("dp", "tensor"),
        P("tensor", "dp"),
        P("dp"),
        P("dp"),
        P("dp", None),
        P("dp", None),
        P(("dp", "tensor"), None),
    )
    out_specs = (
        P(("dp", "tensor"), None),
        P(("dp", "tensor"), None),
        P("dp", "tensor"),
        P("dp", "tensor"),
        P("dp", "tensor"),
        P("tensor", "dp"),
        P("dp", "tensor"),
        P("tensor", "dp"),
        P("dp"),
        P("dp"),
    )
    return jax.shard_map(local, mesh=mesh, in_specs=in_specs, out_specs=out_specs, check_vma=False)
```

```python
import jax
import jax.numpy as jnp
from jax import lax
from jax.experimental import pallas as pl
from jax.experimental.pallas import tpu as pltpu
from jax.sharding import Mesh
from jax.sharding import PartitionSpec as P

HEAD_DIM = 80


highest = lax.Precision.HIGHEST
epsilon = 1e-06
stat_eps = 1e-05
masked_score = -1e30
contract_last = (((1,), (1,)), ((), ()))
contract_first = (((0,), (0,)), ((), ()))


def against(left, right):
    return lax.dot_general(left, right, contract_last, preferred_element_type=jnp.float32)


def across(left, right):
    return lax.dot_general(left, right, contract_first, preferred_element_type=jnp.float32)


def row_layout(lengths, offsets, group_rows):
    row_ids = jnp.arange(group_rows, dtype=jnp.int32)
    inside = (row_ids[:, None] >= offsets[None, :]) & (
        row_ids[:, None] < offsets[None, :] + lengths[None, :]
    )
    member = inside.astype(jnp.float32)
    slot_ids = jnp.arange(offsets.shape[0], dtype=jnp.int32)
    segment = jnp.sum(jnp.where(inside, slot_ids[None, :] + 1, 0), axis=1) - 1
    seq_start = jnp.sum(jnp.where(inside, offsets[None, :], 0), axis=1)
    position = jnp.where(segment >= 0, row_ids - seq_start, 0).astype(jnp.float32)
    first_rows = (row_ids[:, None] == offsets[None, :]).astype(jnp.float32)
    return (member, segment, position, first_rows)


def rotary_tables(position):
    half_dim = HEAD_DIM // 2
    freqs = 10000.0 ** (-2.0 * jnp.arange(half_dim, dtype=jnp.float32) / HEAD_DIM)
    angles = position[:, None] * freqs[None, :]
    return (jnp.cos(angles), jnp.sin(angles))


def rotate(values, cosine, sine, direction):
    row_count = values.shape[0]
    shaped = values.reshape(row_count, -1, HEAD_DIM)
    half_dim = HEAD_DIM // 2
    first_half = shaped[..., :half_dim]
    second_half = shaped[..., half_dim:]
    cos_b = cosine[:, None, :]
    sin_b = sine[:, None, :] * direction
    turned = jnp.concatenate(
        [first_half * cos_b - second_half * sin_b, first_half * sin_b + second_half * cos_b],
        axis=-1,
    )
    return turned.reshape(row_count, -1)


def rms_norm(values):
    factor = lax.rsqrt(jnp.mean(values * values, axis=-1, keepdims=True) + epsilon)
    return (values * factor, factor)


def norm_back(grad_normed, normed, factor):
    return factor * (grad_normed - normed * jnp.mean(grad_normed * normed, axis=-1, keepdims=True))


def allowed_mask(seg_query, query_ids, segment, key_ids):
    same = (
        (seg_query[:, None] == segment[None, :])
        & (key_ids[None, :] <= query_ids[:, None])
        & (seg_query[:, None] >= 0)
    )
    return same | (query_ids[:, None] == key_ids[None, :])


def block_scores(query_all, key_all, segment, row_begin, block_rows):
    group_rows = key_all.shape[0]
    key_ids = jnp.arange(group_rows, dtype=jnp.int32)
    query_ids = row_begin + jnp.arange(block_rows, dtype=jnp.int32)
    queries = lax.dynamic_slice_in_dim(query_all, row_begin, block_rows, 0)
    scores = jnp.einsum(
        "qhd,khd->hqk", queries, key_all, preferred_element_type=jnp.float32
    ) * HEAD_DIM ** (-0.5)
    seg_query = lax.dynamic_slice_in_dim(segment, row_begin, block_rows, 0)
    mask = allowed_mask(seg_query, query_ids, segment, key_ids)
    return (jnp.where(mask[None], scores, masked_score), queries)


def attention_forward(q_rot, k_rot, values, segment):
    group_rows, head_width = q_rot.shape
    block_rows = min(512, group_rows)
    query_all = q_rot.reshape(group_rows, -1, HEAD_DIM)
    key_all = k_rot.reshape(group_rows, -1, HEAD_DIM)
    value_all = values.reshape(group_rows, -1, HEAD_DIM)

    def one_block(block_index):
        scores, queries = block_scores(
            query_all, key_all, segment, block_index * block_rows, block_rows
        )
        top = jnp.max(scores, axis=-1, keepdims=True)
        expo = jnp.exp(scores - top)
        total_exp = jnp.sum(expo, axis=-1, keepdims=True)
        probs = (expo / total_exp).astype(jnp.bfloat16)
        heads = jnp.einsum("hqk,khd->qhd", probs, value_all, preferred_element_type=jnp.float32)
        return (heads.reshape(block_rows, head_width), (top + jnp.log(total_exp))[..., 0])

    outs, log_sums = lax.map(one_block, jnp.arange(group_rows // block_rows, dtype=jnp.int32))
    return (outs.reshape(group_rows, head_width), log_sums)


def attention_backward(q_rot, k_rot, values, segment, log_sums, heads_grad):
    group_rows, head_width = q_rot.shape
    block_rows = min(512, group_rows)
    query_all = q_rot.reshape(group_rows, -1, HEAD_DIM)
    key_all = k_rot.reshape(group_rows, -1, HEAD_DIM)
    value_all = values.reshape(group_rows, -1, HEAD_DIM)
    grad_all = heads_grad.reshape(group_rows, -1, HEAD_DIM)
    scale_factor = HEAD_DIM ** (-0.5)

    def one_block(carry, block_index):
        key_grad, value_grad = carry
        row_begin = block_index * block_rows
        scores, queries = block_scores(query_all, key_all, segment, row_begin, block_rows)
        probs = jnp.exp(scores - log_sums[block_index][..., None])
        grads_block = lax.dynamic_slice_in_dim(grad_all, row_begin, block_rows, 0)
        prob_grad = jnp.einsum(
            "qhd,khd->hqk", grads_block, value_all, preferred_element_type=jnp.float32
        )
        inner = jnp.sum(probs * prob_grad, axis=-1, keepdims=True)
        score_grad = (probs * (prob_grad - inner)).astype(jnp.bfloat16)
        query_grad = (
            jnp.einsum("hqk,khd->qhd", score_grad, key_all, preferred_element_type=jnp.float32)
            * scale_factor
        )
        key_grad = (
            key_grad
            + jnp.einsum("hqk,qhd->khd", score_grad, queries, preferred_element_type=jnp.float32)
            * scale_factor
        )
        value_grad = value_grad + jnp.einsum(
            "hqk,qhd->khd",
            probs.astype(jnp.bfloat16),
            grads_block,
            preferred_element_type=jnp.float32,
        )
        return ((key_grad, value_grad), query_grad.reshape(block_rows, head_width))

    zeros = jnp.zeros(query_all.shape, jnp.float32)
    (key_grad, value_grad), query_grads = lax.scan(
        one_block, (zeros, zeros), jnp.arange(group_rows // block_rows, dtype=jnp.int32)
    )
    return (
        query_grads.reshape(group_rows, head_width),
        key_grad.reshape(group_rows, head_width),
        value_grad.reshape(group_rows, head_width),
    )


def split_weights(rows_full, columns_full, gains_full, head_width):
    qkv_width = 3 * head_width
    return (
        rows_full[:, :qkv_width],
        rows_full[:, qkv_width:],
        columns_full[:head_width],
        columns_full[head_width:],
        gains_full[0].astype(jnp.float32),
        gains_full[1].astype(jnp.float32),
    )


def local(
    tokens,
    w_query,
    w_key,
    w_value,
    w_output,
    w_in,
    w_out,
    gain_attn,
    gain_mlp,
    seq_lengths,
    seq_offsets,
    cotangent,
):
    own_rows = tokens.shape[0]
    feature_count = tokens.shape[1]
    head_width = w_query.shape[1]
    qkv_width = 3 * head_width
    row_blocks = jnp.concatenate([w_query, w_key, w_value, w_in], axis=1)
    column_blocks = jnp.concatenate([w_output, w_out], axis=0)
    gain_pair = jnp.stack([gain_attn, gain_mlp])
    rows_full, columns_full, gains_full = (
        lax.all_gather(row_blocks, "dp", axis=0, tiled=True),
        lax.all_gather(column_blocks, "dp", axis=1, tiled=True),
        lax.all_gather(gain_pair, "dp", axis=1, tiled=True),
    )
    w_qkv_full, w_in_full, w_output_full, w_out_full, gain_in, gain_mid = split_weights(
        rows_full, columns_full, gains_full, head_width
    )
    tokens_full = lax.all_gather(tokens, "tensor", axis=0, tiled=True)
    group_rows = tokens_full.shape[0]
    member, segment, position, first_rows = row_layout(seq_lengths[0], seq_offsets[0], group_rows)
    firsts = jnp.dot(
        first_rows.T.astype(jnp.bfloat16), tokens_full, preferred_element_type=jnp.float32
    )
    mu_seq = jnp.mean(firsts, axis=1)
    sd_seq = jnp.sqrt(jnp.mean(jnp.square(firsts - mu_seq[:, None]), axis=1) + stat_eps)
    live = jnp.sum(member, axis=1)
    mu_row = jnp.dot(member, mu_seq, precision=highest)
    sd_row = jnp.dot(member, sd_seq, precision=highest) + (1.0 - live)
    centered = (tokens_full.astype(jnp.float32) - mu_row[:, None]) / sd_row[:, None]
    normed_in, scale_in = rms_norm(centered)
    attn_in = (normed_in * gain_in).astype(jnp.bfloat16)
    projected = jnp.dot(attn_in, w_qkv_full, preferred_element_type=jnp.float32)
    cosine, sine = rotary_tables(position)
    q_rot = rotate(projected[:, :head_width], cosine, sine, 1.0).astype(jnp.bfloat16)
    k_rot = rotate(projected[:, head_width : 2 * head_width], cosine, sine, 1.0).astype(
        jnp.bfloat16
    )
    values = projected[:, 2 * head_width :].astype(jnp.bfloat16)
    heads_out, log_sums = attention_forward(q_rot, k_rot, values, segment)
    heads_low = heads_out.astype(jnp.bfloat16)
    attn_own = lax.psum_scatter(
        jnp.dot(heads_low, w_output_full, preferred_element_type=jnp.float32),
        "tensor",
        scatter_dimension=0,
        tiled=True,
    )
    own_start = lax.axis_index("tensor") * own_rows

    def own_part(array):
        return lax.dynamic_slice_in_dim(array, own_start, own_rows, 0)

    centered_own = own_part(centered)
    resid = centered_own + attn_own
    normed_mid, scale_mid = rms_norm(resid)
    mid_low = (normed_mid * gain_mid).astype(jnp.bfloat16)
    mid_full = lax.all_gather(mid_low, "tensor", axis=0, tiled=True)
    pre_act = jnp.dot(mid_full, w_in_full, preferred_element_type=jnp.float32)
    hidden = jax.nn.silu(pre_act).astype(jnp.bfloat16)
    mlp_own = lax.psum_scatter(
        jnp.dot(hidden, w_out_full, preferred_element_type=jnp.float32).astype(jnp.bfloat16),
        "tensor",
        scatter_dimension=0,
        tiled=True,
    ).astype(jnp.float32)
    final = resid + mlp_own
    mu_own = own_part(mu_row)
    sd_own = own_part(sd_row)
    mixed = (mu_own[:, None] + sd_own[:, None] * final).astype(jnp.bfloat16)
    rows_full, columns_full, gains_full = (
        lax.all_gather(row_blocks, "dp", axis=0, tiled=True),
        lax.all_gather(column_blocks, "dp", axis=1, tiled=True),
        lax.all_gather(gain_pair, "dp", axis=1, tiled=True),
    )
    w_qkv_full, w_in_full, w_output_full, w_out_full, gain_in, gain_mid = split_weights(
        rows_full, columns_full, gains_full, head_width
    )
    grad_out = cotangent.astype(jnp.float32)
    final_grad = grad_out * sd_own[:, None]
    mlp_grad_full = lax.all_gather(final_grad.astype(jnp.bfloat16), "tensor", axis=0, tiled=True)
    hidden_grad = against(mlp_grad_full, w_out_full)
    d_w_out = across(hidden, mlp_grad_full)
    sigmoid_act = jax.nn.sigmoid(pre_act)
    act_grad = (hidden_grad * sigmoid_act * (1.0 + pre_act * (1.0 - sigmoid_act))).astype(
        jnp.bfloat16
    )
    d_w_in = across(mid_full, act_grad)
    mid_grad = lax.psum_scatter(
        against(act_grad, w_in_full), "tensor", scatter_dimension=0, tiled=True
    )
    gain_mid_grad = jnp.sum(mid_grad * normed_mid, axis=0)
    resid_grad = final_grad + norm_back(mid_grad * gain_mid, normed_mid, scale_mid)
    attn_grad_full = lax.all_gather(resid_grad.astype(jnp.bfloat16), "tensor", axis=0, tiled=True)
    heads_grad = against(attn_grad_full, w_output_full).astype(jnp.bfloat16)
    d_w_output = across(heads_low, attn_grad_full)
    q_rot_grad, k_rot_grad, values_grad = attention_backward(
        q_rot, k_rot, values, segment, log_sums, heads_grad
    )
    proj_grad = jnp.concatenate(
        [
            rotate(q_rot_grad, cosine, sine, -1.0).astype(jnp.bfloat16),
            rotate(k_rot_grad, cosine, sine, -1.0).astype(jnp.bfloat16),
            values_grad.astype(jnp.bfloat16),
        ],
        axis=1,
    )
    d_w_qkv = across(attn_in, proj_grad)
    in_grad = lax.psum_scatter(
        against(proj_grad, w_qkv_full), "tensor", scatter_dimension=0, tiled=True
    )
    normed_own = own_part(normed_in)
    gain_in_grad = jnp.sum(in_grad * normed_own, axis=0)
    centered_grad = resid_grad + norm_back(in_grad * gain_in, normed_own, own_part(scale_in))
    scaled_grad = centered_grad / sd_own[:, None]
    per_row = jnp.stack(
        [
            jnp.sum(grad_out - scaled_grad, axis=1),
            jnp.sum(grad_out * final - scaled_grad * centered_own, axis=1),
        ],
        axis=1,
    )
    seq_part = jnp.dot(own_part(member).T, per_row, precision=highest)
    gain_part = jnp.stack([gain_in_grad, gain_mid_grad])
    gain_total, seq_total = lax.psum((gain_part, seq_part), "tensor")
    first_own = own_part(first_rows)
    mean_term = jnp.dot(first_own, seq_total[:, 0] / feature_count, precision=highest)
    spread_term = jnp.dot(first_own, seq_total[:, 1] / (feature_count * sd_seq), precision=highest)
    grad_tokens = (
        scaled_grad
        + mean_term[:, None]
        + spread_term[:, None] * (tokens.astype(jnp.float32) - mu_own[:, None])
    )
    grad_rows, grad_columns, gain_grads = (
        lax.psum_scatter(
            jnp.concatenate([d_w_qkv, d_w_in], axis=1), "dp", scatter_dimension=0, tiled=True
        ),
        lax.psum_scatter(
            jnp.concatenate([d_w_output, d_w_out], axis=0), "dp", scatter_dimension=1, tiled=True
        ),
        lax.psum_scatter(gain_total, "dp", scatter_dimension=1, tiled=True),
    )
    return (
        mixed,
        grad_tokens,
        grad_rows[:, :head_width],
        grad_rows[:, head_width : 2 * head_width],
        grad_rows[:, 2 * head_width : qkv_width],
        grad_columns[:head_width],
        grad_rows[:, qkv_width:],
        grad_columns[head_width:],
        gain_grads[0],
        gain_grads[1],
    )


HALF = HEAD_DIM // 2
VMEM_SPEC = pl.BlockSpec(memory_space=pltpu.VMEM)
SMEM_SPEC = pl.BlockSpec(memory_space=pltpu.SMEM)


def low16(value):
    return value.astype(jnp.bfloat16)


def wide(value):
    return value.astype(jnp.float32)


def dot(left, right):
    return jnp.dot(left, right, preferred_element_type=jnp.float32)


def local_kernel(body, outs, scalars, scratch, name, mib, gates=(), after=(), loose=0):
    def call(*operands):
        count = len(operands)
        left, held = len(gates) + len(after), len(gates)

        def trimmed(*refs):
            end = count + left + len(outs)
            body(*refs[:count], *refs[count + left : end], *refs[end + held :])

        any_spec = pl.BlockSpec(memory_space=pl.ANY)
        return pl.pallas_call(
            trimmed,
            out_shape=tuple(jax.ShapeDtypeStruct(shape, kind) for shape, kind in outs)
            + tuple(jax.ShapeDtypeStruct(gate.shape, gate.dtype) for gate in gates),
            in_specs=[SMEM_SPEC] * scalars
            + [VMEM_SPEC] * (count - scalars - loose)
            + [pl.BlockSpec(memory_space=pltpu.HBM)] * loose
            + [any_spec] * left,
            out_specs=(VMEM_SPEC,) * len(outs) + (any_spec,) * held,
            scratch_shapes=[
                pltpu.VMEM(*item) if isinstance(item, tuple) else item for item in scratch
            ],
            input_output_aliases={count + i: len(outs) + i for i in range(held)},
            compiler_params=pltpu.CompilerParams(vmem_limit_bytes=mib * 2**20),
            cost_estimate=pl.CostEstimate(flops=1000, bytes_accessed=1000, transcendentals=0),
            name=name,
        )(*operands, *gates, *after)

    return call


BF, F32 = jnp.bfloat16, jnp.float32


def head_window(head):
    begin = head * HEAD_DIM
    first = begin // 128 * 128
    last = -(-(begin + HEAD_DIM) // 128) * 128
    lane = lax.broadcasted_iota(jnp.int32, (1, last - first), 1) + first
    inside = (lane >= begin) & (lane < begin + HEAD_DIM)
    return slice(first, last), low16(jnp.where(inside, 1.0, 0.0))


def swap_halves(value):
    width = value.shape[1]
    lane = lax.broadcasted_iota(jnp.int32, value.shape, 1) % HEAD_DIM
    return jnp.where(
        lane < HALF, pltpu.roll(value, width - HALF, 1), pltpu.roll(value, HALF, 1)
    )


def fill_bias(bias, seg_column, seg_row):
    rows = bias.shape[0]
    query = lax.broadcasted_iota(jnp.int32, (rows, rows), 0)
    key = lax.broadcasted_iota(jnp.int32, (rows, rows), 1)
    allowed = (seg_column[...] == seg_row[...]) & (key <= query)
    bias[...] = jnp.where(allowed, 0.0, masked_score)


def stack_kernel(*refs):
    for i, block in enumerate(refs[:-1]):
        refs[-1][i] = block[...]


def stack_blocks(blocks, name, after=()):
    rows, width = blocks[0].shape
    outs = [((len(blocks), rows, width), BF)]
    return local_kernel(stack_kernel, outs, 0, [], name, 4, after=after)(*blocks)[0]


def hold(arrays, after):
    mark = ((8, 128), F32)

    def body(out):
        out[...] = jnp.zeros_like(out)

    return local_kernel(body, [mark], 0, [], "hold", 1, gates=arrays, after=after)()[1:]


def group_kernel(
    side, lengths, offsets, own, other, turns, normed, rows_own, stats, tables,
    seg_column, seg_row, full,
):
    half_rows = own.shape[0]
    width = tables.shape[1] // 2
    lane = lax.broadcasted_iota(jnp.int32, (HEAD_DIM, width), 1) % HEAD_DIM
    source = lax.broadcasted_iota(jnp.int32, (HEAD_DIM, width), 0)
    high = low16(turns[...])
    low = low16(turns[...] - wide(high))
    same = lane % HALF == source % HALF
    for first, spread in (
        (0, jnp.where(same & (source < HALF), 1.0, 0.0)),
        (width, jnp.where(same & (source >= HALF), jnp.where(lane < HALF, -1.0, 1.0), 0.0)),
    ):
        tables[:, first : first + width] = dot(high, low16(spread)) + dot(low, low16(spread))
    for table, axis in ((seg_column, 0), (seg_row, 1)):
        row = lax.broadcasted_iota(jnp.int32, table.shape, axis)
        series = -1 - row
        for s in range(offsets.shape[0]):
            inside = (row >= offsets[s]) & (row < offsets[s] + lengths[s])
            series = jnp.where(inside, s, series)
        table[...] = series
    mine = pl.multiple_of(side[1] * half_rows, 16)
    full[pl.ds(mine, half_rows), :] = own[...]
    full[pl.ds(pl.multiple_of((1 - side[1]) * half_rows, 16), half_rows), :] = other[...]
    slots = offsets.shape[0]
    slot = lax.broadcasted_iota(jnp.int32, (8, 2 * half_rows), 0)
    column = lax.broadcasted_iota(jnp.int32, (8, 2 * half_rows), 1)
    chosen = jnp.zeros((8, 2 * half_rows), F32)
    for s in range(slots):
        chosen = jnp.where((slot == s) & (column == offsets[s]), 1.0, chosen)
    firsts = dot(low16(chosen), full[...])
    mu = jnp.mean(firsts, axis=1, keepdims=True)
    sd = jnp.sqrt(jnp.mean(jnp.square(firsts - mu), axis=1, keepdims=True) + stat_eps)
    lane = lax.broadcasted_iota(jnp.int32, (8, 128), 1)
    stats[...] = jnp.where(lane == 0, mu, sd)
    features = own.shape[1]
    extra = lax.broadcasted_iota(jnp.int32, (half_rows, 128), 1)
    for r in range(2):
        row = lax.broadcasted_iota(jnp.int32, (half_rows, 1), 0) + r * half_rows
        mu_row = jnp.zeros((half_rows, 1), F32)
        sd_row = jnp.ones((half_rows, 1), F32)
        for s in range(slots):
            inside = (row >= offsets[s]) & (row < offsets[s] + lengths[s])
            mu_row = jnp.where(inside, mu[s : s + 1, :], mu_row)
            sd_row = jnp.where(inside, sd[s : s + 1, :], sd_row)
        rows = slice(half_rows * r, half_rows * (r + 1))
        centered = (wide(full[rows, :]) - mu_row) / sd_row
        value, factor = rms_norm(centered)
        normed[rows, :] = value

        @pl.when(side[1] == r)
        def _():
            rows_own[:, :features] = centered
            rows_own[:, features:] = jnp.where(
                extra == 0, mu_row, jnp.where(extra == 1, sd_row, factor)
            )


def first_sum_kernel(kept, recv, q_kept, q_recv, send, rest, far):
    rest[...] = low16(wide(kept[0]) + wide(recv[0]))
    send[...] = low16(wide(kept[1]) + wide(recv[1]))
    far[...] = low16(wide(q_kept[2]) + wide(q_recv[...]))


def second_sum_kernel(side, kept, recv, *outs):
    for step, out in enumerate(outs):
        there = lax.rem(side[3] + step, 4)
        out[...] = (wide(kept[there]) + wide(recv[there])).astype(out.dtype)


def third_sum_kernel(kept, recv, send):
    send[...] = low16(kept[...] + wide(recv[...]))


def near_sum_kernel(side, kept, recv, passing, gain_parts, own, send_one, send_three, gain_grads):
    own[...] = wide(kept[0]) + wide(recv[0])
    send_one[...] = low16(wide(kept[1]) + wide(recv[1]) + wide(passing[...]))
    send_three[...] = low16(wide(kept[3]) + wide(recv[2]))
    place = (side[3] * 2 + side[2]) * 2 + side[0]
    shift = place * 80 - jnp.minimum(place * 80 // 128 * 128, 1024)
    gain_sum = jnp.concatenate([jnp.sum(gain_parts[...], axis=0), jnp.zeros((6, 256), F32)], 0)
    gain_grads[...] = pltpu.roll(gain_sum, lax.rem(256 - shift, 256), 1)[0:2, 0:80]


def first_total_kernel(own, one, three, *outs):
    for j, out in enumerate(outs):
        part = slice(640 * j, 640 * (j + 1))
        out[...] = own[:, part] + wide(one[:, part]) + wide(three[:, part])


def middle_total_kernel(own, one, three, *outs):
    for j, out in enumerate(outs):
        part = slice(80 * j, 80 * (j + 1))
        total = own[part, :] + wide(one[part, :]) + wide(three[part, :])
        out[...] = total


def token_sums_kernel(
    side, lengths, offsets, in_own, in_recv, gains, resid_grad, normed, own, cot, scaled, sums
):
    half_rows, features = in_own.shape
    sd, factor = own[:, features + 1 : features + 2], own[:, features + 2 : features + 3]
    mine = pl.ds(pl.multiple_of(side[1] * half_rows, 16), half_rows)
    in_grad = in_own[...] + wide(in_recv[...])
    back = norm_back(in_grad * gains[0:1, :], normed[mine, :], factor)
    value = (resid_grad[:, :features] + back) / sd
    scaled[...] = value
    first = jnp.sum(wide(cot[...]) - value, axis=1, keepdims=True)
    second = resid_grad[:, features : features + 1] - jnp.sum(value * own[:, :features], axis=1, keepdims=True)
    row = lax.broadcasted_iota(jnp.int32, (half_rows, 1), 0) + side[1] * half_rows
    slot = lax.broadcasted_iota(jnp.int32, (8, 128), 0)
    lane = lax.broadcasted_iota(jnp.int32, (8, 128), 1)
    table = jnp.zeros((8, 128), F32)
    for s in range(offsets.shape[0]):
        inside = (row >= offsets[s]) & (row < offsets[s] + lengths[s])
        for j, column in enumerate((first, second)):
            total = jnp.sum(jnp.where(inside, column, 0.0), axis=0, keepdims=True)
            table = jnp.where((slot == s) & (lane == j), total, table)
    sums[...] = table


def token_grad_kernel(side, offsets, scaled, sums, recv, stats, tokens, own, out):
    half_rows, feature_count = scaled.shape
    total = sums[...] + recv[...]
    row = lax.broadcasted_iota(jnp.int32, (half_rows, 1), 0) + side[1] * half_rows
    mean_term = jnp.zeros((half_rows, 1), F32)
    spread_term = jnp.zeros((half_rows, 1), F32)
    for s in range(offsets.shape[0]):
        here = row == offsets[s]
        mean_term = jnp.where(here, total[s : s + 1, 0:1] / feature_count, mean_term)
        spread = total[s : s + 1, 1:2] / (feature_count * stats[s : s + 1, 1:2])
        spread_term = jnp.where(here, spread, spread_term)
    out[...] = scaled[...] + mean_term + spread_term * (wide(tokens[...]) - own[:, feature_count : feature_count + 1])


def project_kernel(side, normed, tables, spot, *refs):
    arrays, outs = refs[:8], refs[8:]
    w_full, at_mine, at_send, q_out, k_out, v_out, gains = outs[:7]
    tail, attn_in, turned = outs[7:]
    group_rows, feature_count = normed.shape
    half_rows = group_rows // 2
    width = q_out.shape[1]
    blocks = [(array, index) for array in arrays for index in range(array.shape[0])]
    for i, (array, index) in enumerate(blocks):
        row = pl.multiple_of(side[68 + i] * 80, 16)
        for j in range(3):
            w_full[pl.ds(row, 80), pl.ds(width * j, width)] = array[index, pl.ds(80 * j, 80), :]
        ends = wide(array[index, pl.ds(240, 16), :128])
        tail[i : i + 1, :] = ends[0:1]
        tail[16 + i : 17 + i, :] = ends[1:2]
    lane = lax.broadcasted_iota(jnp.int32, (128, feature_count), 1)
    source = lax.broadcasted_iota(jnp.int32, (128, feature_count), 0)
    spread = low16(jnp.where(lane % 80 == source, 1.0, 0.0))
    held = lax.broadcasted_iota(jnp.int32, (16, feature_count), 1) // 80 == spot[...]
    gain_in = jnp.sum(jnp.where(held, dot(low16(tail[0:16]), spread), 0.0), 0, keepdims=True)
    gains[0:1, :] = gain_in
    gains[1:2, :] = jnp.sum(jnp.where(held, dot(low16(tail[16:32]), spread), 0.0), 0, keepdims=True)
    for i in range(feature_count // 128):
        part = normed[:, 128 * i : 128 * i + 128] * gain_in[:, 128 * i : 128 * i + 128]
        attn_in[:, 128 * i : 128 * i + 128] = low16(part)
        turned[128 * i : 128 * i + 128, :] = low16(part.T)
    for i in range(8):
        mine = pl.multiple_of((2 * i + side[0]) * 80, 16)
        other = pl.multiple_of((2 * i + 1 - side[0]) * 80, 16)
        at_mine[80 * i : 80 * i + 80, :] = turned[pl.ds(mine, 80), :]
        at_send[80 * i : 80 * i + 80, :] = turned[pl.ds(other, 80), :]
    for r in range(2):
        rows = slice(half_rows * r, half_rows * (r + 1))
        for j, out in enumerate((q_out, k_out)):
            part = dot(attn_in[rows, :], w_full[:, width * j : width * (j + 1)])
            part = part * tables[rows, :width] + swap_halves(part) * tables[rows, width:]
            out[rows, :] = low16(part)
        v_out[rows, :] = low16(dot(attn_in[rows, :], w_full[:, 2 * width :]))


def attention_kernel(side, q, k, v, seg_column, seg_row, lse_out, h_own, h_send, bias, heads):
    group_rows, width = q.shape
    half_rows = group_rows // 2
    fill_bias(bias, seg_column, seg_row)
    heads[...] = jnp.zeros_like(heads)
    for r in range(2):
        rows = slice(half_rows * r, half_rows * (r + 1))
        seen = slice(0, half_rows * (r + 1))
        head_lane = lax.broadcasted_iota(jnp.int32, (half_rows, 128), 1)
        lse = jnp.zeros((half_rows, 128), F32)
        for h in range(width // HEAD_DIM):
            window, keep = head_window(h)
            scores = against(q[rows, window] * keep, k[seen, window])
            scores = scores * HEAD_DIM ** (-0.5) + bias[rows, seen]
            top = jnp.max(scores, axis=1, keepdims=True)
            expo = jnp.exp(scores - top)
            total = jnp.sum(expo, axis=1, keepdims=True)
            probs = low16(expo * (1.0 / total))
            heads[rows, window] += dot(probs, v[seen, window] * keep)
            lse = jnp.where(head_lane == h, top + jnp.log(total), lse)
        lse_out[rows, :] = lse
    own = pl.multiple_of(side[1] * half_rows, 16)
    other = pl.multiple_of((1 - side[1]) * half_rows, 16)
    h_own[...] = low16(heads[pl.ds(own, half_rows), :])
    h_send[...] = low16(heads[pl.ds(other, half_rows), :])


def middle_kernel(side, h_own, h_recv, own, cot, gains, *refs):
    arrays, outs = refs[:8], refs[8:]
    mixed, resid_grad, gain_grad, hg_own, hg_send, xt_mine, xt_send, y_out = outs[:8]
    wo, wi, wt, turned, keep, final, pre = outs[8:]
    own_rows, feature_count = cot.shape
    mu, sd = own[:, feature_count : feature_count + 1], own[:, feature_count + 1 : feature_count + 2]
    gain_mid = gains[1:2, :]
    blocks = [(array, index) for array in arrays for index in range(array.shape[0])]
    for i, (array, index) in enumerate(blocks):
        row = pl.multiple_of(side[4 + i] * 80, 16)
        for j, full in enumerate((wo, wi, wt)):
            full[side[36 + i], pl.ds(row, 80), :] = array[index, 80 * j : 80 * j + 80, :]

    def turn(j, value):
        for i in range(feature_count // 128):
            turned[128 * i : 128 * i + 128, :] = low16(value[:, 128 * i : 128 * i + 128].T)
        for i in range(8):
            mine = pl.multiple_of((2 * i + side[0]) * 80, 16)
            other = pl.multiple_of((2 * i + 1 - side[0]) * 80, 16)
            xt_mine[j, 80 * i : 80 * i + 80, :] = turned[pl.ds(mine, 80), :]
            xt_send[j, 80 * i : 80 * i + 80, :] = turned[pl.ds(other, 80), :]

    y_out[0, 0] = h_own[...]
    y_out[0, 1] = h_recv[...]
    resid = own[:, :feature_count] + against(h_own[...], wo[0]) + against(h_recv[...], wo[1])
    normed, factor = rms_norm(resid)
    keep[...] = normed
    mid = normed * gain_mid
    turn(1, mid)
    mid = low16(mid)
    final_grad = wide(cot[...]) * sd
    mlp_grad = low16(final_grad)
    turn(2, final_grad)
    final[...] = resid
    for r in range(2):
        pre_act = dot(mid, wi[r])
        pre[r] = pre_act
        y_out[2, r] = low16(pre_act * (1.0 / (1.0 + jnp.exp(-pre_act))))
    final[...] += against(y_out[2, 0], wt[0]) + against(y_out[2, 1], wt[1])
    mixed[...] = low16(mu + sd * final[...])
    spread = jnp.sum(wide(cot[...]) * final[...], axis=1, keepdims=True)
    resid_grad[:, feature_count:] = jnp.broadcast_to(spread, (own_rows, 128))
    for r in range(2):
        hidden_grad = dot(mlp_grad, wt[r])
        pre_act = pre[r]
        sigmoid = 1.0 / (1.0 + jnp.exp(-pre_act))
        y_out[1, r] = low16(hidden_grad * sigmoid * (1.0 + pre_act * (1.0 - sigmoid)))
    mid_grad = against(y_out[1, 0], wi[0]) + against(y_out[1, 1], wi[1])
    normed = keep[...]
    gain_grad[...] = jnp.sum(mid_grad * normed, axis=0, keepdims=True)
    total = final_grad + norm_back(mid_grad * gain_mid, normed, factor)
    resid_grad[:, :feature_count] = total
    attn_grad = low16(total)
    hg_own[...] = low16(dot(attn_grad, wo[0]))
    hg_send[...] = low16(dot(attn_grad, wo[1]))
    turn(0, total)


def middle_weights_kernel(side, xt, xt_recv, y_own, y_recv, send, kept, total):
    for j in range(3):
        for r in range(2):
            total[j, r] = dot(xt[j], y_own[j, r]) + dot(xt_recv[j], y_recv[j, r])
    core, x = side[0], side[2]
    for u in range(2):
        for z in range(4):
            for out, sent in ((send, 1), (kept, 0)):
                other_x = jnp.where(core == 0, u, sent)
                other_y = jnp.where(core == 0, sent, u)
                spot = 2 * z + jnp.where(other_x == 0, x, 1 - x)
                row = pl.multiple_of(spot * 80, 16)
                for j in range(3):
                    out[u, z, 80 * j : 80 * j + 80, :] = low16(total[j, other_y, pl.ds(row, 80), :])


def attention_back_kernel(
    side, q, k, v, lse, hg_own, hg_recv, tables, seg_column, seg_row, out, bias, grad, dq, dk, dv
):
    group_rows, width = q.shape
    half_rows = group_rows // 2
    grad[pl.ds(pl.multiple_of(side[1] * half_rows, 16), half_rows), :] = hg_own[...]
    grad[pl.ds(pl.multiple_of((1 - side[1]) * half_rows, 16), half_rows), :] = hg_recv[...]
    fill_bias(bias, seg_column, seg_row)
    for part in (dq, dk, dv):
        part[...] = jnp.zeros_like(part)
    scale = HEAD_DIM ** (-0.5)
    for r in range(2):
        rows = slice(half_rows * r, half_rows * (r + 1))
        seen = slice(0, half_rows * (r + 1))
        for h in range(width // HEAD_DIM):
            window, keep = head_window(h)
            q_head = q[rows, window] * keep
            g_head = grad[rows, window] * keep
            scores = against(q_head, k[seen, window]) * scale + bias[rows, seen]
            probs = jnp.exp(scores - lse[rows, h : h + 1])
            prob_grad = against(g_head, v[seen, window])
            inner = jnp.sum(probs * prob_grad, axis=1, keepdims=True)
            score_grad = low16(probs * (prob_grad - inner))
            dq[rows, window] += dot(score_grad, k[seen, window] * keep)
            dk[seen, window] += across(score_grad, q_head)
            dv[seen, window] += across(low16(probs), g_head)
    for r in range(2):
        rows = slice(half_rows * r, half_rows * (r + 1))
        for j, part in enumerate((dq, dk)):
            value = part[rows, :] * scale
            out[rows, width * j : width * (j + 1)] = low16(
                value * tables[rows, :width] - swap_halves(value) * tables[rows, width:]
            )
        out[rows, 2 * width :] = low16(dv[rows, :])


def gain_window(place):
    return min(place * 80 // 128 * 128, 1024)


def input_grad_kernel(side, d_qkv, w_full, normed, gain_mid_grad, own, send, gain_parts):
    half_rows = own.shape[0]
    mine = pl.ds(pl.multiple_of(side[1] * half_rows, 16), half_rows)
    other = pl.ds(pl.multiple_of((1 - side[1]) * half_rows, 16), half_rows)
    part = against(d_qkv[other, :], w_full[...])
    send[...] = low16(part)
    gain = jnp.sum(part * normed[other, :], axis=0, keepdims=True)
    part = against(d_qkv[mine, :], w_full[...])
    own[...] = part
    gain = gain + jnp.sum(part * normed[mine, :], axis=0, keepdims=True)
    for place in range(16):
        first = gain_window(place)
        for y in range(2):
            gain_parts[2 * place + y, 0:1] = gain[:, first : first + 256]
            gain_parts[2 * place + y, 1:2] = gain_mid_grad[:, first : first + 256]


def first_weights_kernel(side, at, at_recv, d_qkv, d_recv, *outs):
    far, near, kept, total = outs
    width = total.shape[1] // 3
    for j in range(3):
        columns = slice(width * j, width * (j + 1))
        total[:, columns] = dot(at[...], d_qkv[:, columns]) + dot(at_recv[...], d_recv[:, columns])
    x, z = side[2], side[3]
    for step in range(4):
        there = lax.rem(z + step, 4)
        row = pl.multiple_of((2 * there + 1 - x) * 80, 16)
        if step == 2:
            far[...] = low16(total[pl.ds(row, 80), :])
        else:
            near[step % 4 // 2 + step % 2] = low16(total[pl.ds(row, 80), :])
        row = pl.multiple_of((2 * there + x) * 80, 16)
        kept[step] = low16(total[pl.ds(row, 80), :])


ALL_AXES = ("z", "x", "c", "y")
Z_STEPS = (1, 3, 2)


def flip(value, axis):
    return lax.ppermute(value, axis, [(0, 1), (1, 0)])


def shift_z(value, step):
    return lax.ppermute(value, "z", [(i, (i + step) % 4) for i in range(4)])


def flip_split(value, first):
    pairs = []
    for z in range(4):
        for x in range(2):
            for c in range(2):
                for y in range(2):
                    there = (z, 1 - x, c, y) if c == first else (z, x, c, 1 - y)
                    here = ((z * 2 + x) * 2 + c) * 2 + y
                    pairs.append((here, ((there[0] * 2 + there[1]) * 2 + there[2]) * 2 + there[3]))
    return lax.ppermute(value, ALL_AXES, pairs)


def pick(array, index, axis=0):
    return lax.dynamic_index_in_dim(array, index, axis, keepdims=False)


def local_fast(
    tokens,
    w_query,
    w_key,
    w_value,
    w_output,
    w_in,
    w_out,
    gain_attn,
    gain_mlp,
    seq_lengths,
    seq_offsets,
    cotangent,
):
    z, x, c, y = (lax.axis_index(name) for name in ALL_AXES)
    own_rows, feature_count = tokens.shape
    head_width = w_query.shape[1]
    group_rows = 2 * own_rows

    q_marks = [(0, 0), (1, 0), (3, 0), (0, 1), (2, 0), (2, 1), (1, 1), (3, 1)]
    q_place = jnp.stack(
        [
            ((z - step) % 4 * 2 + (x ^ xr)) * 2 + (c ^ cr)
            for cr in range(2)
            for step, xr in q_marks
        ]
    ).astype(jnp.int32)
    places, halves = [], []
    for cr in range(2):
        core = c ^ cr
        for second, third in ((0, 0), (1, 0), (0, 1), (1, 1)):
            for step in (0, 1, 3, 2):
                xr = jnp.where(core == 0, second, third)
                places.append(((z - step) % 4 * 2 + (x ^ xr)) * 2 + core)
                halves.append(jnp.where(core == 0, third, second))
    side = jnp.concatenate(
        [jnp.stack([c, y, x, z, *places, *halves]).astype(jnp.int32), q_place]
    )

    gains = jnp.pad(
        jnp.stack([gain_attn, gain_mlp]), ((0, 14), (0, head_width - gain_attn.shape[0]))
    )
    q_block = jnp.concatenate([w_query, w_key, w_value, gains], axis=0)
    p_block = jnp.concatenate([w_output.T, w_in, w_out.T], axis=0)
    tokens_other = flip(tokens, "y")
    near = [shift_z(q_block, step) for step in (1, 3)]
    far = shift_z(near[0], 1)
    across_own = flip(q_block, "x")
    q_first = stack_blocks([q_block, *near, across_own], "stack_first", [far])
    near = stack_blocks(near, "stack_near")
    lengths, offsets = seq_lengths[0], seq_offsets[0]
    half = (own_rows, head_width)
    group = (group_rows, head_width)
    own_full = (own_rows, feature_count)
    own_more = (own_rows, feature_count + 128)
    position = row_layout(lengths, offsets, group_rows)[2]
    turns = jnp.concatenate(rotary_tables(position), axis=1)
    normed_in, rows_own, stats, tables, seg_column, seg_row = local_kernel(
        group_kernel,
        [
            ((group_rows, feature_count), F32),
            (own_more, F32),
            ((8, 128), F32),
            ((group_rows, 2 * head_width), F32),
            ((group_rows, 1), jnp.int32),
            ((1, group_rows), jnp.int32),
        ],
        3,
        [((group_rows, feature_count), BF)],
        "group",
        10,
    )(side, lengths, offsets, tokens, tokens_other, turns)

    (near_other,) = hold([flip(near, "x")], [normed_in])
    q_parts = [q_first, far[None], flip(far, "x")[None], near_other]
    q_all = q_parts + [flip(part, "c") for part in q_parts]

    (p_block,) = hold([p_block], [far])
    p_near = [shift_z(p_block, step) for step in (1, 3)]
    vector = ((1, feature_count), F32)
    w_full, at_mine, at_send, q_rot, k_rot, values, gains = local_kernel(
        project_kernel,
        [
            ((feature_count, 3 * head_width), BF),
            ((feature_count // 2, group_rows), BF),
            ((feature_count // 2, group_rows), BF),
            (group, BF),
            (group, BF),
            (group, BF),
            ((2, feature_count), F32),
        ],
        1,
        [((32, 128), F32), ((group_rows, feature_count), BF), ((feature_count, group_rows), BF)],
        "project",
        10,
    )(side, normed_in, tables, q_place[:, None], *q_all)
    (p_near[0],) = hold([p_near[0]], [q_rot])
    p_far = shift_z(p_near[0], 1)
    lse, h_own, h_send = local_kernel(
        attention_kernel,
        [((group_rows, 128), F32), (half, BF), (half, BF)],
        1,
        [((group_rows, group_rows), F32), (group, F32)],
        "attention",
        8,
    )(side, q_rot, k_rot, values, seg_column, seg_row)
    (p_block,) = hold([p_block], [lse])
    p_first = stack_blocks([p_block, *p_near, p_far], "stack_middle")
    p_second = flip_split(p_first, 0)
    p_third = flip_split(p_first, 1)
    h_recv = flip(h_send, "y")
    (p_second,) = hold([p_second], [h_recv])
    p_parts = [p_first, p_second, p_third, flip_split(p_second, 1)]
    p_all = p_parts + [flip(part, "c") for part in p_parts]
    at_recv = flip(at_send, "c")

    mixed, resid_grad, gain_mid_grad, hg_own, hg_send, xt_mine, xt_send, y_own = (
        local_kernel(
            middle_kernel,
            [
                (own_full, BF),
                (own_more, F32),
                ((1, feature_count), F32),
                (half, BF),
                (half, BF),
                ((3, feature_count // 2, own_rows), BF),
                ((3, feature_count // 2, own_rows), BF),
                ((3, 2) + half, BF),
            ],
            1,
            [((2, feature_count, head_width), BF)] * 3
            + [((feature_count, own_rows), BF), (own_full, F32), (own_full, F32), ((2,) + half, F32)],
            "middle",
            31,
        )(
            side, h_own, h_recv, rows_own, cotangent, gains, *p_all
        )
    )
    hg_recv = flip(hg_send, "y")
    xt_recv, y_recv = flip(xt_send, "c"), flip(y_own, "c")

    quarter = (2, 4, 3 * 80, head_width)
    p_send, p_kept = local_kernel(
        middle_weights_kernel,
        [(quarter, BF), (quarter, BF)],
        1,
        [((3, 2, feature_count // 2, head_width), F32)],
        "middle_weights",
        14,
    )(side, xt_mine, xt_recv, y_own, y_recv)
    (p_send,) = hold([p_send], [hg_recv])
    p_recv = flip_split(p_send, 1)

    (d_qkv,) = local_kernel(
        attention_back_kernel,
        [((group_rows, 3 * head_width), BF)],
        1,
        [((group_rows, group_rows), F32), (group, BF), (group, F32), (group, F32), (group, F32)],
        "attention_back",
        11,
        after=[p_send],
    )(side, q_rot, k_rot, values, lse, hg_own, hg_recv, tables, seg_column, seg_row)
    d_recv = flip(d_qkv, "c")
    in_own, in_send, gain_parts = local_kernel(
        input_grad_kernel,
        [(own_full, F32), (own_full, BF), ((32, 2, 256), F32)],
        1,
        [],
        "input_grad",
        10,
    )(side, d_qkv, w_full, normed_in, gain_mid_grad)
    slab = (80, 3 * head_width)
    far, near, q_kept, p_kept, gain_parts, in_own = local_kernel(
        first_weights_kernel,
        [(slab, BF), ((3,) + slab, BF), ((4,) + slab, BF)],
        1,
        [((feature_count // 2, 3 * head_width), F32)],
        "first_weights",
        12,
        gates=[p_kept, gain_parts, in_own],
    )(side, at_mine, at_recv, d_qkv, d_recv)
    far = flip(far, "x")

    p_send, p_kept, far = local_kernel(
        first_sum_kernel, [(quarter[1:], BF)] * 2 + [(slab, BF)], 0, [], "first_sum", 4
    )(p_kept, p_recv, q_kept, far)
    p_recv = flip_split(p_send, 0)
    q_two = shift_z(far, 1)
    gain_parts = lax.all_to_all(gain_parts, ALL_AXES, 0, 0, tiled=True)
    (near,) = hold([near], [p_recv, q_two, gain_parts])
    near = flip(near, "x")
    piece = quarter[2:]
    p_own, p_one, p_two, p_three = local_kernel(
        second_sum_kernel,
        [(piece, F32), (piece, F32)] + [(piece, BF)] * 2,
        1,
        [],
        "second_sum",
        4,
    )(side, p_kept, p_recv)
    p_three = shift_z(p_three, 3)
    (p_one,) = local_kernel(third_sum_kernel, [(piece, BF)], 0, [], "third_sum", 2)(
        p_one, shift_z(p_two, 1)
    )
    q_own, near_one, near_three, gain_grads = local_kernel(
        near_sum_kernel,
        [(slab, F32), (slab, BF), (slab, BF), ((2, 80), F32)],
        1,
        [],
        "near_sum",
        4,
        after=[p_one],
    )(side, q_kept, near, q_two, gain_parts)
    q_one, q_three = shift_z(near_one, 1), shift_z(near_three, 3)
    p_one = shift_z(p_one, 1)
    (in_send,) = hold([in_send], [p_own])
    in_recv = flip(in_send, "y")
    scaled, sums = local_kernel(
        token_sums_kernel,
        [(own_full, F32), ((8, 128), F32)],
        3,
        [],
        "token_sums",
        8,
        after=[near_one],
    )(
        side, lengths, offsets, in_own, in_recv, gains, resid_grad, normed_in, rows_own, cotangent
    )
    sums_recv = flip(sums, "y")
    (grad_tokens,) = local_kernel(
        token_grad_kernel, [(own_full, F32)], 2, [], "token_grad", 6
    )(side, offsets, scaled, sums, sums_recv, stats, tokens, rows_own)

    shard = ((80, head_width), F32)
    grad_query, grad_key, grad_value = local_kernel(
        first_total_kernel, [shard] * 3, 0, [], "first_total", 4
    )(q_own, q_one, q_three)
    grad_output, grad_in, grad_out = local_kernel(
        middle_total_kernel, [shard] * 3, 0, [], "middle_total", 4
    )(p_own, p_one, p_three)
    return (
        mixed,
        grad_tokens,
        grad_query,
        grad_key,
        grad_value,
        grad_output.T,
        grad_in,
        grad_out.T,
        gain_grads[0],
        gain_grads[1],
    )


def solution_fast(mesh):
    fine = Mesh(mesh.devices.reshape(4, 2, 2, 2), ALL_AXES)
    dp = ("z", "x", "c")
    rows, by_row, by_column = P(ALL_AXES, None), P(dp, "y"), P("y", dp)
    in_specs = (rows,) + (by_row,) * 3 + (by_column, by_row, by_column)
    in_specs += (P(dp), P(dp), P(dp, None), P(dp, None), rows)
    out_specs = (rows, rows) + (by_row,) * 3 + (by_column, by_row, by_column, P(dp), P(dp))
    return jax.shard_map(
        local_fast, mesh=fine, in_specs=in_specs, out_specs=out_specs, check_vma=False
    )


def solution(mesh):
    if dict(mesh.shape) == {"dp": 16, "tensor": 2}:
        return solution_fast(mesh)
    in_specs = (
        P(("dp", "tensor"), None),
        P("dp", "tensor"),
        P("dp", "tensor"),
        P("dp", "tensor"),
        P("tensor", "dp"),
        P("dp", "tensor"),
        P("tensor", "dp"),
        P("dp"),
        P("dp"),
        P("dp", None),
        P("dp", None),
        P(("dp", "tensor"), None),
    )
    out_specs = (
        P(("dp", "tensor"), None),
        P(("dp", "tensor"), None),
        P("dp", "tensor"),
        P("dp", "tensor"),
        P("dp", "tensor"),
        P("tensor", "dp"),
        P("dp", "tensor"),
        P("tensor", "dp"),
        P("dp"),
        P("dp"),
    )
    return jax.shard_map(local, mesh=mesh, in_specs=in_specs, out_specs=out_specs, check_vma=False)
```
